32 devices in a mesh: sx: 8 (over y, x, core), sy: 4 (over z).
Axes of the slice: x: 2, y: 2, z: 4, core: 2. Of those that a mesh axis runs over, the one named last changes fastest.
Arguments:
- a_tiles: bfloat16 [8, 4, 32, 7, 128, 128], P('sx', 'sy'), may hold values from -3 to 3
- columns: int32 [8, 4, 32, 7], P('sx', 'sy'), may hold values from 0 to 1023, as said below
- ptent: bfloat16 [8, 4, 32, 128, 128], P('sx', 'sy'), may hold values from -0.125 to 0.125
- dinv: bfloat16 [8, 4, 32, 128, 128], P('sx', 'sy'), may hold values from -0.5 to 0.5
- agg: int32 [1024], replicated, may hold values from 0 to 63, as said below
Outputs:
- coarse_op: bfloat16 [8, 4, 2, 13, 2, 128, 128], P('sx')
The draws below stay inside these ranges and needn't reach their ends.
Inputs may be any that keep to these rules, and one draw needn't show every extreme that they name: columns[i, j, l, 0] is the row's own global index; every entry is the global index of a fine tile of subdomain (i, j) or of a subdomain one step away along one of the two directions. `agg`: the aggregate of a fine tile is a coarse tile of the same subdomain, and every coarse tile is the aggregate of at least one fine tile.
All inputs are finite; a program needn't handle non-finite values.
Results may differ from the reference program's by a relative error of at most 0.0064.
Values may be sent and summed in bfloat16 or wider, within the bound.
No kernel may reach another device: no remote copies, remote signals or barrier semaphores. Data moves between devices by JAX's collectives and lax.ppermute only.
A program may use at most 192 MiB of HBM per device.

```python
import jax
import jax.numpy as jnp
import numpy as np
from jax import lax

TILE = 128
CW = 128
K = 7
RATIO = 16
NOFF = 13
R = 32
RC = 2
GRID_X = 8
GRID_Y = 4


def draw_columns(key, part):
    fine_count = GRID_X * GRID_Y * R
    row_ids = jnp.arange(fine_count, dtype=jnp.int32)
    device = row_ids // R
    grid_x = (device // GRID_Y)[:, None]
    grid_y = (device % GRID_Y)[:, None]
    key_dir, key_tile = jax.random.split(key)
    choose_dir = jax.random.randint(key_dir, (fine_count, K), 0, 8)
    local_tile = jax.random.randint(key_tile, (fine_count, K), 0, R)
    step_x = jnp.where(choose_dir == 1, -1, jnp.where(choose_dir == 2, 1, 0))
    step_y = jnp.where(choose_dir == 3, -1, jnp.where(choose_dir == 4, 1, 0))
    target_x = grid_x + step_x
    target_y = grid_y + step_y
    inside = (target_x >= 0) & (target_x < GRID_X) & (target_y >= 0) & (target_y < GRID_Y)
    target_x = jnp.where(inside, target_x, grid_x)
    target_y = jnp.where(inside, target_y, grid_y)
    chosen = (target_x * GRID_Y + target_y) * R + local_tile
    chosen = chosen.at[:, 0].set(row_ids)
    return chosen.reshape(GRID_X, GRID_Y, R, K).astype(jnp.int32)


def draw_agg(key, part):
    fine_count = GRID_X * GRID_Y * R
    row_ids = jnp.arange(fine_count, dtype=jnp.int32)
    device = row_ids // R
    local_row = row_ids % R
    key_turn, key_pick = jax.random.split(key)
    turned = jax.random.randint(key_turn, (GRID_X * GRID_Y,), 0, RC)[device]
    picked = jax.random.randint(key_pick, (fine_count,), 0, RC)
    member = jnp.where(local_row < RC, (local_row + turned) % RC, picked)
    return (device * RC + member).astype(jnp.int32)


def level_of(stream_key, dims, shards, least, top_value):
    def one(axis_at, blocks):
        draws = jax.random.uniform(jax.random.fold_in(jax.random.fold_in(stream_key, 6), axis_at), (blocks,), jnp.float32, least / len(shards), top_value / len(shards))
        return jnp.repeat(jnp.exp(draws), dims[axis_at] // blocks).reshape((-1,) + (1,) * (len(dims) - axis_at - 1))

    loudness = one(*shards[0])
    for cut in shards[1:]:
        loudness = loudness * one(*cut)
    return loudness


def bell_draw(rng, shape, scale, limit, pieces=(), held_as=jnp.bfloat16):
    loudness = level_of(rng, shape, pieces, -0.22, 0.18) if pieces else 1.0
    entries = jax.random.normal(rng, shape, jnp.float32) * scale * loudness
    return jnp.minimum(jnp.maximum(entries, -limit), limit).astype(held_as)


def setup_inputs(seed: int = 0) -> dict:
    streams_of = jax.random.split(jax.random.key(seed), 6)
    a_tiles = bell_draw(streams_of[0], (GRID_X, GRID_Y, R, K, TILE, TILE), 0.5, 3.0, ((0, 8), (1, 4)))
    columns = draw_columns(jax.random.fold_in(streams_of[5], 71), 0)
    ptent = bell_draw(streams_of[2], (GRID_X, GRID_Y, R, TILE, CW), (TILE * RATIO) ** -0.5, 0.125, ((0, 8), (1, 4)))
    dinv = bell_draw(streams_of[3], (GRID_X, GRID_Y, R, TILE, TILE), TILE ** -0.5, 0.5, ((0, 8), (1, 4)))
    agg = draw_agg(jax.random.fold_in(streams_of[5], 71), 0)
    return {"a_tiles": a_tiles, "columns": columns, "ptent": ptent, "dinv": dinv, "agg": agg}


WINDOW_SHIFTS = ((-2, 0), (-1, -1), (-1, 0), (-1, 1), (0, -2), (0, -1), (0, 0), (0, 1), (0, 2), (1, -1), (1, 0), (1, 1), (2, 0))
smoothing = 2.0 / 3.0


def reference(a_tiles, columns, ptent, dinv, agg):
    devices_all = GRID_X * GRID_Y
    fine_count = devices_all * R
    coarse_count = devices_all * RC
    coupling = a_tiles.reshape(devices_all, R, K, TILE, TILE)
    targets = columns.reshape(devices_all, R, K)
    inverse = dinv.reshape(devices_all, R, TILE, TILE)
    tentative = ptent.reshape(fine_count, TILE, CW)
    code_table = np.zeros(25, np.int32)
    for position in range(len(WINDOW_SHIFTS)):
        pair = WINDOW_SHIFTS[position]
        code_table[(pair[0] + 2) * 5 + pair[1] + 2] = position
    lookup = jnp.asarray(code_table)
    leading = (jnp.arange(K) == 0)[None, :, None, None]

    def one_device(running, inputs):
        device, coupling_rows, targets_dev, inverse_dev = inputs
        fetched = tentative[targets_dev].astype(jnp.float32)
        applied = jnp.einsum("rkij,rkjc->rkic", coupling_rows.astype(jnp.float32), fetched).astype(jnp.bfloat16)
        smooth = jnp.einsum("rij,rkjc->rkic", inverse_dev.astype(jnp.float32), applied.astype(jnp.float32))
        own_tiles = lax.dynamic_slice_in_dim(tentative, (device * R).astype(jnp.int32), R, 0).astype(jnp.float32)
        smoothed = jnp.where(leading, own_tiles[:, None] - smoothing * smooth, -smoothing * smooth).astype(jnp.bfloat16)
        coarse = agg[targets_dev]
        holder = targets_dev // R
        holder_x = holder // GRID_Y
        holder_y = holder % GRID_Y
        shift_x = holder_x[:, None, :] - holder_x[:, :, None]
        shift_y = holder_y[:, None, :] - holder_y[:, :, None]
        offset = lookup[(shift_x + 2) * 5 + shift_y + 2]
        slot_index = (coarse[:, :, None] * NOFF + offset) * RC + coarse[:, None, :] % RC
        products = jnp.einsum("raic,rbid->rabcd", smoothed.astype(jnp.float32), applied.astype(jnp.float32))
        return running.at[slot_index.reshape(-1)].add(products.reshape(-1, CW, CW)), None

    start = jnp.zeros((coarse_count * NOFF * RC, CW, CW), jnp.float32)
    running, _ = lax.scan(one_device, start, (jnp.arange(devices_all, dtype=jnp.int32), coupling, targets, inverse))
    return running.reshape(GRID_X, GRID_Y, RC, NOFF, RC, CW, CW).astype(jnp.bfloat16)
```

```python
import functools

import jax
import jax.numpy as jnp
from jax import lax
from jax.experimental import pallas as pl
from jax.experimental.pallas import tpu as pltpu
from jax.sharding import PartitionSpec as P

CROSS_SHIFTS = ((0, 0), (-1, 0), (1, 0), (0, -1), (0, 1))
WINDOW_SHIFTS = (
    (-2, 0),
    (-1, -1),
    (-1, 0),
    (-1, 1),
    (0, -2),
    (0, -1),
    (0, 0),
    (0, 1),
    (0, 2),
    (1, -1),
    (1, 0),
    (1, 1),
    (2, 0),
)
TRAVEL = tuple(sorted(range(13), key=lambda o: (WINDOW_SHIFTS[o][1] > 0) - (WINDOW_SHIFTS[o][1] < 0)))
BELOW = sum(shift[1] < 0 for shift in WINDOW_SHIFTS)
ABOVE = sum(shift[1] > 0 for shift in WINDOW_SHIFTS)
smoothing = 2.0 / 3.0
MEMBERS = 2
ROWS_PER_STEP = 4
NT = (((1,), (1,)), ((), ()))


def shifted(x, axis, by):
    length = lax.axis_size(axis)
    pairs = [(i, i + by) for i in range(length) if 0 <= i + by < length]
    return lax.ppermute(x, axis, pairs)


def products_kernel(count_y, rows, members, taps, *refs):
    columns, agg, place, a_ref, dinv_ref = refs[:5]
    sources = refs[5:10]
    outs = refs[10:15]
    tent, right, left, sems = refs[15:19]
    sums = refs[19:]
    tile = a_ref.shape[-1]
    step = pl.program_id(0)

    @pl.when(step == 0)
    def _():
        copies = [
            pltpu.make_async_copy(sources[d], tent.at[pl.ds(d * rows, rows)], sems.at[d])
            for d in range(5)
        ]
        for copy in copies:
            copy.start()
        for copy in copies:
            copy.wait()

    for u in range(ROWS_PER_STEP):
        g = step * ROWS_PER_STEP + u
        total = sums[u]
        total[...] = jnp.zeros_like(total)
        own_slot = 0
        for k in range(taps):
            target = columns[g * taps + k]
            holder = target // rows
            step_x = holder // count_y - place[0]
            step_y = holder % count_y - place[1]
            direction = jnp.where(
                step_x == -1,
                1,
                jnp.where(step_x == 1, 2, jnp.where(step_y == -1, 3, jnp.where(step_y == 1, 4, 0))),
            )
            slot = direction * members + agg[target] % members
            if k == 0:
                own_slot = slot
            z = lax.dot_general(
                tent[direction * rows + target % rows],
                a_ref[u, k],
                NT,
                preferred_element_type=jnp.float32,
            )
            at = pl.ds(pl.multiple_of(slot * tile, tile), tile)
            total[at, :] += z.astype(jnp.bfloat16).astype(jnp.float32)
        lanes = pl.ds(pl.multiple_of(g * tile, tile), tile)
        applied = total[...].astype(jnp.bfloat16)
        right[:, lanes] = applied
        smooth = lax.dot_general(applied, dinv_ref[u], NT, preferred_element_type=jnp.float32)
        total[...] = -smoothing * smooth
        at = pl.ds(pl.multiple_of(own_slot * tile, tile), tile)
        total[at, :] += tent[g].astype(jnp.float32)
        left[:, lanes] = total[...].astype(jnp.bfloat16)

    @pl.when(step == pl.num_programs(0) - 1)
    def _():
        width = members * tile

        def one(d2, carry):
            value = lax.dot_general(
                left[...],
                right[pl.ds(pl.multiple_of(d2 * width, width), width), :],
                NT,
                preferred_element_type=jnp.float32,
            )
            for d1 in range(5):
                for m in range(members):
                    for m2 in range(members):
                        block = value[
                            (d1 * members + m) * tile : (d1 * members + m + 1) * tile,
                            m2 * tile : (m2 + 1) * tile,
                        ]
                        outs[d1][d2, m, m2] = block.astype(outs[d1].dtype)
            return carry

        lax.fori_loop(0, 5, one, 0)


def partial_blocks(a_tiles, columns, dinv, tents, agg, place, count_y, members):
    rows, taps, tile = a_tiles.shape[0], a_tiles.shape[1], a_tiles.shape[-1]
    block = (5, members, members, tile, tile)
    whole = pl.BlockSpec(block, lambda s, *_: (0,) * 5)
    slots = 5 * members
    return pl.pallas_call(
        functools.partial(products_kernel, count_y, rows, members, taps),
        grid_spec=pltpu.PrefetchScalarGridSpec(
            num_scalar_prefetch=3,
            grid=(rows // ROWS_PER_STEP,),
            in_specs=[
                pl.BlockSpec((ROWS_PER_STEP, taps, tile, tile), lambda s, *_: (s, 0, 0, 0)),
                pl.BlockSpec((ROWS_PER_STEP, tile, tile), lambda s, *_: (s, 0, 0)),
            ]
            + [pl.BlockSpec(memory_space=pl.ANY)] * 5,
            out_specs=[whole] * 5,
            scratch_shapes=[
                pltpu.VMEM((5 * rows, tile, tile), jnp.bfloat16),
                pltpu.VMEM((slots * tile, rows * tile), jnp.bfloat16),
                pltpu.VMEM((slots * tile, rows * tile), jnp.bfloat16),
                pltpu.SemaphoreType.DMA((5,)),
            ]
            + [pltpu.VMEM((slots * tile, tile), jnp.float32)] * ROWS_PER_STEP,
        ),
        out_shape=[jax.ShapeDtypeStruct(block, jnp.float32)]
        + [jax.ShapeDtypeStruct(block, jnp.bfloat16)] * 4,
        compiler_params=pltpu.CompilerParams(vmem_limit_bytes=56 * 1024 * 1024),
        cost_estimate=pl.CostEstimate(
            flops=2 * tile**3 * (rows * (taps + slots) + rows * slots * slots),
            bytes_accessed=2 * (a_tiles.size + dinv.size * 6),
            transcendentals=0,
        ),
        name="partial_blocks",
    )(columns, agg, place, a_tiles, dinv, *tents)


def window_kernel(own, lower_x, upper_x, lower_y, upper_y, out):
    senders = (
        ((0, 0), own),
        ((-1, 0), lower_x),
        ((1, 0), upper_x),
        ((0, -1), lower_y),
        ((0, 1), upper_y),
    )
    for position, offset in enumerate(TRAVEL):
        total = None
        for shift, values in senders:
            for d, member in enumerate(CROSS_SHIFTS):
                if (shift[0] + member[0], shift[1] + member[1]) == WINDOW_SHIFTS[offset]:
                    term = values[d].astype(jnp.float32)
                    total = term if total is None else total + term
        out[position] = total.astype(out.dtype)


def finished_window(blocks):
    _, members, _, tile, _ = blocks[0].shape
    spec = lambda lead: pl.BlockSpec(
        (lead, 1, members, tile, tile), lambda m: (0, m, 0, 0, 0)
    )
    return pl.pallas_call(
        window_kernel,
        grid=(members,),
        in_specs=[spec(5)] * 5,
        out_specs=spec(13),
        out_shape=jax.ShapeDtypeStruct((13, members, members, tile, tile), jnp.bfloat16),
        compiler_params=pltpu.CompilerParams(vmem_limit_bytes=32 * 1024 * 1024),
        name="finished_window",
    )(*blocks)


def place_kernel(parts, members, where, *refs):
    arrays = refs[: len(parts)]
    out = refs[-2]
    sems = refs[-1]
    jobs = []
    for index, (first, count) in enumerate(parts):
        copies = []
        for p in range(count):
            for m in range(members):
                copies.append((p, m))
        jobs.append((index, first, copies))
    for action in ("start", "wait"):
        slot = 0
        for index, first, copies in jobs:
            base = slot

            @pl.when(where[2 * index + 1] == 1)
            def _():
                for n, (p, m) in enumerate(copies):
                    copy = pltpu.make_async_copy(
                        arrays[index].at[p, m],
                        out.at[where[2 * index], m, TRAVEL[first + p]],
                        sems.at[base + n],
                    )
                    if action == "start":
                        copy.start()
                    else:
                        copy.wait()

            slot += len(copies)


def placed(out, arrays, firsts, origins, valid):
    members = out.shape[1]
    parts = tuple((f, a.shape[0]) for f, a in zip(firsts, arrays))
    where = jnp.stack(
        [jnp.asarray(v, jnp.int32) for pair in zip(origins, valid) for v in pair]
    )
    anywhere = pl.BlockSpec(memory_space=pl.ANY)
    return pl.pallas_call(
        functools.partial(place_kernel, parts, members),
        grid_spec=pltpu.PrefetchScalarGridSpec(
            num_scalar_prefetch=1,
            grid=(1,),
            in_specs=[anywhere] * (len(arrays) + 1),
            out_specs=anywhere,
            scratch_shapes=[
                pltpu.SemaphoreType.DMA((sum(count for _, count in parts) * members,))
            ],
        ),
        out_shape=jax.ShapeDtypeStruct(out.shape, out.dtype),
        input_output_aliases={1 + len(arrays): 0},
        name="placed",
    )(where, *arrays, out)


def local(a_tiles, columns, ptent, dinv, agg):
    grid_x = lax.axis_index("sx")
    grid_y = lax.axis_index("sy")
    count_y = lax.axis_size("sy")
    rows, taps, tile = a_tiles.shape[2], a_tiles.shape[3], a_tiles.shape[-1]
    tent = jnp.swapaxes(ptent.reshape(rows, tile, tile), 1, 2)
    tents = (
        tent,
        shifted(tent, "sx", 1),
        shifted(tent, "sx", -1),
        shifted(tent, "sy", 1),
        shifted(tent, "sy", -1),
    )
    place = jnp.stack([grid_x, grid_y]).astype(jnp.int32)
    own, to_lower_x, to_upper_x, to_lower_y, to_upper_y = partial_blocks(
        a_tiles.reshape(rows, taps, tile, tile),
        columns.reshape(rows * taps),
        dinv.reshape(rows, tile, tile),
        tents,
        agg,
        place,
        count_y,
        MEMBERS,
    )
    shard = finished_window(
        (
            own,
            shifted(to_upper_x, "sx", 1),
            shifted(to_lower_x, "sx", -1),
            shifted(to_upper_y, "sy", 1),
            shifted(to_lower_y, "sy", -1),
        )
    )
    out = jnp.zeros((count_y, MEMBERS, 13, MEMBERS, tile, tile), jnp.bfloat16)
    out = placed(out, [shard], [0], [grid_y], [1])
    from_lower, from_upper = shard, shard
    for hop in range(1, count_y):
        first = 0
        if hop == count_y - 1:
            from_lower = from_lower[BELOW:]
            from_upper = from_upper[: 13 - ABOVE]
            first = BELOW
        from_lower = shifted(from_lower, "sy", 1)
        from_upper = shifted(from_upper, "sy", -1)
        out = placed(
            out,
            [from_lower, from_upper],
            [first, 0],
            [grid_y - hop, grid_y + hop],
            [grid_y >= hop, grid_y + hop < count_y],
        )
    return out[None]


def solution(mesh):
    return jax.shard_map(
        local,
        mesh=mesh,
        in_specs=(
            P("sx", "sy", None, None, None, None),
            P("sx", "sy", None, None),
            P("sx", "sy", None, None, None),
            P("sx", "sy", None, None, None),
            P(),
        ),
        out_specs=P("sx", None, None, None, None, None, None),
        check_vma=False,
    )
```

```python
import functools

import jax
import jax.numpy as jnp
from jax import lax
from jax.experimental import pallas as pl
from jax.experimental.pallas import tpu as pltpu
from jax.sharding import PartitionSpec as P

CROSS_SHIFTS = ((-1, 0), (1, 0), (0, 0), (0, -1), (0, 1))
OWN = 2
WINDOW_SHIFTS = (
    (-2, 0),
    (-1, -1),
    (-1, 0),
    (-1, 1),
    (0, -2),
    (0, -1),
    (0, 0),
    (0, 1),
    (0, 2),
    (1, -1),
    (1, 0),
    (1, 1),
    (2, 0),
)
ALONG_Y = (4, 5, 7, 8)
ALONG_X = (0, 2, 10, 12)
MIXED = (1, 9, 6, 3, 11)
GROUPS = (ALONG_Y, ALONG_X, MIXED)
smoothing = 2.0 / 3.0
MEMBERS = 2
ROWS_PER_STEP = 4
NT = (((1,), (1,)), ((), ()))


def shifted(x, axis, by):
    length = lax.axis_size(axis)
    pairs = [(i, i + by) for i in range(length) if 0 <= i + by < length]
    return lax.ppermute(x, axis, pairs)


def slots_kernel(count_y, rows, members, taps, *refs):
    columns, agg, place, a_ref, dinv_ref = refs[:5]
    sources = refs[5:10]
    left_out, right_out, to_lower, to_upper = refs[10:14]
    tent, right, left, sems = refs[14:18]
    sums = refs[18:]
    tile = a_ref.shape[-1]
    kept = left_out.shape[0]
    step = pl.program_id(0)

    @pl.when(step == 0)
    def _():
        copies = [
            pltpu.make_async_copy(sources[d], tent.at[pl.ds(d * rows, rows)], sems.at[d])
            for d in range(5)
        ]
        for copy in copies:
            copy.start()
        for copy in copies:
            copy.wait()

    for u in range(ROWS_PER_STEP):
        g = step * ROWS_PER_STEP + u
        total = sums[u]
        total[...] = jnp.zeros_like(total)
        own_slot = 0
        for k in range(taps):
            target = columns[g * taps + k]
            holder = target // rows
            step_x = holder // count_y - place[0]
            step_y = holder % count_y - place[1]
            direction = jnp.where(
                step_x == -1,
                0,
                jnp.where(step_x == 1, 1, jnp.where(step_y == -1, 3, jnp.where(step_y == 1, 4, OWN))),
            )
            slot = direction * members + agg[target] % members
            if k == 0:
                own_slot = slot
            z = lax.dot_general(
                tent[direction * rows + target % rows],
                a_ref[u, k],
                NT,
                preferred_element_type=jnp.float32,
            )
            at = pl.ds(pl.multiple_of(slot * tile, tile), tile)
            total[at, :] += z.astype(jnp.bfloat16).astype(jnp.float32)
        lanes = pl.ds(pl.multiple_of(g * tile, tile), tile)
        here = slice(u * tile, (u + 1) * tile)
        applied = total[...].astype(jnp.bfloat16)
        right[:, lanes] = applied
        right_out[:, here] = applied
        smooth = lax.dot_general(applied, dinv_ref[u], NT, preferred_element_type=jnp.float32)
        total[...] = -smoothing * smooth
        at = pl.ds(pl.multiple_of(own_slot * tile, tile), tile)
        total[at, :] += tent[OWN * rows + g].astype(jnp.float32)
        left_out[:, here] = total[:kept, :].astype(jnp.bfloat16)
        left[:, lanes] = total[kept:, :].astype(jnp.bfloat16)

    @pl.when(step == pl.num_programs(0) - 1)
    def _():
        width = members * tile

        def one(d2, carry):
            value = lax.dot_general(
                left[...],
                right[pl.ds(pl.multiple_of(d2 * width, width), width), :],
                NT,
                preferred_element_type=jnp.float32,
            )
            spread(value, (to_lower, to_upper), d2, members, tile)
            return carry

        lax.fori_loop(0, 5, one, 0)


def spread(value, outs, d2, members, tile):
    for d1, out in enumerate(outs):
        for m in range(members):
            for m2 in range(members):
                row = (d1 * members + m) * tile
                block = value[row : row + tile, m2 * tile : (m2 + 1) * tile]
                out[d2, m, m2] = block.astype(out.dtype)


def slot_matrices(a_tiles, columns, dinv, tents, agg, place, count_y, members):
    rows, taps, tile = a_tiles.shape[0], a_tiles.shape[1], a_tiles.shape[-1]
    block = (5, members, members, tile, tile)
    whole = pl.BlockSpec(block, lambda s, *_: (0,) * 5)
    slots = 5 * members
    kept = 3 * members * tile
    span = ROWS_PER_STEP * tile
    return pl.pallas_call(
        functools.partial(slots_kernel, count_y, rows, members, taps),
        grid_spec=pltpu.PrefetchScalarGridSpec(
            num_scalar_prefetch=3,
            grid=(rows // ROWS_PER_STEP,),
            in_specs=[
                pl.BlockSpec((ROWS_PER_STEP, taps, tile, tile), lambda s, *_: (s, 0, 0, 0)),
                pl.BlockSpec((ROWS_PER_STEP, tile, tile), lambda s, *_: (s, 0, 0)),
            ]
            + [pl.BlockSpec(memory_space=pl.ANY)] * 5,
            out_specs=[
                pl.BlockSpec((kept, span), lambda s, *_: (0, s)),
                pl.BlockSpec((slots * tile, span), lambda s, *_: (0, s)),
                whole,
                whole,
            ],
            scratch_shapes=[
                pltpu.VMEM((5 * rows, tile, tile), jnp.bfloat16),
                pltpu.VMEM((slots * tile, rows * tile), jnp.bfloat16),
                pltpu.VMEM((slots * tile - kept, rows * tile), jnp.bfloat16),
                pltpu.SemaphoreType.DMA((5,)),
            ]
            + [pltpu.VMEM((slots * tile, tile), jnp.float32)] * ROWS_PER_STEP,
        ),
        out_shape=[
            jax.ShapeDtypeStruct((kept, rows * tile), jnp.bfloat16),
            jax.ShapeDtypeStruct((slots * tile, rows * tile), jnp.bfloat16),
            jax.ShapeDtypeStruct(block, jnp.bfloat16),
            jax.ShapeDtypeStruct(block, jnp.bfloat16),
        ],
        compiler_params=pltpu.CompilerParams(vmem_limit_bytes=52 * 1024 * 1024),
        cost_estimate=pl.CostEstimate(
            flops=2 * tile**3 * rows * (taps + slots + 2 * members * slots),
            bytes_accessed=2 * (a_tiles.size + dinv.size * 6 + rows * tile * tile * 16),
            transcendentals=0,
        ),
        name="slot_matrices",
    )(columns, agg, place, a_tiles, dinv, *tents)


def rows_kernel(members, tile, left, right, *refs):
    outs, total = refs[:-1], refs[-1]
    step = pl.program_id(0)
    width = members * tile
    for d2 in range(5):
        value = lax.dot_general(
            left[...],
            right[d2 * width : (d2 + 1) * width, :],
            NT,
            preferred_element_type=jnp.float32,
        )

        @pl.when(step == 0)
        def _():
            total[d2] = value

        @pl.when(step > 0)
        def _():
            total[d2] += value

    @pl.when(step == pl.num_programs(0) - 1)
    def _():
        for d2 in range(5):
            spread(total[d2], outs, d2, members, tile)


def partial_rows(left, right, first, count, dtype, members, name):
    slots, depth = right.shape
    tile = slots // (5 * members)
    height = count * members * tile
    chunk = depth // 4
    block = (5, members, members, tile, tile)
    return pl.pallas_call(
        functools.partial(rows_kernel, members, tile),
        grid=(4,),
        in_specs=[
            pl.BlockSpec((height, chunk), lambda s: (first // count, s)),
            pl.BlockSpec((slots, chunk), lambda s: (0, s)),
        ],
        out_specs=[pl.BlockSpec(block, lambda s: (0,) * 5)] * count,
        out_shape=[jax.ShapeDtypeStruct(block, dtype)] * count,
        scratch_shapes=[pltpu.VMEM((5, height, members * tile), jnp.float32)],
        compiler_params=pltpu.CompilerParams(vmem_limit_bytes=40 * 1024 * 1024),
        cost_estimate=pl.CostEstimate(
            flops=2 * height * slots * depth,
            bytes_accessed=2 * (height + slots) * depth,
            transcendentals=0,
        ),
        name=name,
    )(left, right)


def window_kernel(group, shifts, *refs):
    out = refs[-1]
    for position, offset in enumerate(group):
        total = None
        for shift, values in zip(shifts, refs):
            for d, member in enumerate(CROSS_SHIFTS):
                if (shift[0] + member[0], shift[1] + member[1]) == WINDOW_SHIFTS[offset]:
                    term = values[d].astype(jnp.float32)
                    total = term if total is None else total + term
        out[position] = total.astype(out.dtype)


def finished(group, shifts, blocks, name):
    _, members, _, tile, _ = blocks[0].shape
    spec = lambda lead: pl.BlockSpec(
        (lead, 1, members, tile, tile), lambda m: (0, m, 0, 0, 0)
    )
    shape = (len(group), members, members, tile, tile)
    return pl.pallas_call(
        functools.partial(window_kernel, group, shifts),
        grid=(members,),
        in_specs=[spec(5)] * len(blocks),
        out_specs=spec(len(group)),
        out_shape=jax.ShapeDtypeStruct(shape, jnp.bfloat16),
        compiler_params=pltpu.CompilerParams(vmem_limit_bytes=32 * 1024 * 1024),
        cost_estimate=pl.CostEstimate(
            flops=5 * blocks[0].size, bytes_accessed=8 * blocks[0].size, transcendentals=0
        ),
        name=name,
    )(*blocks)


def place_kernel(positions, aliased, row, kind, *refs):
    out = refs[-1]
    entry = pl.program_id(1)
    per = len(GROUPS)
    for source, lists in enumerate(positions):

        @pl.when(kind[entry] == source)
        def _():
            held = set()
            for index, offsets in enumerate(lists):
                for p, offset in enumerate(offsets):
                    out[0, 0, offset] = refs[source * per + index][p, 0]
                    held.add(offset)
            for offset in range(13):
                if offset not in held:
                    out[0, 0, offset] = jnp.zeros(out.shape[3:], out.dtype)


def placed(out, shards, positions, rows, kinds, count):
    arrays = [array for shard in shards for array in shard]
    members, _, tile, _ = arrays[0].shape[1:]
    aliased = out is not None
    in_specs = [
        pl.BlockSpec((a.shape[0], 1, members, tile, tile), lambda m, e, *_: (0, m, 0, 0, 0))
        for a in arrays
    ]
    shape = (count, members, 13, members, tile, tile)
    operands = list(arrays)
    if aliased:
        in_specs.append(pl.BlockSpec(memory_space=pl.ANY))
        operands.append(out)
    return pl.pallas_call(
        functools.partial(place_kernel, positions, aliased),
        grid_spec=pltpu.PrefetchScalarGridSpec(
            num_scalar_prefetch=2,
            grid=(members, len(rows)),
            in_specs=in_specs,
            out_specs=pl.BlockSpec(
                (1, 1, 13, members, tile, tile),
                lambda m, e, row, kind: (row[e], m, 0, 0, 0, 0),
            ),
        ),
        out_shape=jax.ShapeDtypeStruct(shape, jnp.bfloat16),
        input_output_aliases={2 + len(arrays): 0} if aliased else {},
        compiler_params=pltpu.CompilerParams(vmem_limit_bytes=32 * 1024 * 1024),
        cost_estimate=pl.CostEstimate(
            flops=0, bytes_accessed=10 * 13 * members * members * tile * tile, transcendentals=0
        ),
        name="placed",
    )(jnp.stack(rows).astype(jnp.int32), jnp.stack(kinds).astype(jnp.int32), *operands)


def local(a_tiles, columns, ptent, dinv, agg):
    grid_x = lax.axis_index("sx")
    grid_y = lax.axis_index("sy")
    count_y = lax.axis_size("sy")
    rows, taps, tile = a_tiles.shape[2], a_tiles.shape[3], a_tiles.shape[-1]
    tent = jnp.swapaxes(ptent.reshape(rows, tile, tile), 1, 2)
    lower_y, upper_y = shifted(tent, "sy", 1), shifted(tent, "sy", -1)
    lower_x, upper_x = shifted(tent, "sx", 1), shifted(tent, "sx", -1)
    left, right, to_lower_y, to_upper_y = slot_matrices(
        a_tiles.reshape(rows, taps, tile, tile),
        columns.reshape(rows * taps),
        dinv.reshape(rows, tile, tile),
        (lower_x, upper_x, tent, lower_y, upper_y),
        agg,
        jnp.stack([grid_x, grid_y]).astype(jnp.int32),
        count_y,
        MEMBERS,
    )
    from_lower_y, from_upper_y = shifted(to_upper_y, "sy", 1), shifted(to_lower_y, "sy", -1)
    to_lower_x, to_upper_x = partial_rows(left, right, 0, 2, jnp.bfloat16, MEMBERS, "rows_x")
    from_lower_x, from_upper_x = shifted(to_upper_x, "sx", 1), shifted(to_lower_x, "sx", -1)
    (own,) = partial_rows(left, right, OWN, 1, jnp.float32, MEMBERS, "rows_own")
    shards = (
        finished(
            ALONG_Y, ((0, 0), (0, -1), (0, 1)), (own, from_lower_y, from_upper_y), "along_y"
        ),
        finished(
            ALONG_X, ((0, 0), (-1, 0), (1, 0)), (own, from_lower_x, from_upper_x), "along_x"
        ),
        finished(
            MIXED,
            CROSS_SHIFTS,
            (from_lower_x, from_upper_x, own, from_lower_y, from_upper_y),
            "mixed",
        ),
    )
    out = None
    own_lists = lower_lists = upper_lists = GROUPS
    from_lower, from_upper = shards, shards
    for hop in range(1, count_y):
        limit = count_y - 1 - hop
        next_lower, next_upper, lower_kept, upper_kept = [], [], [], []
        for index, group in enumerate(GROUPS):
            lower = [o for o in lower_lists[index] if -WINDOW_SHIFTS[o][1] <= limit]
            upper = [o for o in upper_lists[index] if WINDOW_SHIFTS[o][1] <= limit]
            cut = len(lower_lists[index]) - len(lower)
            next_lower.append(shifted(from_lower[index][cut:], "sy", 1))
            next_upper.append(shifted(from_upper[index][: len(upper)], "sy", -1))
            lower_kept.append(tuple(lower))
            upper_kept.append(tuple(upper))
        from_lower, from_upper = tuple(next_lower), tuple(next_upper)
        lower_lists, upper_lists = tuple(lower_kept), tuple(upper_kept)
        has_lower, has_upper = grid_y >= hop, grid_y + hop < count_y
        targets = [
            jnp.where(has_lower, grid_y - hop, grid_y),
            jnp.where(has_upper, grid_y + hop, grid_y),
        ]
        kinds = [jnp.where(has_lower, 1, 0), jnp.where(has_upper, 2, 0)]
        if hop == 1:
            targets.append(grid_y)
            kinds.append(jnp.zeros_like(grid_y))
        out = placed(
            out,
            (shards, from_lower, from_upper),
            (own_lists, lower_lists, upper_lists),
            targets,
            kinds,
            count_y,
        )
    return out[None]


def solution(mesh):
    return jax.shard_map(
        local,
        mesh=mesh,
        in_specs=(
            P("sx", "sy", None, None, None, None),
            P("sx", "sy", None, None),
            P("sx", "sy", None, None, None),
            P("sx", "sy", None, None, None),
            P(),
        ),
        out_specs=P("sx", None, None, None, None, None, None),
        check_vma=False,
    )
```

```python
import functools

import jax
import jax.numpy as jnp
from jax import lax
from jax.experimental import pallas as pl
from jax.experimental.pallas import tpu as pltpu
from jax.sharding import PartitionSpec as P

CROSS_SHIFTS = ((0, -1), (0, 1), (-1, 0), (1, 0), (0, 0))
OWN = 4
WINDOW_SHIFTS = (
    (-2, 0),
    (-1, -1),
    (-1, 0),
    (-1, 1),
    (0, -2),
    (0, -1),
    (0, 0),
    (0, 1),
    (0, 2),
    (1, -1),
    (1, 0),
    (1, 1),
    (2, 0),
)
ALONG_Y = (4, 5, 7, 8)
REST = (1, 9, 0, 2, 6, 10, 12, 3, 11)
GROUPS = (ALONG_Y, REST)
smoothing = 2.0 / 3.0
MEMBERS = 2
ROWS_PER_STEP = 4
NT = (((1,), (1,)), ((), ()))


def shifted(x, axis, by):
    length = lax.axis_size(axis)
    pairs = [(i, i + by) for i in range(length) if 0 <= i + by < length]
    return lax.ppermute(x, axis, pairs)


def lane_tiles(g, tile, count=1):
    return pl.ds(pl.multiple_of(g * tile, tile), count * tile)


def own_kernel(count_y, rows, members, taps, columns, agg, place, a_ref, dinv_ref, tent, *refs):
    right, left, tiles, sources, slots, ends, found = refs[:7]
    sums = refs[7:]
    tile = a_ref.shape[-1]
    step = pl.program_id(0)

    @pl.when(step == 0)
    def _():
        found[0] = 0

    listed = found[0]
    for u in range(ROWS_PER_STEP):
        g = step * ROWS_PER_STEP + u
        total = sums[u]
        total[...] = jnp.zeros_like(total)
        own_member = 0
        for k in range(taps):
            target = columns[g * taps + k]
            holder = target // rows
            step_x = holder // count_y - place[0]
            step_y = holder % count_y - place[1]
            direction = jnp.where(
                step_y == -1,
                0,
                jnp.where(step_y == 1, 1, jnp.where(step_x == -1, 2, jnp.where(step_x == 1, 3, OWN))),
            )
            member = agg[target] % members
            if k == 0:
                own_member = member
            else:
                tiles[listed] = g * taps + k
                sources[listed] = direction * rows + target % rows
                slots[listed] = direction * members + member
                listed += jnp.where(direction == OWN, 0, 1)
            z = lax.dot_general(
                tent[target % rows], a_ref[u, k], NT, preferred_element_type=jnp.float32
            )
            slot = jnp.where(direction == OWN, member, members)
            total[lane_tiles(slot, tile), :] += z.astype(jnp.bfloat16).astype(jnp.float32)
        here = slice(u * tile, (u + 1) * tile)
        applied = total[: members * tile, :].astype(jnp.bfloat16)
        right[:, here] = applied
        smooth = lax.dot_general(applied, dinv_ref[u], NT, preferred_element_type=jnp.float32)
        total[: members * tile, :] = -smoothing * smooth
        total[lane_tiles(own_member, tile), :] += tent[g].astype(jnp.float32)
        left[:, here] = total[: members * tile, :].astype(jnp.bfloat16)
    found[0] = listed
    ends[step] = listed


def own_slots(a_tiles, columns, dinv, tent, agg, place, count_y, members):
    rows, taps, tile = a_tiles.shape[0], a_tiles.shape[1], a_tiles.shape[-1]
    steps = rows // ROWS_PER_STEP
    span = ROWS_PER_STEP * tile
    scalars = pl.BlockSpec(memory_space=pltpu.SMEM)
    return pl.pallas_call(
        functools.partial(own_kernel, count_y, rows, members, taps),
        grid_spec=pltpu.PrefetchScalarGridSpec(
            num_scalar_prefetch=3,
            grid=(steps,),
            in_specs=[
                pl.BlockSpec((ROWS_PER_STEP, taps, tile, tile), lambda s, *_: (s, 0, 0, 0)),
                pl.BlockSpec((ROWS_PER_STEP, tile, tile), lambda s, *_: (s, 0, 0)),
                pl.BlockSpec((rows, tile, tile), lambda s, *_: (0, 0, 0)),
            ],
            out_specs=[pl.BlockSpec((members * tile, span), lambda s, *_: (0, s))] * 2
            + [scalars] * 4,
            scratch_shapes=[pltpu.SMEM((1,), jnp.int32)]
            + [pltpu.VMEM(((members + 1) * tile, tile), jnp.float32)] * ROWS_PER_STEP,
        ),
        out_shape=[jax.ShapeDtypeStruct((members * tile, rows * tile), jnp.bfloat16)] * 2
        + [jax.ShapeDtypeStruct((rows * taps,), jnp.int32)] * 3
        + [jax.ShapeDtypeStruct((steps,), jnp.int32)],
        compiler_params=pltpu.CompilerParams(vmem_limit_bytes=24 * 1024 * 1024),
        cost_estimate=pl.CostEstimate(
            flops=2 * tile**3 * rows * (taps + members),
            bytes_accessed=2 * (a_tiles.size + dinv.size * 6),
            transcendentals=0,
        ),
        name="own_slots",
    )(columns, agg, place, a_tiles, dinv, tent)


def product(left, right, outs, members, tile):
    width = members * tile

    def one(d2, carry):
        value = lax.dot_general(
            left[...],
            right[lane_tiles(d2, width), :],
            NT,
            preferred_element_type=jnp.float32,
        )
        for d1, out in enumerate(outs):
            for m in range(members):
                for m2 in range(members):
                    row = (d1 * members + m) * tile
                    block = value[row : row + tile, m2 * tile : (m2 + 1) * tile]
                    out[d2, m, m2] = block.astype(out.dtype)
        return carry

    lax.fori_loop(0, 5, one, 0)


def smoothed_rows(left, right, first, count, dinv, g, tile):
    lanes = lane_tiles(g, tile)
    smooth = lax.dot_general(
        right[first : first + count, lanes], dinv[g], NT, preferred_element_type=jnp.float32
    )
    left[:count, lanes] = (-smoothing * smooth).astype(jnp.bfloat16)


def neighbour_kernel(members, taps, tiles, sources, slots, ends, *refs):
    a_tiles, dinv_hbm, *tents = refs[:6]
    right_own, to_lower, to_upper, right_out = refs[6:10]
    a_held, dinv, tent, right, left, sums, sems = refs[10:]
    tile = dinv.shape[-1]
    rows = dinv.shape[0]
    chunks = rows // ROWS_PER_STEP
    outer = 4 * members
    per = ROWS_PER_STEP * taps

    def a_copy(c):
        part = pl.ds(c * per, per)
        return pltpu.make_async_copy(a_tiles.at[part], a_held.at[part], sems.at[c])

    def out_copy(c):
        lanes = lane_tiles(c, ROWS_PER_STEP * tile)
        here = right.at[pl.ds(0, outer * tile), lanes]
        return pltpu.make_async_copy(here, right_out.at[:, lanes], sems.at[chunks + c])

    others = [
        pltpu.make_async_copy(source, tent.at[pl.ds(d * rows, rows)], sems.at[2 * chunks + d])
        for d, source in enumerate(tents)
    ]
    others.append(pltpu.make_async_copy(dinv_hbm, dinv, sems.at[2 * chunks + 4]))
    own_rows = right.at[pl.ds(outer * tile, members * tile), :]
    own_copy = pltpu.make_async_copy(right_own, own_rows, sems.at[2 * chunks + 5])
    for copy in others:
        copy.start()
    for c in range(chunks):
        a_copy(c).start()
    own_copy.start()
    for copy in others:
        copy.wait()

    def one_chunk(c, first):
        sums[...] = jnp.zeros_like(sums)
        a_copy(c).wait()
        last = ends[c]

        def some(n, carry):
            found = []
            for u in range(4):
                at = first + 4 * n + u
                index = jnp.minimum(at, last - 1)
                number = tiles[index]
                slot = jnp.where(at < last, slots[index], outer)
                z = lax.dot_general(
                    tent[sources[index]], a_held[number], NT, preferred_element_type=jnp.float32
                )
                found.append((slot, number // taps - c * ROWS_PER_STEP, z))
            for slot, row, z in found:
                at = (lane_tiles(slot, tile), lane_tiles(row, tile))
                sums[at] += z.astype(jnp.bfloat16).astype(jnp.float32)
            return carry

        lax.fori_loop(0, (last - first + 3) // 4, some, 0)
        lanes = lane_tiles(c, ROWS_PER_STEP * tile)
        right[: outer * tile, lanes] = sums[: outer * tile, :].astype(jnp.bfloat16)
        out_copy(c).start()
        for u in range(ROWS_PER_STEP):
            smoothed_rows(left, right, 0, 2 * members * tile, dinv, c * ROWS_PER_STEP + u, tile)
        return last

    lax.fori_loop(0, chunks, one_chunk, 0)
    own_copy.wait()
    product(left, right, (to_lower, to_upper), members, tile)
    for c in range(chunks):
        out_copy(c).wait()


def neighbour_slots(a_tiles, dinv, tents, own_right, lists, members):
    rows, taps, tile = a_tiles.shape[0], a_tiles.shape[1], a_tiles.shape[-1]
    block = (5, members, members, tile, tile)
    whole = pl.BlockSpec(block, lambda s, *_: (0,) * 5)
    anywhere = pl.BlockSpec(memory_space=pl.ANY)
    outer = 4 * members * tile
    chunks = rows // ROWS_PER_STEP
    return pl.pallas_call(
        functools.partial(neighbour_kernel, members, taps),
        grid_spec=pltpu.PrefetchScalarGridSpec(
            num_scalar_prefetch=4,
            grid=(1,),
            in_specs=[anywhere] * 7,
            out_specs=[whole, whole, anywhere],
            scratch_shapes=[
                pltpu.VMEM((rows * taps, tile, tile), jnp.bfloat16),
                pltpu.VMEM((rows, tile, tile), jnp.bfloat16),
                pltpu.VMEM((4 * rows, tile, tile), jnp.bfloat16),
                pltpu.VMEM((outer + members * tile, rows * tile), jnp.bfloat16),
                pltpu.VMEM((2 * members * tile, rows * tile), jnp.bfloat16),
                pltpu.VMEM((outer + tile, ROWS_PER_STEP * tile), jnp.float32),
                pltpu.SemaphoreType.DMA((2 * chunks + 6,)),
            ],
        ),
        out_shape=[jax.ShapeDtypeStruct(block, jnp.bfloat16)] * 2
        + [jax.ShapeDtypeStruct((outer, rows * tile), jnp.bfloat16)],
        compiler_params=pltpu.CompilerParams(vmem_limit_bytes=48 * 1024 * 1024),
        cost_estimate=pl.CostEstimate(
            flops=2 * tile**3 * rows * 2 * members * (1 + 5 * members),
            bytes_accessed=2 * (a_tiles.size + 16 * dinv.size),
            transcendentals=0,
        ),
        name="neighbour_slots",
    )(*lists, a_tiles.reshape(rows * taps, tile, tile), dinv, *tents, own_right)


def x_rows_kernel(members, dinv, right_outer, right_own, *refs):
    to_lower, to_upper, right, left, sems = refs
    rows, tile = dinv.shape[0], dinv.shape[-1]
    chunks = rows // ROWS_PER_STEP
    half = 2 * members * tile

    def x_copy(c):
        at = (pl.ds(half, half), lane_tiles(c, ROWS_PER_STEP * tile))
        return pltpu.make_async_copy(right_outer.at[at], right.at[at], sems.at[c])

    y_part = (pl.ds(0, half), slice(None))
    own_part = (pl.ds(2 * half, members * tile), slice(None))
    others = [
        pltpu.make_async_copy(right_outer.at[y_part], right.at[y_part], sems.at[chunks]),
        pltpu.make_async_copy(right_own, right.at[own_part], sems.at[chunks + 1]),
    ]
    for c in range(chunks):
        x_copy(c).start()
    for copy in others:
        copy.start()

    def one_chunk(c, carry):
        x_copy(c).wait()
        for u in range(ROWS_PER_STEP):
            smoothed_rows(left, right, half, half, dinv, c * ROWS_PER_STEP + u, tile)
        return carry

    lax.fori_loop(0, chunks, one_chunk, 0)
    for copy in others:
        copy.wait()
    product(left, right, (to_lower, to_upper), members, tile)


def x_rows(dinv, right_outer, right_own, members):
    rows, tile = dinv.shape[0], dinv.shape[-1]
    block = (5, members, members, tile, tile)
    anywhere = pl.BlockSpec(memory_space=pl.ANY)
    return pl.pallas_call(
        functools.partial(x_rows_kernel, members),
        grid=(1,),
        in_specs=[pl.BlockSpec(dinv.shape, lambda s: (0, 0, 0))] + [anywhere] * 2,
        out_specs=[pl.BlockSpec(block, lambda s: (0,) * 5)] * 2,
        out_shape=[jax.ShapeDtypeStruct(block, jnp.bfloat16)] * 2,
        scratch_shapes=[
            pltpu.VMEM((5 * members * tile, rows * tile), jnp.bfloat16),
            pltpu.VMEM((2 * members * tile, rows * tile), jnp.bfloat16),
            pltpu.SemaphoreType.DMA((rows // ROWS_PER_STEP + 2,)),
        ],
        compiler_params=pltpu.CompilerParams(vmem_limit_bytes=56 * 1024 * 1024),
        cost_estimate=pl.CostEstimate(
            flops=2 * tile**3 * rows * members * (2 + 10 * members),
            bytes_accessed=2 * 12 * members * tile * rows * tile,
            transcendentals=0,
        ),
        name="x_rows",
    )(dinv, right_outer, right_own)


def own_rows_kernel(members, right_outer, right_own, left_own, *refs):
    own, right, left, sems = refs
    tile = own.shape[-1]
    outer = 4 * members * tile
    copies = [
        pltpu.make_async_copy(left_own, left, sems.at[0]),
        pltpu.make_async_copy(right_outer, right.at[pl.ds(0, outer), :], sems.at[1]),
        pltpu.make_async_copy(
            right_own, right.at[pl.ds(outer, members * tile), :], sems.at[2]
        ),
    ]
    for copy in copies:
        copy.start()
    for copy in copies:
        copy.wait()
    product(left, right, (own,), members, tile)


def own_rows(right_outer, right_own, left_own, members):
    height, depth = left_own.shape
    tile = height // members
    block = (5, members, members, tile, tile)
    return pl.pallas_call(
        functools.partial(own_rows_kernel, members),
        grid=(1,),
        in_specs=[pl.BlockSpec(memory_space=pl.ANY)] * 3,
        out_specs=pl.BlockSpec(block, lambda s: (0,) * 5),
        out_shape=jax.ShapeDtypeStruct(block, jnp.float32),
        scratch_shapes=[
            pltpu.VMEM((5 * height, depth), jnp.bfloat16),
            pltpu.VMEM((height, depth), jnp.bfloat16),
            pltpu.SemaphoreType.DMA((3,)),
        ],
        compiler_params=pltpu.CompilerParams(vmem_limit_bytes=56 * 1024 * 1024),
        cost_estimate=pl.CostEstimate(
            flops=2 * height * height * depth,
            bytes_accessed=height * depth,
            transcendentals=0,
        ),
        name="own_rows",
    )(right_outer, right_own, left_own)


def window_kernel(group, shifts, *refs):
    out = refs[-1]
    for position, offset in enumerate(group):
        total = None
        for shift, values in zip(shifts, refs):
            for d, member in enumerate(CROSS_SHIFTS):
                if (shift[0] + member[0], shift[1] + member[1]) == WINDOW_SHIFTS[offset]:
                    term = values[d].astype(jnp.float32)
                    total = term if total is None else total + term
        out[position] = total.astype(out.dtype)


def finished(group, shifts, blocks, name):
    _, members, _, tile, _ = blocks[0].shape
    spec = lambda lead: pl.BlockSpec(
        (lead, 1, members, tile, tile), lambda m: (0, m, 0, 0, 0)
    )
    shape = (len(group), members, members, tile, tile)
    return pl.pallas_call(
        functools.partial(window_kernel, group, shifts),
        grid=(members,),
        in_specs=[spec(5)] * len(blocks),
        out_specs=spec(len(group)),
        out_shape=jax.ShapeDtypeStruct(shape, jnp.bfloat16),
        compiler_params=pltpu.CompilerParams(vmem_limit_bytes=32 * 1024 * 1024),
        cost_estimate=pl.CostEstimate(
            flops=5 * blocks[0].size, bytes_accessed=8 * blocks[0].size, transcendentals=0
        ),
        name=name,
    )(*blocks)


def place_kernel(positions, row, kind, *refs):
    out = refs[-1]
    entry = pl.program_id(1)
    per = len(GROUPS)
    for source, lists in enumerate(positions):

        @pl.when(kind[entry] == source)
        def _():
            held = set()
            for index, offsets in enumerate(lists):
                for p, offset in enumerate(offsets):
                    out[0, 0, offset] = refs[source * per + index][p, 0]
                    held.add(offset)
            for offset in range(13):
                if offset not in held:
                    out[0, 0, offset] = jnp.zeros(out.shape[3:], out.dtype)


def placed(out, shards, positions, rows, kinds, count):
    arrays = [array for shard in shards for array in shard]
    members, _, tile, _ = arrays[0].shape[1:]
    in_specs = [
        pl.BlockSpec((a.shape[0], 1, members, tile, tile), lambda m, e, *_: (0, m, 0, 0, 0))
        for a in arrays
    ]
    shape = (count, members, 13, members, tile, tile)
    operands = list(arrays)
    if out is not None:
        in_specs.append(pl.BlockSpec(memory_space=pl.ANY))
        operands.append(out)
    return pl.pallas_call(
        functools.partial(place_kernel, positions),
        grid_spec=pltpu.PrefetchScalarGridSpec(
            num_scalar_prefetch=2,
            grid=(members, len(rows)),
            in_specs=in_specs,
            out_specs=pl.BlockSpec(
                (1, 1, 13, members, tile, tile),
                lambda m, e, row, kind: (row[e], m, 0, 0, 0, 0),
            ),
        ),
        out_shape=jax.ShapeDtypeStruct(shape, jnp.bfloat16),
        input_output_aliases={2 + len(arrays): 0} if out is not None else {},
        compiler_params=pltpu.CompilerParams(vmem_limit_bytes=32 * 1024 * 1024),
        cost_estimate=pl.CostEstimate(
            flops=0, bytes_accessed=10 * 13 * members * members * tile * tile, transcendentals=0
        ),
        name="placed",
    )(jnp.stack(rows).astype(jnp.int32), jnp.stack(kinds).astype(jnp.int32), *operands)


def hopped(shard, lists, hop, count_y):
    limit = count_y - 1 - hop
    lower = tuple(o for o in lists[0] if -WINDOW_SHIFTS[o][1] <= limit)
    upper = tuple(o for o in lists[1] if WINDOW_SHIFTS[o][1] <= limit)
    cut = len(lists[0]) - len(lower)
    arrived = (
        shifted(shard[0][cut:], "sy", 1),
        shifted(shard[1][: len(upper)], "sy", -1),
    )
    return arrived, (lower, upper)


def gathered_rows(along_y, rest_of, inputs, grid_y, count_y):
    ahead, ahead_lists = hopped((along_y, along_y), (ALONG_Y, ALONG_Y), 1, count_y)
    inputs, ahead = lax.optimization_barrier((inputs, ahead))
    rest = rest_of(inputs)
    shards = [along_y, rest]
    behind, behind_lists = (rest, rest), (REST, REST)
    arrivals, lists = [shards], [GROUPS]
    entries = ([grid_y], [jnp.zeros_like(grid_y)])
    out = None
    for hop in range(1, count_y):
        now, now_lists = ahead, ahead_lists
        if hop + 1 < count_y:
            ahead, ahead_lists = hopped(ahead, ahead_lists, hop + 1, count_y)
        behind, behind_lists = hopped(behind, behind_lists, hop, count_y)
        out = placed(out, arrivals, lists, *entries, count_y)
        behind, ahead, out = lax.optimization_barrier((behind, ahead, out))
        lists = [GROUPS, (now_lists[0], behind_lists[0]), (now_lists[1], behind_lists[1])]
        arrivals = [shards, (now[0], behind[0]), (now[1], behind[1])]
        has_lower, has_upper = grid_y >= hop, grid_y + hop < count_y
        entries = (
            [
                jnp.where(has_lower, grid_y - hop, grid_y),
                jnp.where(has_upper, grid_y + hop, grid_y),
            ],
            [jnp.where(has_lower, 1, 0), jnp.where(has_upper, 2, 0)],
        )
    return placed(out, arrivals, lists, *entries, count_y)


def local(a_tiles, columns, ptent, dinv, agg):
    grid_x = lax.axis_index("sx")
    grid_y = lax.axis_index("sy")
    count_y = lax.axis_size("sy")
    rows, taps, tile = a_tiles.shape[2], a_tiles.shape[3], a_tiles.shape[-1]
    coupling = a_tiles.reshape(rows, taps, tile, tile)
    inverse = dinv.reshape(rows, tile, tile)
    tent = jnp.swapaxes(ptent.reshape(rows, tile, tile), 1, 2)
    tents = (
        shifted(tent, "sy", 1),
        shifted(tent, "sy", -1),
        shifted(tent, "sx", 1),
        shifted(tent, "sx", -1),
    )
    own_right, own_left, *lists = own_slots(
        coupling,
        columns.reshape(rows * taps),
        inverse,
        tent,
        agg,
        jnp.stack([grid_x, grid_y]).astype(jnp.int32),
        count_y,
        MEMBERS,
    )
    to_lower_y, to_upper_y, outer_right = neighbour_slots(
        coupling, inverse, tents, own_right, lists, MEMBERS
    )
    from_lower_y, from_upper_y = shifted(to_upper_y, "sy", 1), shifted(to_lower_y, "sy", -1)
    to_lower_x, to_upper_x = x_rows(inverse, outer_right, own_right, MEMBERS)
    from_lower_x, from_upper_x = shifted(to_upper_x, "sx", 1), shifted(to_lower_x, "sx", -1)
    own = own_rows(outer_right, own_right, own_left, MEMBERS)
    along_y = finished(
        ALONG_Y, ((0, -1), (0, 1), (0, 0)), (from_lower_y, from_upper_y, own), "along_y"
    )
    rest_of = functools.partial(finished, REST, CROSS_SHIFTS, name="rest")
    inputs = (from_lower_y, from_upper_y, from_lower_x, from_upper_x, own)
    return gathered_rows(along_y, rest_of, inputs, grid_y, count_y)[None]


def solution(mesh):
    return jax.shard_map(
        local,
        mesh=mesh,
        in_specs=(
            P("sx", "sy", None, None, None, None),
            P("sx", "sy", None, None),
            P("sx", "sy", None, None, None),
            P("sx", "sy", None, None, None),
            P(),
        ),
        out_specs=P("sx", None, None, None, None, None, None),
        check_vma=False,
    )
```

```python
import functools

import jax
import jax.numpy as jnp
from jax import lax
from jax.experimental import pallas as pl
from jax.experimental.pallas import tpu as pltpu
from jax.sharding import PartitionSpec as P

CROSS_SHIFTS = ((0, -1), (0, 1), (-1, 0), (1, 0), (0, 0))
OWN = 4
WINDOW_SHIFTS = (
    (-2, 0),
    (-1, -1),
    (-1, 0),
    (-1, 1),
    (0, -2),
    (0, -1),
    (0, 0),
    (0, 1),
    (0, 2),
    (1, -1),
    (1, 0),
    (1, 1),
    (2, 0),
)
ALONG_Y = (4, 5, 7, 8)
REST = (1, 9, 0, 2, 6, 10, 12, 3, 11)
GROUPS = (ALONG_Y, REST)
smoothing = 2.0 / 3.0
MEMBERS = 2
ROWS_PER_STEP = 4
NT = (((1,), (1,)), ((), ()))


def shifted(x, axis, by):
    length = lax.axis_size(axis)
    pairs = [(i, i + by) for i in range(length) if 0 <= i + by < length]
    return lax.ppermute(x, axis, pairs)


def lane_tiles(g, tile, count=1):
    return pl.ds(pl.multiple_of(g * tile, tile), count * tile)


def own_kernel(count_y, rows, members, taps, columns, agg, place, a_ref, dinv_ref, tent, *refs):
    right, left, tiles, sources, slots, ends, found = refs[:7]
    sums = refs[7:]
    tile = a_ref.shape[-1]
    step = pl.program_id(0)

    @pl.when(step == 0)
    def _():
        found[0] = 0

    listed = found[0]
    for u in range(ROWS_PER_STEP):
        g = step * ROWS_PER_STEP + u
        total = sums[u]
        total[...] = jnp.zeros_like(total)
        own_member = 0
        for k in range(taps):
            target = columns[g * taps + k]
            holder = target // rows
            step_x = holder // count_y - place[0]
            step_y = holder % count_y - place[1]
            direction = jnp.where(
                step_y == -1,
                0,
                jnp.where(step_y == 1, 1, jnp.where(step_x == -1, 2, jnp.where(step_x == 1, 3, OWN))),
            )
            member = agg[target] % members
            if k == 0:
                own_member = member
            else:
                tiles[listed] = g * taps + k
                sources[listed] = direction * rows + target % rows
                slots[listed] = direction * members + member
                listed += jnp.where(direction == OWN, 0, 1)
            z = lax.dot_general(
                tent[target % rows], a_ref[u, k], NT, preferred_element_type=jnp.float32
            )
            slot = jnp.where(direction == OWN, member, members)
            total[lane_tiles(slot, tile), :] += z.astype(jnp.bfloat16).astype(jnp.float32)
        here = slice(u * tile, (u + 1) * tile)
        applied = total[: members * tile, :].astype(jnp.bfloat16)
        right[:, here] = applied
        smooth = lax.dot_general(applied, dinv_ref[u], NT, preferred_element_type=jnp.float32)
        total[: members * tile, :] = -smoothing * smooth
        total[lane_tiles(own_member, tile), :] += tent[g].astype(jnp.float32)
        left[:, here] = total[: members * tile, :].astype(jnp.bfloat16)
    found[0] = listed
    ends[step] = listed


def own_slots(a_tiles, columns, dinv, tent, agg, place, count_y, members):
    rows, taps, tile = a_tiles.shape[0], a_tiles.shape[1], a_tiles.shape[-1]
    steps = rows // ROWS_PER_STEP
    span = ROWS_PER_STEP * tile
    scalars = pl.BlockSpec(memory_space=pltpu.SMEM)
    return pl.pallas_call(
        functools.partial(own_kernel, count_y, rows, members, taps),
        grid_spec=pltpu.PrefetchScalarGridSpec(
            num_scalar_prefetch=3,
            grid=(steps,),
            in_specs=[
                pl.BlockSpec((ROWS_PER_STEP, taps, tile, tile), lambda s, *_: (s, 0, 0, 0)),
                pl.BlockSpec((ROWS_PER_STEP, tile, tile), lambda s, *_: (s, 0, 0)),
                pl.BlockSpec((rows, tile, tile), lambda s, *_: (0, 0, 0)),
            ],
            out_specs=[pl.BlockSpec((members * tile, span), lambda s, *_: (0, s))] * 2
            + [scalars] * 4,
            scratch_shapes=[pltpu.SMEM((1,), jnp.int32)]
            + [pltpu.VMEM(((members + 1) * tile, tile), jnp.float32)] * ROWS_PER_STEP,
        ),
        out_shape=[jax.ShapeDtypeStruct((members * tile, rows * tile), jnp.bfloat16)] * 2
        + [jax.ShapeDtypeStruct((rows * taps,), jnp.int32)] * 3
        + [jax.ShapeDtypeStruct((steps,), jnp.int32)],
        compiler_params=pltpu.CompilerParams(vmem_limit_bytes=24 * 1024 * 1024),
        cost_estimate=pl.CostEstimate(
            flops=2 * tile**3 * rows * (taps + members),
            bytes_accessed=2 * (a_tiles.size + dinv.size * 6),
            transcendentals=0,
        ),
        name="own_slots",
    )(columns, agg, place, a_tiles, dinv, tent)


def product(left, right, outs, members, tile):
    width = members * tile

    def one(d2, carry):
        value = lax.dot_general(
            left[...],
            right[lane_tiles(d2, width), :],
            NT,
            preferred_element_type=jnp.float32,
        )
        for d1, out in enumerate(outs):
            for m in range(members):
                for m2 in range(members):
                    row = (d1 * members + m) * tile
                    block = value[row : row + tile, m2 * tile : (m2 + 1) * tile]
                    out[d2, m, m2] = block.astype(out.dtype)
        return carry

    lax.fori_loop(0, 5, one, 0)


def smoothed_rows(left, right, first, count, dinv, g, tile):
    lanes = lane_tiles(g, tile)
    smooth = lax.dot_general(
        right[first : first + count, lanes], dinv[g], NT, preferred_element_type=jnp.float32
    )
    left[:count, lanes] = (-smoothing * smooth).astype(jnp.bfloat16)


def neighbour_kernel(members, taps, tiles, sources, slots, ends, *refs):
    a_tiles, dinv_hbm, *tents = refs[:6]
    right_own, to_lower, to_upper, right_out = refs[6:10]
    a_held, dinv, tent, right, left, sums, sems = refs[10:]
    tile = dinv.shape[-1]
    rows = dinv.shape[0]
    chunks = rows // ROWS_PER_STEP
    outer = 4 * members
    per = ROWS_PER_STEP * taps

    def a_copy(c):
        part = pl.ds(c * per, per)
        return pltpu.make_async_copy(a_tiles.at[part], a_held.at[part], sems.at[c])

    def out_copy(c):
        lanes = lane_tiles(c, ROWS_PER_STEP * tile)
        here = right.at[pl.ds(0, outer * tile), lanes]
        return pltpu.make_async_copy(here, right_out.at[:, lanes], sems.at[chunks + c])

    others = [
        pltpu.make_async_copy(source, tent.at[pl.ds(d * rows, rows)], sems.at[2 * chunks + d])
        for d, source in enumerate(tents)
    ]
    others.append(pltpu.make_async_copy(dinv_hbm, dinv, sems.at[2 * chunks + 4]))
    own_rows = right.at[pl.ds(outer * tile, members * tile), :]
    own_copy = pltpu.make_async_copy(right_own, own_rows, sems.at[2 * chunks + 5])
    for copy in others:
        copy.start()
    for c in range(chunks):
        a_copy(c).start()
    own_copy.start()
    for copy in others:
        copy.wait()

    def one_chunk(c, first):
        sums[...] = jnp.zeros_like(sums)
        a_copy(c).wait()
        last = ends[c]

        def some(n, carry):
            found = []
            for u in range(4):
                at = first + 4 * n + u
                index = jnp.minimum(at, last - 1)
                number = tiles[index]
                slot = jnp.where(at < last, slots[index], outer)
                z = lax.dot_general(
                    tent[sources[index]], a_held[number], NT, preferred_element_type=jnp.float32
                )
                found.append((slot, number // taps - c * ROWS_PER_STEP, z))
            for slot, row, z in found:
                at = (lane_tiles(slot, tile), lane_tiles(row, tile))
                sums[at] += z.astype(jnp.bfloat16).astype(jnp.float32)
            return carry

        lax.fori_loop(0, (last - first + 3) // 4, some, 0)
        lanes = lane_tiles(c, ROWS_PER_STEP * tile)
        right[: outer * tile, lanes] = sums[: outer * tile, :].astype(jnp.bfloat16)
        out_copy(c).start()
        for u in range(ROWS_PER_STEP):
            smoothed_rows(left, right, 0, 2 * members * tile, dinv, c * ROWS_PER_STEP + u, tile)
        return last

    lax.fori_loop(0, chunks, one_chunk, 0)
    own_copy.wait()
    product(left, right, (to_lower, to_upper), members, tile)
    for c in range(chunks):
        out_copy(c).wait()


def neighbour_slots(a_tiles, dinv, tents, own_right, lists, members):
    rows, taps, tile = a_tiles.shape[0], a_tiles.shape[1], a_tiles.shape[-1]
    block = (5, members, members, tile, tile)
    whole = pl.BlockSpec(block, lambda s, *_: (0,) * 5)
    anywhere = pl.BlockSpec(memory_space=pl.ANY)
    outer = 4 * members * tile
    chunks = rows // ROWS_PER_STEP
    return pl.pallas_call(
        functools.partial(neighbour_kernel, members, taps),
        grid_spec=pltpu.PrefetchScalarGridSpec(
            num_scalar_prefetch=4,
            grid=(1,),
            in_specs=[anywhere] * 7,
            out_specs=[whole, whole, anywhere],
            scratch_shapes=[
                pltpu.VMEM((rows * taps, tile, tile), jnp.bfloat16),
                pltpu.VMEM((rows, tile, tile), jnp.bfloat16),
                pltpu.VMEM((4 * rows, tile, tile), jnp.bfloat16),
                pltpu.VMEM((outer + members * tile, rows * tile), jnp.bfloat16),
                pltpu.VMEM((2 * members * tile, rows * tile), jnp.bfloat16),
                pltpu.VMEM((outer + tile, ROWS_PER_STEP * tile), jnp.float32),
                pltpu.SemaphoreType.DMA((2 * chunks + 6,)),
            ],
        ),
        out_shape=[jax.ShapeDtypeStruct(block, jnp.bfloat16)] * 2
        + [jax.ShapeDtypeStruct((outer, rows * tile), jnp.bfloat16)],
        compiler_params=pltpu.CompilerParams(vmem_limit_bytes=48 * 1024 * 1024),
        cost_estimate=pl.CostEstimate(
            flops=2 * tile**3 * rows * 2 * members * (1 + 5 * members),
            bytes_accessed=2 * (a_tiles.size + 16 * dinv.size),
            transcendentals=0,
        ),
        name="neighbour_slots",
    )(*lists, a_tiles.reshape(rows * taps, tile, tile), dinv, *tents, own_right)


def other_rows_kernel(members, dinv, right_outer, right_own, left_own, *refs):
    to_lower, to_upper, own, right, left, sems = refs
    rows, tile = dinv.shape[0], dinv.shape[-1]
    chunks = rows // ROWS_PER_STEP
    half = 2 * members * tile

    def x_copy(c):
        at = (pl.ds(half, half), lane_tiles(c, ROWS_PER_STEP * tile))
        return pltpu.make_async_copy(right_outer.at[at], right.at[at], sems.at[c])

    y_part = (pl.ds(0, half), slice(None))
    own_part = (pl.ds(2 * half, members * tile), slice(None))
    left_part = (pl.ds(half, members * tile), slice(None))
    others = [
        pltpu.make_async_copy(right_outer.at[y_part], right.at[y_part], sems.at[chunks]),
        pltpu.make_async_copy(right_own, right.at[own_part], sems.at[chunks + 1]),
        pltpu.make_async_copy(left_own, left.at[left_part], sems.at[chunks + 2]),
    ]
    for c in range(chunks):
        x_copy(c).start()
    for copy in others:
        copy.start()

    def one_chunk(c, carry):
        x_copy(c).wait()
        for u in range(ROWS_PER_STEP):
            smoothed_rows(left, right, half, half, dinv, c * ROWS_PER_STEP + u, tile)
        return carry

    lax.fori_loop(0, chunks, one_chunk, 0)
    for copy in others:
        copy.wait()
    product(left, right, (to_lower, to_upper, own), members, tile)


def other_rows(dinv, right_outer, right_own, left_own, members):
    rows, tile = dinv.shape[0], dinv.shape[-1]
    block = (5, members, members, tile, tile)
    anywhere = pl.BlockSpec(memory_space=pl.ANY)
    return pl.pallas_call(
        functools.partial(other_rows_kernel, members),
        grid=(1,),
        in_specs=[pl.BlockSpec(dinv.shape, lambda s: (0, 0, 0))] + [anywhere] * 3,
        out_specs=[pl.BlockSpec(block, lambda s: (0,) * 5)] * 3,
        out_shape=[jax.ShapeDtypeStruct(block, jnp.bfloat16)] * 2
        + [jax.ShapeDtypeStruct(block, jnp.float32)],
        scratch_shapes=[
            pltpu.VMEM((5 * members * tile, rows * tile), jnp.bfloat16),
            pltpu.VMEM((3 * members * tile, rows * tile), jnp.bfloat16),
            pltpu.SemaphoreType.DMA((rows // ROWS_PER_STEP + 3,)),
        ],
        compiler_params=pltpu.CompilerParams(vmem_limit_bytes=56 * 1024 * 1024),
        cost_estimate=pl.CostEstimate(
            flops=2 * tile**3 * rows * members * (2 + 15 * members),
            bytes_accessed=2 * 14 * members * tile * rows * tile,
            transcendentals=0,
        ),
        name="other_rows",
    )(dinv, right_outer, right_own, left_own)


def window_kernel(group, shifts, *refs):
    out = refs[-1]
    for position, offset in enumerate(group):
        total = None
        for shift, values in zip(shifts, refs):
            for d, member in enumerate(CROSS_SHIFTS):
                if (shift[0] + member[0], shift[1] + member[1]) == WINDOW_SHIFTS[offset]:
                    term = values[d].astype(jnp.float32)
                    total = term if total is None else total + term
        out[position] = total.astype(out.dtype)


def finished(group, shifts, blocks, name):
    _, members, _, tile, _ = blocks[0].shape
    spec = lambda lead: pl.BlockSpec(
        (lead, 1, members, tile, tile), lambda m: (0, m, 0, 0, 0)
    )
    shape = (len(group), members, members, tile, tile)
    return pl.pallas_call(
        functools.partial(window_kernel, group, shifts),
        grid=(members,),
        in_specs=[spec(5)] * len(blocks),
        out_specs=spec(len(group)),
        out_shape=jax.ShapeDtypeStruct(shape, jnp.bfloat16),
        compiler_params=pltpu.CompilerParams(vmem_limit_bytes=32 * 1024 * 1024),
        cost_estimate=pl.CostEstimate(
            flops=5 * blocks[0].size, bytes_accessed=8 * blocks[0].size, transcendentals=0
        ),
        name=name,
    )(*blocks)


def place_kernel(sources, row, kind, *refs):
    out = refs[-1]
    entry = pl.program_id(1)
    for source, (held, lists) in enumerate(sources):

        @pl.when(kind[entry] == source)
        def _():
            written = set()
            for array, offsets in zip(held, lists):
                for p, offset in enumerate(offsets):
                    out[0, 0, offset] = refs[array][p, 0]
                    written.add(offset)
            for offset in range(13):
                if offset not in written:
                    out[0, 0, offset] = jnp.zeros(out.shape[3:], out.dtype)


def placed(out, arrays, sources, entries, count):
    rows, kinds = entries
    members, _, tile, _ = arrays[0].shape[1:]
    in_specs = [
        pl.BlockSpec((a.shape[0], 1, members, tile, tile), lambda m, e, *_: (0, m, 0, 0, 0))
        for a in arrays
    ]
    shape = (count, members, 13, members, tile, tile)
    operands = list(arrays)
    if out is not None:
        in_specs.append(pl.BlockSpec(memory_space=pl.ANY))
        operands.append(out)
    return pl.pallas_call(
        functools.partial(place_kernel, sources),
        grid_spec=pltpu.PrefetchScalarGridSpec(
            num_scalar_prefetch=2,
            grid=(members, len(rows)),
            in_specs=in_specs,
            out_specs=pl.BlockSpec(
                (1, 1, 13, members, tile, tile),
                lambda m, e, row, kind: (row[e], m, 0, 0, 0, 0),
            ),
        ),
        out_shape=jax.ShapeDtypeStruct(shape, jnp.bfloat16),
        input_output_aliases={2 + len(arrays): 0} if out is not None else {},
        compiler_params=pltpu.CompilerParams(vmem_limit_bytes=32 * 1024 * 1024),
        cost_estimate=pl.CostEstimate(
            flops=0, bytes_accessed=6 * 13 * members * members * tile * tile, transcendentals=0
        ),
        name="placed",
    )(jnp.stack(rows).astype(jnp.int32), jnp.stack(kinds).astype(jnp.int32), *operands)


def hopped(shard, lists, hop, count_y):
    limit = count_y - 1 - hop
    lower = tuple(o for o in lists[0] if -WINDOW_SHIFTS[o][1] <= limit)
    upper = tuple(o for o in lists[1] if WINDOW_SHIFTS[o][1] <= limit)
    cut = len(lists[0]) - len(lower)
    arrived = (
        shifted(shard[0][cut:], "sy", 1),
        shifted(shard[1][: len(upper)], "sy", -1),
    )
    return arrived, (lower, upper)


def end_to_end(shard, group, grid_y, count_y):
    lower = tuple(o for o in group if WINDOW_SHIFTS[o][1] >= 0)
    upper = tuple(o for o in group if WINDOW_SHIFTS[o][1] <= 0)
    first = jnp.where(grid_y == 0, len(group) - len(lower), 0)
    sent = lax.dynamic_slice_in_dim(shard, first, len(lower), axis=0)
    last = count_y - 1
    return lax.ppermute(sent, "sy", [(0, last), (last, 0)]), (lower, upper)


def gathered_rows(along_y, rest_of, inputs, grid_y, count_y):
    first = hopped((along_y, along_y), (ALONG_Y, ALONG_Y), 1, count_y)
    inputs, moved = lax.optimization_barrier((inputs, first[0]))
    first = (moved, first[1])
    rest = rest_of(inputs)
    shards = [along_y, rest]
    ends = [end_to_end(shard, group, grid_y, count_y) for shard, group in zip(shards, GROUPS)]
    own = ((0, 1), GROUPS)
    out = None
    arrays, sources, entries = shards, (own,), ([grid_y], [jnp.zeros_like(grid_y)])
    chains = [None, ((rest, rest), (REST, REST))]
    ahead = first
    for hop in range(1, count_y - 1):
        chains[0] = ahead
        if hop + 2 < count_y:
            ahead = hopped(*ahead, hop + 1, count_y)
        chains[1] = hopped(*chains[1], hop, count_y)
        out = placed(out, arrays, sources, entries, count_y)
        behind = [chains[1][0], ahead[0]] + ([moved for moved, _ in ends] if hop == 1 else [])
        behind, out = lax.optimization_barrier((behind, out))
        chains[1], ahead = (behind[0], chains[1][1]), (behind[1], ahead[1])
        if hop == 1:
            ends = [(moved, lists) for moved, (_, lists) in zip(behind[2:], ends)]
        arrays = [chain[0][side] for side in (0, 1) for chain in chains]
        sources = tuple(
            ((2 * side, 2 * side + 1), tuple(chain[1][side] for chain in chains))
            for side in (0, 1)
        )
        has_lower, has_upper = grid_y >= hop, grid_y + hop < count_y
        lower, upper = (grid_y - hop, 0), (grid_y + hop, 1)
        spare = (lower, upper)
        if 2 * hop > count_y:
            arrays, sources = arrays + shards, sources + (((4, 5), GROUPS),)
            spare = ((grid_y, 2), (grid_y, 2))
        chosen = [
            tuple(jnp.where(has_lower, a, b) for a, b in zip(lower, spare[1])),
            tuple(jnp.where(has_upper, a, b) for a, b in zip(upper, spare[0])),
        ]
        if hop == 1:
            base, kind = len(arrays), len(sources)
            arrays = arrays + [moved for moved, _ in ends]
            sources = sources + tuple(
                ((base, base + 1), tuple(lists[side] for _, lists in ends)) for side in (0, 1)
            )
            at_end = [
                jnp.where(grid_y == 0, a, jnp.where(grid_y == count_y - 1, b, c))
                for a, b, c in zip((count_y - 1, kind + 1), (0, kind), chosen[1])
            ]
            chosen.append(tuple(at_end))
        entries = ([row for row, _ in chosen], [kind for _, kind in chosen])
    return placed(out, arrays, sources, entries, count_y)


def local(a_tiles, columns, ptent, dinv, agg):
    grid_x = lax.axis_index("sx")
    grid_y = lax.axis_index("sy")
    count_y = lax.axis_size("sy")
    rows, taps, tile = a_tiles.shape[2], a_tiles.shape[3], a_tiles.shape[-1]
    coupling = a_tiles.reshape(rows, taps, tile, tile)
    inverse = dinv.reshape(rows, tile, tile)
    tent = jnp.swapaxes(ptent.reshape(rows, tile, tile), 1, 2)
    tents = (
        shifted(tent, "sy", 1),
        shifted(tent, "sy", -1),
        shifted(tent, "sx", 1),
        shifted(tent, "sx", -1),
    )
    own_right, own_left, *lists = own_slots(
        coupling,
        columns.reshape(rows * taps),
        inverse,
        tent,
        agg,
        jnp.stack([grid_x, grid_y]).astype(jnp.int32),
        count_y,
        MEMBERS,
    )
    to_lower_y, to_upper_y, outer_right = neighbour_slots(
        coupling, inverse, tents, own_right, lists, MEMBERS
    )
    from_lower_y, from_upper_y = shifted(to_upper_y, "sy", 1), shifted(to_lower_y, "sy", -1)
    to_lower_x, to_upper_x, own = other_rows(inverse, outer_right, own_right, own_left, MEMBERS)
    from_lower_x, from_upper_x = shifted(to_upper_x, "sx", 1), shifted(to_lower_x, "sx", -1)
    along_y = finished(
        ALONG_Y, ((0, -1), (0, 1), (0, 0)), (from_lower_y, from_upper_y, own), "along_y"
    )
    rest_of = functools.partial(finished, REST, CROSS_SHIFTS, name="rest")
    inputs = (from_lower_y, from_upper_y, from_lower_x, from_upper_x, own)
    return gathered_rows(along_y, rest_of, inputs, grid_y, count_y)[None]


def solution(mesh):
    return jax.shard_map(
        local,
        mesh=mesh,
        in_specs=(
            P("sx", "sy", None, None, None, None),
            P("sx", "sy", None, None),
            P("sx", "sy", None, None, None),
            P("sx", "sy", None, None, None),
            P(),
        ),
        out_specs=P("sx", None, None, None, None, None, None),
        check_vma=False,
    )
```

```python
import functools

import jax
import jax.numpy as jnp
from jax import lax
from jax.experimental import pallas as pl
from jax.experimental.pallas import tpu as pltpu
from jax.sharding import PartitionSpec as P

CROSS_SHIFTS = ((0, -1), (0, 1), (-1, 0), (1, 0), (0, 0))
OWN = 4
WINDOW_SHIFTS = (
    (-2, 0),
    (-1, -1),
    (-1, 0),
    (-1, 1),
    (0, -2),
    (0, -1),
    (0, 0),
    (0, 1),
    (0, 2),
    (1, -1),
    (1, 0),
    (1, 1),
    (2, 0),
)
ALONG_Y = (4, 5, 7, 8)
REST = (1, 9, 0, 2, 6, 10, 12, 3, 11)
GROUPS = (ALONG_Y, REST)
smoothing = 2.0 / 3.0
MEMBERS = 2
ROWS_PER_STEP = 4
UNROLL = 8
NT = (((1,), (1,)), ((), ()))


def shifted(x, axis, by):
    length = lax.axis_size(axis)
    pairs = [(i, i + by) for i in range(length) if 0 <= i + by < length]
    return lax.ppermute(x, axis, pairs)


def lane_tiles(g, tile, count=1):
    return pl.ds(pl.multiple_of(g * tile, tile), count * tile)


def own_kernel(count_y, rows, members, taps, columns, agg, place, a_ref, dinv_ref, tent, *refs):
    right, left, tiles, sources, slots, ends, found = refs[:7]
    sums = refs[7:]
    tile = a_ref.shape[-1]
    step = pl.program_id(0)

    @pl.when(step == 0)
    def _():
        found[0] = 0

    listed = found[0]
    for u in range(ROWS_PER_STEP):
        g = step * ROWS_PER_STEP + u
        total = sums[u]
        total[...] = jnp.zeros_like(total)
        own_member = 0
        for k in range(taps):
            target = columns[g * taps + k]
            holder = target // rows
            step_x = holder // count_y - place[0]
            step_y = holder % count_y - place[1]
            direction = jnp.where(
                step_y == -1,
                0,
                jnp.where(step_y == 1, 1, jnp.where(step_x == -1, 2, jnp.where(step_x == 1, 3, OWN))),
            )
            member = agg[target] % members
            if k == 0:
                own_member = member
            else:
                tiles[listed] = g * taps + k
                sources[listed] = direction * rows + target % rows
                slots[listed] = direction * members + member
                listed += jnp.where(direction == OWN, 0, 1)
            z = lax.dot_general(
                tent[target % rows], a_ref[u, k], NT, preferred_element_type=jnp.float32
            )
            slot = jnp.where(direction == OWN, member, members)
            total[lane_tiles(slot, tile), :] += z.astype(jnp.bfloat16).astype(jnp.float32)
        here = slice(u * tile, (u + 1) * tile)
        applied = total[: members * tile, :].astype(jnp.bfloat16)
        right[:, here] = applied
        smooth = lax.dot_general(applied, dinv_ref[u], NT, preferred_element_type=jnp.float32)
        total[: members * tile, :] = -smoothing * smooth
        total[lane_tiles(own_member, tile), :] += tent[g].astype(jnp.float32)
        left[:, here] = total[: members * tile, :].astype(jnp.bfloat16)
    found[0] = listed
    ends[step] = listed


def own_slots(a_tiles, columns, dinv, tent, agg, place, count_y, members):
    rows, taps, tile = a_tiles.shape[0], a_tiles.shape[1], a_tiles.shape[-1]
    steps = rows // ROWS_PER_STEP
    span = ROWS_PER_STEP * tile
    scalars = pl.BlockSpec(memory_space=pltpu.SMEM)
    return pl.pallas_call(
        functools.partial(own_kernel, count_y, rows, members, taps),
        grid_spec=pltpu.PrefetchScalarGridSpec(
            num_scalar_prefetch=3,
            grid=(steps,),
            in_specs=[
                pl.BlockSpec((ROWS_PER_STEP, taps, tile, tile), lambda s, *_: (s, 0, 0, 0)),
                pl.BlockSpec((ROWS_PER_STEP, tile, tile), lambda s, *_: (s, 0, 0)),
                pl.BlockSpec((rows, tile, tile), lambda s, *_: (0, 0, 0)),
            ],
            out_specs=[pl.BlockSpec((members * tile, span), lambda s, *_: (0, s))] * 2
            + [scalars] * 4,
            scratch_shapes=[pltpu.SMEM((1,), jnp.int32)]
            + [pltpu.VMEM(((members + 1) * tile, tile), jnp.float32)] * ROWS_PER_STEP,
        ),
        out_shape=[jax.ShapeDtypeStruct((members * tile, rows * tile), jnp.bfloat16)] * 2
        + [jax.ShapeDtypeStruct((rows * taps,), jnp.int32)] * 3
        + [jax.ShapeDtypeStruct((steps,), jnp.int32)],
        compiler_params=pltpu.CompilerParams(vmem_limit_bytes=24 * 1024 * 1024),
        cost_estimate=pl.CostEstimate(
            flops=2 * tile**3 * rows * (taps + members),
            bytes_accessed=2 * (a_tiles.size + dinv.size * 6),
            transcendentals=0,
        ),
        name="own_slots",
    )(columns, agg, place, a_tiles, dinv, tent)


def product(left, right, outs, members, tile):
    width = members * tile

    def one(d2, carry):
        value = lax.dot_general(
            left[...],
            right[lane_tiles(d2, width), :],
            NT,
            preferred_element_type=jnp.float32,
        )
        for d1, out in enumerate(outs):
            for m in range(members):
                for m2 in range(members):
                    row = (d1 * members + m) * tile
                    block = value[row : row + tile, m2 * tile : (m2 + 1) * tile]
                    out[d2, m, m2] = block.astype(out.dtype)
        return carry

    lax.fori_loop(0, 5, one, 0)


def smoothed_rows(left, right, first, count, dinv, g, tile):
    lanes = lane_tiles(g, tile)
    smooth = lax.dot_general(
        right[first : first + count, lanes], dinv[g], NT, preferred_element_type=jnp.float32
    )
    left[:count, lanes] = (-smoothing * smooth).astype(jnp.bfloat16)


def neighbour_kernel(members, taps, tiles, sources, slots, ends, *refs):
    a_tiles, dinv_hbm, *tents = refs[:6]
    right_own, to_lower, to_upper, right_out = refs[6:10]
    a_held, dinv, tent, right, left, sums, sems = refs[10:]
    tile = dinv.shape[-1]
    rows = dinv.shape[0]
    chunks = rows // ROWS_PER_STEP
    outer = 4 * members
    per = ROWS_PER_STEP * taps

    def a_copy(c):
        part = pl.ds(c * per, per)
        return pltpu.make_async_copy(a_tiles.at[part], a_held.at[part], sems.at[c])

    def out_copy(c):
        lanes = lane_tiles(c, ROWS_PER_STEP * tile)
        here = right.at[pl.ds(0, outer * tile), lanes]
        return pltpu.make_async_copy(here, right_out.at[:, lanes], sems.at[chunks + c])

    others = [
        pltpu.make_async_copy(source, tent.at[pl.ds(d * rows, rows)], sems.at[2 * chunks + d])
        for d, source in enumerate(tents)
    ]
    others.append(pltpu.make_async_copy(dinv_hbm, dinv, sems.at[2 * chunks + 4]))
    own_rows = right.at[pl.ds(outer * tile, members * tile), :]
    own_copy = pltpu.make_async_copy(right_own, own_rows, sems.at[2 * chunks + 5])
    for copy in others:
        copy.start()
    for c in range(chunks):
        a_copy(c).start()
    own_copy.start()
    for copy in others:
        copy.wait()

    def one_chunk(c, first):
        sums[...] = jnp.zeros_like(sums)
        a_copy(c).wait()
        last = ends[c]

        def some(n, carry):
            found = []
            for u in range(UNROLL):
                at = first + UNROLL * n + u
                index = jnp.minimum(at, last - 1)
                number = tiles[index]
                slot = jnp.where(at < last, slots[index], outer)
                z = lax.dot_general(
                    tent[sources[index]], a_held[number], NT, preferred_element_type=jnp.float32
                )
                found.append((slot, number // taps - c * ROWS_PER_STEP, z))
            for slot, row, z in found:
                at = (lane_tiles(slot, tile), lane_tiles(row, tile))
                sums[at] += z.astype(jnp.bfloat16).astype(jnp.float32)
            return carry

        lax.fori_loop(0, (last - first + UNROLL - 1) // UNROLL, some, 0)
        lanes = lane_tiles(c, ROWS_PER_STEP * tile)
        right[: outer * tile, lanes] = sums[: outer * tile, :].astype(jnp.bfloat16)
        out_copy(c).start()
        for u in range(ROWS_PER_STEP):
            smoothed_rows(left, right, 0, 2 * members * tile, dinv, c * ROWS_PER_STEP + u, tile)
        return last

    lax.fori_loop(0, chunks, one_chunk, 0)
    own_copy.wait()
    product(left, right, (to_lower, to_upper), members, tile)
    for c in range(chunks):
        out_copy(c).wait()


def neighbour_slots(a_tiles, dinv, tents, own_right, lists, members):
    rows, taps, tile = a_tiles.shape[0], a_tiles.shape[1], a_tiles.shape[-1]
    block = (5, members, members, tile, tile)
    whole = pl.BlockSpec(block, lambda s, *_: (0,) * 5)
    anywhere = pl.BlockSpec(memory_space=pl.ANY)
    outer = 4 * members * tile
    chunks = rows // ROWS_PER_STEP
    return pl.pallas_call(
        functools.partial(neighbour_kernel, members, taps),
        grid_spec=pltpu.PrefetchScalarGridSpec(
            num_scalar_prefetch=4,
            grid=(1,),
            in_specs=[anywhere] * 7,
            out_specs=[whole, whole, anywhere],
            scratch_shapes=[
                pltpu.VMEM((rows * taps, tile, tile), jnp.bfloat16),
                pltpu.VMEM((rows, tile, tile), jnp.bfloat16),
                pltpu.VMEM((4 * rows, tile, tile), jnp.bfloat16),
                pltpu.VMEM((outer + members * tile, rows * tile), jnp.bfloat16),
                pltpu.VMEM((2 * members * tile, rows * tile), jnp.bfloat16),
                pltpu.VMEM((outer + tile, ROWS_PER_STEP * tile), jnp.float32),
                pltpu.SemaphoreType.DMA((2 * chunks + 6,)),
            ],
        ),
        out_shape=[jax.ShapeDtypeStruct(block, jnp.bfloat16)] * 2
        + [jax.ShapeDtypeStruct((outer, rows * tile), jnp.bfloat16)],
        compiler_params=pltpu.CompilerParams(vmem_limit_bytes=48 * 1024 * 1024),
        cost_estimate=pl.CostEstimate(
            flops=2 * tile**3 * rows * 2 * members * (1 + 5 * members),
            bytes_accessed=2 * (a_tiles.size + 16 * dinv.size),
            transcendentals=0,
        ),
        name="neighbour_slots",
    )(*lists, a_tiles.reshape(rows * taps, tile, tile), dinv, *tents, own_right)


def other_rows_kernel(members, dinv, right_outer, right_own, left_own, *refs):
    to_lower, to_upper, own, right, left, sems = refs
    rows, tile = dinv.shape[0], dinv.shape[-1]
    chunks = rows // ROWS_PER_STEP
    half = 2 * members * tile

    def x_copy(c):
        at = (pl.ds(half, half), lane_tiles(c, ROWS_PER_STEP * tile))
        return pltpu.make_async_copy(right_outer.at[at], right.at[at], sems.at[c])

    y_part = (pl.ds(0, half), slice(None))
    own_part = (pl.ds(2 * half, members * tile), slice(None))
    left_part = (pl.ds(half, members * tile), slice(None))
    others = [
        pltpu.make_async_copy(right_outer.at[y_part], right.at[y_part], sems.at[chunks]),
        pltpu.make_async_copy(right_own, right.at[own_part], sems.at[chunks + 1]),
        pltpu.make_async_copy(left_own, left.at[left_part], sems.at[chunks + 2]),
    ]
    for c in range(chunks):
        x_copy(c).start()
    for copy in others:
        copy.start()

    def one_chunk(c, carry):
        x_copy(c).wait()
        for u in range(ROWS_PER_STEP):
            smoothed_rows(left, right, half, half, dinv, c * ROWS_PER_STEP + u, tile)
        return carry

    lax.fori_loop(0, chunks, one_chunk, 0)
    for copy in others:
        copy.wait()
    product(left, right, (to_lower, to_upper, own), members, tile)


def other_rows(dinv, right_outer, right_own, left_own, members):
    rows, tile = dinv.shape[0], dinv.shape[-1]
    block = (5, members, members, tile, tile)
    anywhere = pl.BlockSpec(memory_space=pl.ANY)
    return pl.pallas_call(
        functools.partial(other_rows_kernel, members),
        grid=(1,),
        in_specs=[pl.BlockSpec(dinv.shape, lambda s: (0, 0, 0))] + [anywhere] * 3,
        out_specs=[pl.BlockSpec(block, lambda s: (0,) * 5)] * 3,
        out_shape=[jax.ShapeDtypeStruct(block, jnp.bfloat16)] * 2
        + [jax.ShapeDtypeStruct(block, jnp.float32)],
        scratch_shapes=[
            pltpu.VMEM((5 * members * tile, rows * tile), jnp.bfloat16),
            pltpu.VMEM((3 * members * tile, rows * tile), jnp.bfloat16),
            pltpu.SemaphoreType.DMA((rows // ROWS_PER_STEP + 3,)),
        ],
        compiler_params=pltpu.CompilerParams(vmem_limit_bytes=56 * 1024 * 1024),
        cost_estimate=pl.CostEstimate(
            flops=2 * tile**3 * rows * members * (2 + 15 * members),
            bytes_accessed=2 * 14 * members * tile * rows * tile,
            transcendentals=0,
        ),
        name="other_rows",
    )(dinv, right_outer, right_own, left_own)


def window_kernel(group, shifts, *refs):
    out = refs[-1]
    for position, offset in enumerate(group):
        total = None
        for shift, values in zip(shifts, refs):
            for d, member in enumerate(CROSS_SHIFTS):
                if (shift[0] + member[0], shift[1] + member[1]) == WINDOW_SHIFTS[offset]:
                    term = values[d].astype(jnp.float32)
                    total = term if total is None else total + term
        out[position] = total.astype(out.dtype)


def finished(group, shifts, blocks, name):
    _, members, _, tile, _ = blocks[0].shape
    spec = lambda lead: pl.BlockSpec(
        (lead, 1, members, tile, tile), lambda m: (0, m, 0, 0, 0)
    )
    shape = (len(group), members, members, tile, tile)
    return pl.pallas_call(
        functools.partial(window_kernel, group, shifts),
        grid=(members,),
        in_specs=[spec(5)] * len(blocks),
        out_specs=spec(len(group)),
        out_shape=jax.ShapeDtypeStruct(shape, jnp.bfloat16),
        compiler_params=pltpu.CompilerParams(vmem_limit_bytes=32 * 1024 * 1024),
        cost_estimate=pl.CostEstimate(
            flops=5 * blocks[0].size, bytes_accessed=8 * blocks[0].size, transcendentals=0
        ),
        name=name,
    )(*blocks)


def place_kernel(sources, row, kind, *refs):
    out = refs[-1]
    entry = pl.program_id(2)
    for source, (held, lists) in enumerate(sources):

        @pl.when(kind[entry] == source)
        def _():
            written = set()
            for array, offsets in zip(held, lists):
                for p, offset in enumerate(offsets):
                    out[0, 0, offset, 0] = refs[array][p, 0, 0]
                    written.add(offset)
            for offset in range(13):
                if offset not in written:
                    out[0, 0, offset, 0] = jnp.zeros(out.shape[4:], out.dtype)


def placed(out, arrays, sources, entries, count):
    rows, kinds = entries
    members, _, tile, _ = arrays[0].shape[1:]
    in_specs = [
        pl.BlockSpec((a.shape[0], 1, 1, tile, tile), lambda m, n, e, *_: (0, m, n, 0, 0))
        for a in arrays
    ]
    shape = (count, members, 13, members, tile, tile)
    operands = list(arrays)
    if out is not None:
        in_specs.append(pl.BlockSpec(memory_space=pl.ANY))
        operands.append(out)
    return pl.pallas_call(
        functools.partial(place_kernel, sources),
        grid_spec=pltpu.PrefetchScalarGridSpec(
            num_scalar_prefetch=2,
            grid=(members, members, len(rows)),
            in_specs=in_specs,
            out_specs=pl.BlockSpec(
                (1, 1, 13, 1, tile, tile),
                lambda m, n, e, row, kind: (row[e], m, 0, n, 0, 0),
            ),
        ),
        out_shape=jax.ShapeDtypeStruct(shape, jnp.bfloat16),
        input_output_aliases={2 + len(arrays): 0} if out is not None else {},
        compiler_params=pltpu.CompilerParams(vmem_limit_bytes=32 * 1024 * 1024),
        cost_estimate=pl.CostEstimate(
            flops=0, bytes_accessed=6 * 13 * members * members * tile * tile, transcendentals=0
        ),
        name="placed",
    )(jnp.stack(rows).astype(jnp.int32), jnp.stack(kinds).astype(jnp.int32), *operands)


def hopped(shard, lists, hop, count_y):
    limit = count_y - 1 - hop
    lower = tuple(o for o in lists[0] if -WINDOW_SHIFTS[o][1] <= limit)
    upper = tuple(o for o in lists[1] if WINDOW_SHIFTS[o][1] <= limit)
    cut = len(lists[0]) - len(lower)
    arrived = (
        shifted(shard[0][cut:], "sy", 1),
        shifted(shard[1][: len(upper)], "sy", -1),
    )
    return arrived, (lower, upper)


def end_to_end(shards, after, grid_y, count_y):
    lower = tuple(tuple(o for o in group if WINDOW_SHIFTS[o][1] >= 0) for group in GROUPS)
    upper = tuple(tuple(o for o in group if WINDOW_SHIFTS[o][1] <= 0) for group in GROUPS)
    sent = [
        lax.dynamic_slice_in_dim(
            shard, jnp.where(grid_y == 0, len(group) - len(kept), 0), len(kept), axis=0
        )
        for shard, group, kept in zip(shards, GROUPS, lower)
    ]
    sent, after = lax.optimization_barrier((jnp.concatenate(sent, axis=0), after))
    last = count_y - 1
    moved = lax.ppermute(sent, "sy", [(0, last), (last, 0)])
    return moved, after, (sum(lower, ()), sum(upper, ()))


def gathered_rows(along_y, rest_of, inputs, grid_y, count_y):
    ahead = hopped((along_y, along_y), (ALONG_Y, ALONG_Y), 1, count_y)
    inputs, moved = lax.optimization_barrier((inputs, ahead[0]))
    ahead = (moved, ahead[1])
    rest = rest_of(inputs)
    shards = [along_y, rest]
    behind = ((rest, rest), (REST, REST))
    own = ((0, 1), GROUPS)
    out = None
    arrays, sources, entries = shards, (own,), ([grid_y], [jnp.zeros_like(grid_y)])
    for hop in range(1, count_y - 1):
        now = ahead
        behind = hopped(*behind, hop, count_y)
        if hop + 2 < count_y:
            ahead = hopped(*ahead, hop + 1, count_y)
        if hop == 1:
            direct, moved, direct_lists = end_to_end(shards, ahead[0], grid_y, count_y)
            ahead = (moved, ahead[1])
        out = placed(out, arrays, sources, entries, count_y)
        moved, out = lax.optimization_barrier((behind[0], out))
        behind = (moved, behind[1])
        arrays = [chain[0][side] for side in (0, 1) for chain in (now, behind)]
        sources = tuple(
            ((2 * side, 2 * side + 1), tuple(chain[1][side] for chain in (now, behind)))
            for side in (0, 1)
        )
        has_lower, has_upper = grid_y >= hop, grid_y + hop < count_y
        lower, upper = (grid_y - hop, 0), (grid_y + hop, 1)
        spare = (lower, upper)
        if 2 * hop > count_y:
            arrays, sources = arrays + shards, sources + (((4, 5), GROUPS),)
            spare = ((grid_y, 2), (grid_y, 2))
        chosen = [
            tuple(jnp.where(has_lower, a, b) for a, b in zip(lower, spare[1])),
            tuple(jnp.where(has_upper, a, b) for a, b in zip(upper, spare[0])),
        ]
        if hop == 1:
            kind = len(sources)
            sources = sources + tuple(((len(arrays),), (held,)) for held in direct_lists)
            arrays = arrays + [direct]
            at_end = [
                jnp.where(grid_y == 0, a, jnp.where(grid_y == count_y - 1, b, c))
                for a, b, c in zip((count_y - 1, kind + 1), (0, kind), chosen[1])
            ]
            chosen.append(tuple(at_end))
        entries = ([row for row, _ in chosen], [kind for _, kind in chosen])
    return placed(out, arrays, sources, entries, count_y)


def local(a_tiles, columns, ptent, dinv, agg):
    grid_x = lax.axis_index("sx")
    grid_y = lax.axis_index("sy")
    count_y = lax.axis_size("sy")
    rows, taps, tile = a_tiles.shape[2], a_tiles.shape[3], a_tiles.shape[-1]
    coupling = a_tiles.reshape(rows, taps, tile, tile)
    inverse = dinv.reshape(rows, tile, tile)
    tent = jnp.swapaxes(ptent.reshape(rows, tile, tile), 1, 2)
    tents = (
        shifted(tent, "sy", 1),
        shifted(tent, "sy", -1),
        shifted(tent, "sx", 1),
        shifted(tent, "sx", -1),
    )
    own_right, own_left, *lists = own_slots(
        coupling,
        columns.reshape(rows * taps),
        inverse,
        tent,
        agg,
        jnp.stack([grid_x, grid_y]).astype(jnp.int32),
        count_y,
        MEMBERS,
    )
    to_lower_y, to_upper_y, outer_right = neighbour_slots(
        coupling, inverse, tents, own_right, lists, MEMBERS
    )
    from_lower_y, from_upper_y = shifted(to_upper_y, "sy", 1), shifted(to_lower_y, "sy", -1)
    to_lower_x, to_upper_x, own = other_rows(inverse, outer_right, own_right, own_left, MEMBERS)
    along_y = finished(
        ALONG_Y, ((0, -1), (0, 1), (0, 0)), (from_lower_y, from_upper_y, own), "along_y"
    )
    from_lower_x, from_upper_x = shifted(to_upper_x, "sx", 1), shifted(to_lower_x, "sx", -1)
    rest_of = functools.partial(finished, REST, CROSS_SHIFTS, name="rest")
    inputs = (from_lower_y, from_upper_y, from_lower_x, from_upper_x, own)
    return gathered_rows(along_y, rest_of, inputs, grid_y, count_y)[None]


def solution(mesh):
    return jax.shard_map(
        local,
        mesh=mesh,
        in_specs=(
            P("sx", "sy", None, None, None, None),
            P("sx", "sy", None, None),
            P("sx", "sy", None, None, None),
            P("sx", "sy", None, None, None),
            P(),
        ),
        out_specs=P("sx", None, None, None, None, None, None),
        check_vma=False,
    )
```

```python
import functools

import jax
import jax.numpy as jnp
from jax import lax
from jax.experimental import pallas as pl
from jax.experimental.pallas import tpu as pltpu
from jax.sharding import PartitionSpec as P

CROSS_SHIFTS = ((0, -1), (0, 1), (-1, 0), (1, 0), (0, 0))
OWN = 4
WINDOW_SHIFTS = (
    (-2, 0),
    (-1, -1),
    (-1, 0),
    (-1, 1),
    (0, -2),
    (0, -1),
    (0, 0),
    (0, 1),
    (0, 2),
    (1, -1),
    (1, 0),
    (1, 1),
    (2, 0),
)
TRAVEL = (4, 1, 5, 9, 0, 2, 6, 10, 12, 3, 7, 11, 8)
smoothing = 2.0 / 3.0
MEMBERS = 2
ROWS_PER_STEP = 4
UNROLL = 8
NT = (((1,), (1,)), ((), ()))


def shifted(x, axis, by):
    length = lax.axis_size(axis)
    pairs = [(i, i + by) for i in range(length) if 0 <= i + by < length]
    return lax.ppermute(x, axis, pairs)


def lane_tiles(g, tile):
    return pl.ds(pl.multiple_of(g * tile, tile), tile)


def own_kernel(count_y, rows, members, taps, columns, agg, place, a_ref, dinv_ref, tent, *refs):
    right, left, tiles, sources, slots, ends, found = refs[:7]
    sums = refs[7:]
    tile = a_ref.shape[-1]
    step = pl.program_id(0)

    @pl.when(step == 0)
    def _():
        found[0] = 0

    listed = found[0]
    for u in range(ROWS_PER_STEP):
        g = step * ROWS_PER_STEP + u
        total = sums[u]
        total[...] = jnp.zeros_like(total)
        own_member = 0
        for k in range(taps):
            target = columns[g * taps + k]
            holder = target // rows
            step_x = holder // count_y - place[0]
            step_y = holder % count_y - place[1]
            direction = jnp.where(
                step_y == -1,
                0,
                jnp.where(step_y == 1, 1, jnp.where(step_x == -1, 2, jnp.where(step_x == 1, 3, OWN))),
            )
            member = agg[target] % members
            if k == 0:
                own_member = member
            else:
                tiles[listed] = g * taps + k
                sources[listed] = direction * rows + target % rows
                slots[listed] = direction * members + member
                listed += jnp.where(direction == OWN, 0, 1)
            z = lax.dot_general(
                tent[target % rows], a_ref[u, k], NT, preferred_element_type=jnp.float32
            )
            slot = jnp.where(direction == OWN, member, members)
            total[lane_tiles(slot, tile), :] += z.astype(jnp.bfloat16).astype(jnp.float32)
        here = slice(u * tile, (u + 1) * tile)
        applied = total[: members * tile, :].astype(jnp.bfloat16)
        right[:, here] = applied
        smooth = lax.dot_general(applied, dinv_ref[u], NT, preferred_element_type=jnp.float32)
        total[: members * tile, :] = -smoothing * smooth
        total[lane_tiles(own_member, tile), :] += tent[g].astype(jnp.float32)
        left[:, here] = total[: members * tile, :].astype(jnp.bfloat16)
    found[0] = listed
    ends[step] = listed


def own_slots(a_tiles, columns, dinv, tent, agg, place, count_y, members):
    rows, taps, tile = a_tiles.shape[0], a_tiles.shape[1], a_tiles.shape[-1]
    steps = rows // ROWS_PER_STEP
    span = ROWS_PER_STEP * tile
    scalars = pl.BlockSpec(memory_space=pltpu.SMEM)
    return pl.pallas_call(
        functools.partial(own_kernel, count_y, rows, members, taps),
        grid_spec=pltpu.PrefetchScalarGridSpec(
            num_scalar_prefetch=3,
            grid=(steps,),
            in_specs=[
                pl.BlockSpec((ROWS_PER_STEP, taps, tile, tile), lambda s, *_: (s, 0, 0, 0)),
                pl.BlockSpec((ROWS_PER_STEP, tile, tile), lambda s, *_: (s, 0, 0)),
                pl.BlockSpec((rows, tile, tile), lambda s, *_: (0, 0, 0)),
            ],
            out_specs=[pl.BlockSpec((members * tile, span), lambda s, *_: (0, s))] * 2
            + [scalars] * 4,
            scratch_shapes=[pltpu.SMEM((1,), jnp.int32)]
            + [pltpu.VMEM(((members + 1) * tile, tile), jnp.float32)] * ROWS_PER_STEP,
        ),
        out_shape=[jax.ShapeDtypeStruct((members * tile, rows * tile), jnp.bfloat16)] * 2
        + [jax.ShapeDtypeStruct((rows * taps,), jnp.int32)] * 3
        + [jax.ShapeDtypeStruct((steps,), jnp.int32)],
        compiler_params=pltpu.CompilerParams(vmem_limit_bytes=24 * 1024 * 1024),
        cost_estimate=pl.CostEstimate(
            flops=2 * tile**3 * rows * (taps + members),
            bytes_accessed=2 * (a_tiles.size + dinv.size * 6),
            transcendentals=0,
        ),
        name="own_slots",
    )(columns, agg, place, a_tiles, dinv, tent)


def product(left, right, outs, members, tile):
    width = members * tile

    def one(d2, carry):
        value = lax.dot_general(
            left[...],
            right[lane_tiles(d2, width), :],
            NT,
            preferred_element_type=jnp.float32,
        )
        for d1, out in enumerate(outs):
            for m in range(members):
                for m2 in range(members):
                    row = (d1 * members + m) * tile
                    block = value[row : row + tile, m2 * tile : (m2 + 1) * tile]
                    out[d2, m, m2] = block.astype(out.dtype)
        return carry

    lax.fori_loop(0, 5, one, 0)


def smoothed_rows(left, right, first, count, dinv, g, tile):
    lanes = lane_tiles(g, tile)
    smooth = lax.dot_general(
        right[first : first + count, lanes], dinv[g], NT, preferred_element_type=jnp.float32
    )
    left[:count, lanes] = (-smoothing * smooth).astype(jnp.bfloat16)


def partial_kernel(members, taps, tiles, sources, slots, ends, *refs):
    a_tiles, dinv_hbm, *tents = refs[:6]
    right_own, left_own, *outs = refs[6:13]
    a_held, dinv, tent, right, left, sums, sems = refs[13:]
    tile = dinv.shape[-1]
    rows = dinv.shape[0]
    chunks = rows // ROWS_PER_STEP
    outer = 4 * members
    per = ROWS_PER_STEP * taps

    def a_copy(c):
        part = pl.ds(c * per, per)
        return pltpu.make_async_copy(a_tiles.at[part], a_held.at[part], sems.at[c])

    others = [
        pltpu.make_async_copy(source, tent.at[pl.ds(d * rows, rows)], sems.at[chunks + d])
        for d, source in enumerate(tents)
    ]
    others.append(pltpu.make_async_copy(dinv_hbm, dinv, sems.at[chunks + 4]))
    own_part = (pl.ds(outer * tile, members * tile), slice(None))
    own_copies = [
        pltpu.make_async_copy(right_own, right.at[own_part], sems.at[chunks + 5]),
        pltpu.make_async_copy(left_own, left.at[own_part], sems.at[chunks + 6]),
    ]
    for copy in others:
        copy.start()
    for c in range(chunks):
        a_copy(c).start()
    for copy in own_copies:
        copy.start()
    for copy in others:
        copy.wait()

    def one_chunk(c, first):
        sums[...] = jnp.zeros_like(sums)
        a_copy(c).wait()
        last = ends[c]

        def some(n, carry):
            found = []
            for u in range(UNROLL):
                at = first + UNROLL * n + u
                index = jnp.minimum(at, last - 1)
                number = tiles[index]
                slot = jnp.where(at < last, slots[index], outer)
                z = lax.dot_general(
                    tent[sources[index]], a_held[number], NT, preferred_element_type=jnp.float32
                )
                found.append((slot, number // taps - c * ROWS_PER_STEP, z))
            for slot, row, z in found:
                at = (lane_tiles(slot, tile), lane_tiles(row, tile))
                sums[at] += z.astype(jnp.bfloat16).astype(jnp.float32)
            return carry

        lax.fori_loop(0, (last - first + UNROLL - 1) // UNROLL, some, 0)
        lanes = lane_tiles(c, ROWS_PER_STEP * tile)
        right[: outer * tile, lanes] = sums[: outer * tile, :].astype(jnp.bfloat16)
        for u in range(ROWS_PER_STEP):
            g = c * ROWS_PER_STEP + u
            lanes = lane_tiles(g, tile)
            smooth = lax.dot_general(
                right[: outer * tile, lanes], dinv[g], NT, preferred_element_type=jnp.float32
            )
            left[: outer * tile, lanes] = (-smoothing * smooth).astype(jnp.bfloat16)
        return last

    lax.fori_loop(0, chunks, one_chunk, 0)
    for copy in own_copies:
        copy.wait()
    width = members * tile

    def one_direction(d2, carry):
        value = lax.dot_general(
            left[...], right[lane_tiles(d2, width), :], NT, preferred_element_type=jnp.float32
        )
        for d1, out in enumerate(outs):
            for m in range(members):
                for m2 in range(members):
                    row = (d1 * members + m) * tile
                    block = value[row : row + tile, m2 * tile : (m2 + 1) * tile]
                    out[d2, m, m2] = block.astype(out.dtype)
        return carry

    lax.fori_loop(0, 5, one_direction, 0)


def partial_blocks(a_tiles, dinv, tents, own_right, own_left, lists, members):
    rows, taps, tile = a_tiles.shape[0], a_tiles.shape[1], a_tiles.shape[-1]
    block = (5, members, members, tile, tile)
    whole = pl.BlockSpec(block, lambda s, *_: (0,) * 5)
    outer = 4 * members * tile
    slots = outer + members * tile
    return pl.pallas_call(
        functools.partial(partial_kernel, members, taps),
        grid_spec=pltpu.PrefetchScalarGridSpec(
            num_scalar_prefetch=4,
            grid=(1,),
            in_specs=[pl.BlockSpec(memory_space=pl.ANY)] * 8,
            out_specs=[whole] * 5,
            scratch_shapes=[
                pltpu.VMEM((rows * taps, tile, tile), jnp.bfloat16),
                pltpu.VMEM((rows, tile, tile), jnp.bfloat16),
                pltpu.VMEM((4 * rows, tile, tile), jnp.bfloat16),
                pltpu.VMEM((slots, rows * tile), jnp.bfloat16),
                pltpu.VMEM((slots, rows * tile), jnp.bfloat16),
                pltpu.VMEM((outer + tile, ROWS_PER_STEP * tile), jnp.float32),
                pltpu.SemaphoreType.DMA((rows // ROWS_PER_STEP + 7,)),
            ],
        ),
        out_shape=[jax.ShapeDtypeStruct(block, jnp.bfloat16)] * 4
        + [jax.ShapeDtypeStruct(block, jnp.float32)],
        compiler_params=pltpu.CompilerParams(vmem_limit_bytes=50 * 1024 * 1024),
        cost_estimate=pl.CostEstimate(
            flops=2 * tile**3 * rows * members * (4 + 25 * members),
            bytes_accessed=2 * (a_tiles.size + 20 * dinv.size),
            transcendentals=0,
        ),
        name="partial_blocks",
    )(*lists, a_tiles.reshape(rows * taps, tile, tile), dinv, *tents, own_right, own_left)


def window_kernel(*refs):
    out = refs[-1]
    for position, offset in enumerate(TRAVEL):
        total = None
        for shift, values in zip(CROSS_SHIFTS, refs):
            for d, member in enumerate(CROSS_SHIFTS):
                if (shift[0] + member[0], shift[1] + member[1]) == WINDOW_SHIFTS[offset]:
                    term = values[d].astype(jnp.float32)
                    total = term if total is None else total + term
        out[position] = total.astype(out.dtype)


def finished_window(blocks):
    _, members, _, tile, _ = blocks[0].shape
    spec = lambda lead: pl.BlockSpec(
        (lead, 1, members, tile, tile), lambda m: (0, m, 0, 0, 0)
    )
    return pl.pallas_call(
        window_kernel,
        grid=(members,),
        in_specs=[spec(5)] * 5,
        out_specs=spec(13),
        out_shape=jax.ShapeDtypeStruct((13, members, members, tile, tile), jnp.bfloat16),
        compiler_params=pltpu.CompilerParams(vmem_limit_bytes=32 * 1024 * 1024),
        cost_estimate=pl.CostEstimate(
            flops=5 * blocks[0].size, bytes_accessed=16 * blocks[0].size, transcendentals=0
        ),
        name="finished_window",
    )(*blocks)


def place_kernel(lists, members, row, kind, *refs):
    arrays, (out, nothing, sems) = refs[: len(lists)], refs[-3:]
    nothing[...] = jnp.zeros_like(nothing)

    def each(act):
        for index, (array, held) in enumerate(zip(arrays, lists)):

            @pl.when(kind[index] == 1)
            def _():
                for offset in range(13):
                    for m in range(members):
                        source = array.at[held.index(offset), m] if offset in held else nothing
                        act(
                            pltpu.make_async_copy(
                                source,
                                out.at[row[index], m, offset],
                                sems.at[(index * 13 + offset) * members + m],
                            )
                        )

    each(lambda copy: copy.start())
    each(lambda copy: copy.wait())


def placed(out, pieces, count):
    arrays = [piece[0] for piece in pieces]
    members, _, tile, _ = arrays[0].shape[1:]
    in_specs = [pl.BlockSpec(a.shape, lambda s, *_: (0,) * 5) for a in arrays]
    shape = (count, members, 13, members, tile, tile)
    operands = list(arrays)
    if out is not None:
        in_specs.append(pl.BlockSpec(memory_space=pl.ANY))
        operands.append(out)
    rows = jnp.stack([jnp.asarray(jnp.where(p[3], p[2], 0), jnp.int32) for p in pieces])
    kinds = jnp.stack([jnp.asarray(p[3], jnp.int32) for p in pieces])
    return pl.pallas_call(
        functools.partial(place_kernel, tuple(p[1] for p in pieces), members),
        grid_spec=pltpu.PrefetchScalarGridSpec(
            num_scalar_prefetch=2,
            grid=(1,),
            in_specs=in_specs,
            out_specs=pl.BlockSpec(memory_space=pl.ANY),
            scratch_shapes=[
                pltpu.VMEM((members, tile, tile), jnp.bfloat16),
                pltpu.SemaphoreType.DMA((len(pieces) * 13 * members,)),
            ],
        ),
        out_shape=jax.ShapeDtypeStruct(shape, jnp.bfloat16),
        input_output_aliases={2 + len(arrays): 0} if out is not None else {},
        compiler_params=pltpu.CompilerParams(vmem_limit_bytes=32 * 1024 * 1024),
        cost_estimate=pl.CostEstimate(
            flops=0, bytes_accessed=6 * 13 * members * members * tile * tile, transcendentals=0
        ),
        name="placed",
    )(rows, kinds, *operands)


def hopped(shard, lists, hop, count_y):
    limit = count_y - 1 - hop
    lower = tuple(o for o in lists[0] if -WINDOW_SHIFTS[o][1] <= limit)
    upper = tuple(o for o in lists[1] if WINDOW_SHIFTS[o][1] <= limit)
    cut = len(lists[0]) - len(lower)
    arrived = (
        shifted(shard[0][cut:], "sy", 1),
        shifted(shard[1][: len(upper)], "sy", -1),
    )
    return arrived, (lower, upper)


def end_to_end(shard, grid_y, count_y):
    lower = tuple(o for o in TRAVEL if WINDOW_SHIFTS[o][1] >= 0)
    upper = tuple(o for o in TRAVEL if WINDOW_SHIFTS[o][1] <= 0)
    start = jnp.where(grid_y == 0, len(TRAVEL) - len(lower), 0)
    sent = lax.dynamic_slice_in_dim(shard, start, len(lower), axis=0)
    last = count_y - 1
    moved = lax.ppermute(sent, "sy", [(0, last), (last, 0)])
    return [(moved, lower, 0, grid_y == last), (moved, upper, last, grid_y == 0)]


def gathered_rows(shard, grid_y, count_y):
    arrived, lists = (shard, shard), (TRAVEL, TRAVEL)
    pieces = [(shard, TRAVEL, grid_y, True)]
    direct = end_to_end(shard, grid_y, count_y)
    out = None
    for hop in range(1, count_y - 1):
        arrived, lists = hopped(arrived, lists, hop, count_y)
        out = placed(out, pieces, count_y)
        arrived, out = lax.optimization_barrier((arrived, out))
        pieces = [
            (arrived[0], lists[0], grid_y - hop, grid_y >= hop),
            (arrived[1], lists[1], grid_y + hop, grid_y + hop < count_y),
        ]
        if hop == 1:
            pieces += direct
    return placed(out, pieces, count_y)


def local(a_tiles, columns, ptent, dinv, agg):
    grid_x = lax.axis_index("sx")
    grid_y = lax.axis_index("sy")
    count_y = lax.axis_size("sy")
    rows, taps, tile = a_tiles.shape[2], a_tiles.shape[3], a_tiles.shape[-1]
    coupling = a_tiles.reshape(rows, taps, tile, tile)
    inverse = dinv.reshape(rows, tile, tile)
    tent = jnp.swapaxes(ptent.reshape(rows, tile, tile), 1, 2)
    tents = (
        shifted(tent, "sy", 1),
        shifted(tent, "sy", -1),
        shifted(tent, "sx", 1),
        shifted(tent, "sx", -1),
    )
    own_right, own_left, *lists = own_slots(
        coupling,
        columns.reshape(rows * taps),
        inverse,
        tent,
        agg,
        jnp.stack([grid_x, grid_y]).astype(jnp.int32),
        count_y,
        MEMBERS,
    )
    to_lower_y, to_upper_y, to_lower_x, to_upper_x, own = partial_blocks(
        coupling, inverse, tents, own_right, own_left, lists, MEMBERS
    )
    shard = finished_window(
        (
            shifted(to_upper_y, "sy", 1),
            shifted(to_lower_y, "sy", -1),
            shifted(to_upper_x, "sx", 1),
            shifted(to_lower_x, "sx", -1),
            own,
        )
    )
    return gathered_rows(shard, grid_y, count_y)[None]


def solution(mesh):
    return jax.shard_map(
        local,
        mesh=mesh,
        in_specs=(
            P("sx", "sy", None, None, None, None),
            P("sx", "sy", None, None),
            P("sx", "sy", None, None, None),
            P("sx", "sy", None, None, None),
            P(),
        ),
        out_specs=P("sx", None, None, None, None, None, None),
        check_vma=False,
    )
```

```python
import functools

import jax
import jax.numpy as jnp
from jax import lax
from jax.experimental import pallas as pl
from jax.experimental.pallas import tpu as pltpu
from jax.sharding import PartitionSpec as P

CROSS_SHIFTS = ((0, -1), (0, 1), (-1, 0), (1, 0), (0, 0))
OWN = 4
WINDOW_SHIFTS = (
    (-2, 0),
    (-1, -1),
    (-1, 0),
    (-1, 1),
    (0, -2),
    (0, -1),
    (0, 0),
    (0, 1),
    (0, 2),
    (1, -1),
    (1, 0),
    (1, 1),
    (2, 0),
)
TRAVEL = (4, 1, 5, 9, 0, 2, 6, 10, 12, 3, 7, 11, 8)
HALVES = (TRAVEL[:6], TRAVEL[6:])
smoothing = 2.0 / 3.0
MEMBERS = 2
ROWS_PER_STEP = 4
UNROLL = 8
NT = (((1,), (1,)), ((), ()))


def shifted(x, axis, by):
    length = lax.axis_size(axis)
    pairs = [(i, i + by) for i in range(length) if 0 <= i + by < length]
    return lax.ppermute(x, axis, pairs)


def lane_tiles(g, tile):
    return pl.ds(pl.multiple_of(g * tile, tile), tile)


def own_kernel(count_y, rows, members, taps, columns, agg, place, a_ref, dinv_ref, tent, *refs):
    right, left, tiles, sources, slots, ends, found = refs[:7]
    sums = refs[7:]
    tile = a_ref.shape[-1]
    step = pl.program_id(0)

    @pl.when(step == 0)
    def _():
        found[0] = 0

    listed = found[0]
    for u in range(ROWS_PER_STEP):
        g = step * ROWS_PER_STEP + u
        total = sums[u]
        total[...] = jnp.zeros_like(total)
        own_member = 0
        for k in range(taps):
            target = columns[g * taps + k]
            holder = target // rows
            step_x = holder // count_y - place[0]
            step_y = holder % count_y - place[1]
            direction = jnp.where(
                step_y == -1,
                0,
                jnp.where(step_y == 1, 1, jnp.where(step_x == -1, 2, jnp.where(step_x == 1, 3, OWN))),
            )
            member = agg[target] % members
            if k == 0:
                own_member = member
            else:
                tiles[listed] = g * taps + k
                sources[listed] = direction * rows + target % rows
                slots[listed] = direction * members + member
                listed += jnp.where(direction == OWN, 0, 1)
            z = lax.dot_general(
                tent[target % rows], a_ref[u, k], NT, preferred_element_type=jnp.float32
            )
            slot = jnp.where(direction == OWN, member, members)
            total[lane_tiles(slot, tile), :] += z.astype(jnp.bfloat16).astype(jnp.float32)
        here = slice(u * tile, (u + 1) * tile)
        applied = total[: members * tile, :].astype(jnp.bfloat16)
        right[:, here] = applied
        smooth = lax.dot_general(applied, dinv_ref[u], NT, preferred_element_type=jnp.float32)
        total[: members * tile, :] = -smoothing * smooth
        total[lane_tiles(own_member, tile), :] += tent[g].astype(jnp.float32)
        left[:, here] = total[: members * tile, :].astype(jnp.bfloat16)
    found[0] = listed
    ends[step] = listed


def own_slots(a_tiles, columns, dinv, tent, agg, place, count_y, members):
    rows, taps, tile = a_tiles.shape[0], a_tiles.shape[1], a_tiles.shape[-1]
    steps = rows // ROWS_PER_STEP
    span = ROWS_PER_STEP * tile
    scalars = pl.BlockSpec(memory_space=pltpu.SMEM)
    return pl.pallas_call(
        functools.partial(own_kernel, count_y, rows, members, taps),
        grid_spec=pltpu.PrefetchScalarGridSpec(
            num_scalar_prefetch=3,
            grid=(steps,),
            in_specs=[
                pl.BlockSpec((ROWS_PER_STEP, taps, tile, tile), lambda s, *_: (s, 0, 0, 0)),
                pl.BlockSpec((ROWS_PER_STEP, tile, tile), lambda s, *_: (s, 0, 0)),
                pl.BlockSpec((rows, tile, tile), lambda s, *_: (0, 0, 0)),
            ],
            out_specs=[pl.BlockSpec((members * tile, span), lambda s, *_: (0, s))] * 2
            + [scalars] * 4,
            scratch_shapes=[pltpu.SMEM((1,), jnp.int32)]
            + [pltpu.VMEM(((members + 1) * tile, tile), jnp.float32)] * ROWS_PER_STEP,
        ),
        out_shape=[jax.ShapeDtypeStruct((members * tile, rows * tile), jnp.bfloat16)] * 2
        + [jax.ShapeDtypeStruct((rows * taps,), jnp.int32)] * 3
        + [jax.ShapeDtypeStruct((steps,), jnp.int32)],
        compiler_params=pltpu.CompilerParams(vmem_limit_bytes=24 * 1024 * 1024),
        cost_estimate=pl.CostEstimate(
            flops=2 * tile**3 * rows * (taps + members),
            bytes_accessed=2 * (a_tiles.size + dinv.size * 6),
            transcendentals=0,
        ),
        name="own_slots",
    )(columns, agg, place, a_tiles, dinv, tent)


def product(left, right, outs, members, tile):
    width = members * tile

    def one(d2, carry):
        value = lax.dot_general(
            left[...],
            right[lane_tiles(d2, width), :],
            NT,
            preferred_element_type=jnp.float32,
        )
        for d1, out in enumerate(outs):
            for m in range(members):
                for m2 in range(members):
                    row = (d1 * members + m) * tile
                    block = value[row : row + tile, m2 * tile : (m2 + 1) * tile]
                    out[d2, m, m2] = block.astype(out.dtype)
        return carry

    lax.fori_loop(0, 5, one, 0)


def smoothed_rows(left, right, first, count, dinv, g, tile):
    lanes = lane_tiles(g, tile)
    smooth = lax.dot_general(
        right[first : first + count, lanes], dinv[g], NT, preferred_element_type=jnp.float32
    )
    left[:count, lanes] = (-smoothing * smooth).astype(jnp.bfloat16)


def partial_kernel(members, taps, tiles, sources, slots, ends, *refs):
    a_tiles, dinv_hbm, *tents = refs[:6]
    right_own, *outs, right_out = refs[6:12]
    a_held, dinv, tent, right, left, sums, sems = refs[12:]
    tile = dinv.shape[-1]
    rows = dinv.shape[0]
    chunks = rows // ROWS_PER_STEP
    outer = 4 * members
    per = ROWS_PER_STEP * taps

    def a_copy(c):
        part = pl.ds(c * per, per)
        return pltpu.make_async_copy(a_tiles.at[part], a_held.at[part], sems.at[c])

    others = [
        pltpu.make_async_copy(source, tent.at[pl.ds(d * rows, rows)], sems.at[chunks + d])
        for d, source in enumerate(tents)
    ]
    others.append(pltpu.make_async_copy(dinv_hbm, dinv, sems.at[chunks + 4]))
    own_part = (pl.ds(outer * tile, members * tile), slice(None))
    own_copy = pltpu.make_async_copy(right_own, right.at[own_part], sems.at[chunks + 5])
    out_copy = pltpu.make_async_copy(right, right_out, sems.at[chunks + 6])
    for copy in others:
        copy.start()
    for c in range(chunks):
        a_copy(c).start()
    own_copy.start()
    for copy in others:
        copy.wait()

    def one_chunk(c, first):
        sums[...] = jnp.zeros_like(sums)
        a_copy(c).wait()
        last = ends[c]

        def some(n, carry):
            found = []
            for u in range(UNROLL):
                at = first + UNROLL * n + u
                index = jnp.minimum(at, last - 1)
                number = tiles[index]
                slot = jnp.where(at < last, slots[index], outer)
                z = lax.dot_general(
                    tent[sources[index]], a_held[number], NT, preferred_element_type=jnp.float32
                )
                found.append((slot, number // taps - c * ROWS_PER_STEP, z))
            for slot, row, z in found:
                at = (lane_tiles(slot, tile), lane_tiles(row, tile))
                sums[at] += z.astype(jnp.bfloat16).astype(jnp.float32)
            return carry

        lax.fori_loop(0, (last - first + UNROLL - 1) // UNROLL, some, 0)
        lanes = lane_tiles(c, ROWS_PER_STEP * tile)
        right[: outer * tile, lanes] = sums[: outer * tile, :].astype(jnp.bfloat16)
        for u in range(ROWS_PER_STEP):
            g = c * ROWS_PER_STEP + u
            lanes = lane_tiles(g, tile)
            smooth = lax.dot_general(
                right[: outer * tile, lanes], dinv[g], NT, preferred_element_type=jnp.float32
            )
            left[: outer * tile, lanes] = (-smoothing * smooth).astype(jnp.bfloat16)
        return last

    lax.fori_loop(0, chunks, one_chunk, 0)
    own_copy.wait()
    out_copy.start()
    product(left, right, outs, members, tile)
    out_copy.wait()


def partial_blocks(a_tiles, dinv, tents, own_right, lists, members):
    rows, taps, tile = a_tiles.shape[0], a_tiles.shape[1], a_tiles.shape[-1]
    block = (5, members, members, tile, tile)
    whole = pl.BlockSpec(block, lambda s, *_: (0,) * 5)
    outer = 4 * members * tile
    slots = outer + members * tile
    return pl.pallas_call(
        functools.partial(partial_kernel, members, taps),
        grid_spec=pltpu.PrefetchScalarGridSpec(
            num_scalar_prefetch=4,
            grid=(1,),
            in_specs=[pl.BlockSpec(memory_space=pl.ANY)] * 7,
            out_specs=[whole] * 4 + [pl.BlockSpec(memory_space=pl.ANY)],
            scratch_shapes=[
                pltpu.VMEM((rows * taps, tile, tile), jnp.bfloat16),
                pltpu.VMEM((rows, tile, tile), jnp.bfloat16),
                pltpu.VMEM((4 * rows, tile, tile), jnp.bfloat16),
                pltpu.VMEM((slots, rows * tile), jnp.bfloat16),
                pltpu.VMEM((outer, rows * tile), jnp.bfloat16),
                pltpu.VMEM((outer + tile, ROWS_PER_STEP * tile), jnp.float32),
                pltpu.SemaphoreType.DMA((rows // ROWS_PER_STEP + 7,)),
            ],
        ),
        out_shape=[jax.ShapeDtypeStruct(block, jnp.bfloat16)] * 4
        + [jax.ShapeDtypeStruct((slots, rows * tile), jnp.bfloat16)],
        compiler_params=pltpu.CompilerParams(vmem_limit_bytes=48 * 1024 * 1024),
        cost_estimate=pl.CostEstimate(
            flops=2 * tile**3 * rows * members * (4 + 20 * members),
            bytes_accessed=2 * (a_tiles.size + 20 * dinv.size),
            transcendentals=0,
        ),
        name="partial_blocks",
    )(*lists, a_tiles.reshape(rows * taps, tile, tile), dinv, *tents, own_right)


def own_rows_kernel(members, left_own, right_all, own, left, right, sems):
    copies = [
        pltpu.make_async_copy(left_own, left, sems.at[0]),
        pltpu.make_async_copy(right_all, right, sems.at[1]),
    ]
    for copy in copies:
        copy.start()
    for copy in copies:
        copy.wait()
    product(left, right, (own,), members, own.shape[-1])


def own_rows(left, right, members):
    tile = left.shape[0] // members
    block = (5, members, members, tile, tile)
    return pl.pallas_call(
        functools.partial(own_rows_kernel, members),
        grid=(1,),
        in_specs=[pl.BlockSpec(memory_space=pl.ANY)] * 2,
        out_specs=pl.BlockSpec(block, lambda s: (0,) * 5),
        out_shape=jax.ShapeDtypeStruct(block, jnp.float32),
        scratch_shapes=[
            pltpu.VMEM(left.shape, left.dtype),
            pltpu.VMEM(right.shape, right.dtype),
            pltpu.SemaphoreType.DMA((2,)),
        ],
        compiler_params=pltpu.CompilerParams(vmem_limit_bytes=32 * 1024 * 1024),
        cost_estimate=pl.CostEstimate(
            flops=2 * left.size * right.shape[0],
            bytes_accessed=2 * (left.size + right.size),
            transcendentals=0,
        ),
        name="own_rows",
    )(left, right)


def window_kernel(*refs):
    for out, half in zip(refs[5:], HALVES):
        for position, offset in enumerate(half):
            total = None
            for shift, values in zip(CROSS_SHIFTS, refs):
                for d, member in enumerate(CROSS_SHIFTS):
                    if (shift[0] + member[0], shift[1] + member[1]) == WINDOW_SHIFTS[offset]:
                        term = values[d].astype(jnp.float32)
                        total = term if total is None else total + term
            out[position] = total.astype(out.dtype)


def finished_window(blocks):
    _, members, _, tile, _ = blocks[0].shape
    spec = lambda lead: pl.BlockSpec(
        (lead, 1, members, tile, tile), lambda m: (0, m, 0, 0, 0)
    )
    return pl.pallas_call(
        window_kernel,
        grid=(members,),
        in_specs=[spec(5)] * 5,
        out_specs=[spec(len(half)) for half in HALVES],
        out_shape=[
            jax.ShapeDtypeStruct((len(half), members, members, tile, tile), jnp.bfloat16)
            for half in HALVES
        ],
        compiler_params=pltpu.CompilerParams(vmem_limit_bytes=32 * 1024 * 1024),
        cost_estimate=pl.CostEstimate(
            flops=5 * blocks[0].size, bytes_accessed=16 * blocks[0].size, transcendentals=0
        ),
        name="finished_window",
    )(*blocks)


def place_kernel(lists, members, row, valid, *refs):
    arrays, (out, nothing, sems) = refs[: len(lists)], refs[-3:]
    nothing[...] = jnp.zeros_like(nothing)

    def each(act):
        for index, (array, (held, written)) in enumerate(zip(arrays, lists)):

            @pl.when(valid[index] == 1)
            def _():
                for offset in written:
                    for m in range(members):
                        source = array.at[held.index(offset), m] if offset in held else nothing
                        act(
                            pltpu.make_async_copy(
                                source,
                                out.at[row[index], m, offset],
                                sems.at[(index * 13 + offset) * members + m],
                            )
                        )

    each(lambda copy: copy.start())
    each(lambda copy: copy.wait())


def placed(out, pieces, count):
    arrays = [piece[0] for piece in pieces]
    members, _, tile, _ = arrays[0].shape[1:]
    scalars = pl.BlockSpec(memory_space=pltpu.SMEM)
    in_specs = [scalars] * 2 + [pl.BlockSpec(memory_space=pltpu.VMEM)] * len(arrays)
    operands = list(arrays)
    if out is not None:
        in_specs.append(pl.BlockSpec(memory_space=pl.ANY))
        operands.append(out)
    rows = jnp.stack([jnp.asarray(jnp.where(p[4], p[3], 0), jnp.int32) for p in pieces])
    valid = jnp.stack([jnp.asarray(p[4], jnp.int32) for p in pieces])
    return pl.pallas_call(
        functools.partial(place_kernel, tuple(p[1:3] for p in pieces), members),
        in_specs=in_specs,
        out_specs=pl.BlockSpec(memory_space=pl.ANY),
        scratch_shapes=[
            pltpu.VMEM((members, tile, tile), jnp.bfloat16),
            pltpu.SemaphoreType.DMA((len(pieces) * 13 * members,)),
        ],
        out_shape=jax.ShapeDtypeStruct(
            (count, members, 13, members, tile, tile), jnp.bfloat16
        ),
        input_output_aliases={2 + len(arrays): 0} if out is not None else {},
        compiler_params=pltpu.CompilerParams(vmem_limit_bytes=24 * 1024 * 1024),
        cost_estimate=pl.CostEstimate(
            flops=0, bytes_accessed=6 * 13 * members * members * tile * tile, transcendentals=0
        ),
        name="placed",
    )(rows, valid, *operands)


def hopped(shard, lists, hop, count_y):
    limit = count_y - 1 - hop
    lower = tuple(o for o in lists[0] if -WINDOW_SHIFTS[o][1] <= limit)
    upper = tuple(o for o in lists[1] if WINDOW_SHIFTS[o][1] <= limit)
    cut = len(lists[0]) - len(lower)
    arrived = (
        shifted(shard[0][cut:], "sy", 1),
        shifted(shard[1][: len(upper)], "sy", -1),
    )
    return arrived, (lower, upper)


def end_to_end(halves, grid_y, count_y):
    lower = tuple(o for o in TRAVEL if WINDOW_SHIFTS[o][1] >= 0)
    upper = tuple(o for o in TRAVEL if WINDOW_SHIFTS[o][1] <= 0)
    start = jnp.where(grid_y == 0, len(TRAVEL) - len(lower), 0)
    sent = lax.dynamic_slice_in_dim(jnp.concatenate(halves, axis=0), start, len(lower), axis=0)
    last = count_y - 1
    moved = lax.ppermute(sent, "sy", [(0, last), (last, 0)])
    return [
        (moved, lower, TRAVEL, 0, grid_y == last),
        (moved, upper, TRAVEL, last, grid_y == 0),
    ]


def gathered_rows(halves, grid_y, count_y):
    chains = [((half, half), (group, group)) for half, group in zip(halves, HALVES)]
    pieces = [(half, group, group, grid_y, True) for half, group in zip(halves, HALVES)]
    out = None
    for hop in range(1, count_y - 1):
        chains = [hopped(*chain, hop, count_y) for chain in chains]
        if hop == 1:
            direct = end_to_end(halves, grid_y, count_y)
        out = placed(out, pieces, count_y)
        (first, lists), second = chains
        second, out = (second[0], out) if hop > 1 else lax.optimization_barrier((second[0], out))
        chains = [(first, lists), (second, chains[1][1])]
        pieces = []
        for (arrived, lists), group in zip(chains, HALVES):
            has_lower, has_upper = grid_y >= hop, grid_y + hop < count_y
            pieces += [
                (arrived[0], lists[0], group, grid_y - hop, has_lower),
                (arrived[1], lists[1], group, grid_y + hop, has_upper),
            ]
    out = placed(out, direct + pieces[:2], count_y)
    return placed(out, pieces[2:], count_y)


def local(a_tiles, columns, ptent, dinv, agg):
    grid_x = lax.axis_index("sx")
    grid_y = lax.axis_index("sy")
    count_y = lax.axis_size("sy")
    rows, taps, tile = a_tiles.shape[2], a_tiles.shape[3], a_tiles.shape[-1]
    coupling = a_tiles.reshape(rows, taps, tile, tile)
    inverse = dinv.reshape(rows, tile, tile)
    tent = jnp.swapaxes(ptent.reshape(rows, tile, tile), 1, 2)
    tents = (
        shifted(tent, "sy", 1),
        shifted(tent, "sy", -1),
        shifted(tent, "sx", 1),
        shifted(tent, "sx", -1),
    )
    own_right, own_left, *lists = own_slots(
        coupling,
        columns.reshape(rows * taps),
        inverse,
        tent,
        agg,
        jnp.stack([grid_x, grid_y]).astype(jnp.int32),
        count_y,
        MEMBERS,
    )
    to_lower_y, to_upper_y, to_lower_x, to_upper_x, right = partial_blocks(
        coupling, inverse, tents, own_right, lists, MEMBERS
    )
    halves = finished_window(
        (
            shifted(to_upper_y, "sy", 1),
            shifted(to_lower_y, "sy", -1),
            shifted(to_upper_x, "sx", 1),
            shifted(to_lower_x, "sx", -1),
            own_rows(own_left, right, MEMBERS),
        )
    )
    return gathered_rows(halves, grid_y, count_y)[None]


def solution(mesh):
    return jax.shard_map(
        local,
        mesh=mesh,
        in_specs=(
            P("sx", "sy", None, None, None, None),
            P("sx", "sy", None, None),
            P("sx", "sy", None, None, None),
            P("sx", "sy", None, None, None),
            P(),
        ),
        out_specs=P("sx", None, None, None, None, None, None),
        check_vma=False,
    )
```

```python
import functools

import jax
import jax.numpy as jnp
from jax import lax
from jax.experimental import pallas as pl
from jax.experimental.pallas import tpu as pltpu
from jax.sharding import PartitionSpec as P

CROSS_SHIFTS = ((0, -1), (-1, 0), (0, 1), (1, 0), (0, 0))
OWN = 4
WINDOW_SHIFTS = (
    (-2, 0),
    (-1, -1),
    (-1, 0),
    (-1, 1),
    (0, -2),
    (0, -1),
    (0, 0),
    (0, 1),
    (0, 2),
    (1, -1),
    (1, 0),
    (1, 1),
    (2, 0),
)
TRAVEL = (4, 1, 5, 9, 0, 2, 6, 10, 12, 3, 7, 11, 8)
HALVES = (TRAVEL[:6], TRAVEL[6:])
smoothing = 2.0 / 3.0
MEMBERS = 2
ROWS_PER_STEP = 4
UNROLL = 8
NT = (((1,), (1,)), ((), ()))


def shifted(x, axis, by):
    length = lax.axis_size(axis)
    pairs = [(i, i + by) for i in range(length) if 0 <= i + by < length]
    return lax.ppermute(x, axis, pairs)


def lane_tiles(g, tile):
    return pl.ds(pl.multiple_of(g * tile, tile), tile)


def own_kernel(count_y, rows, members, taps, columns, agg, place, a_ref, dinv_ref, tent, *refs):
    right, left, tiles, sources, slots, ends, found = refs[:7]
    sums = refs[7:]
    tile = a_ref.shape[-1]
    step = pl.program_id(0)

    @pl.when(step == 0)
    def _():
        found[0] = 0

    listed = found[0]
    for u in range(ROWS_PER_STEP):
        g = step * ROWS_PER_STEP + u
        total = sums[u]
        total[...] = jnp.zeros_like(total)
        own_member = 0
        for k in range(taps):
            target = columns[g * taps + k]
            holder = target // rows
            step_x = holder // count_y - place[0]
            step_y = holder % count_y - place[1]
            direction = jnp.where(
                step_y == -1,
                0,
                jnp.where(step_x == -1, 1, jnp.where(step_y == 1, 2, jnp.where(step_x == 1, 3, OWN))),
            )
            member = agg[target] % members
            if k == 0:
                own_member = member
            else:
                tiles[listed] = g * taps + k
                sources[listed] = direction * rows + target % rows
                slots[listed] = direction * members + member
                listed += jnp.where(direction == OWN, 0, 1)
            z = lax.dot_general(
                tent[target % rows], a_ref[u, k], NT, preferred_element_type=jnp.float32
            )
            slot = jnp.where(direction == OWN, member, members)
            total[lane_tiles(slot, tile), :] += z.astype(jnp.bfloat16).astype(jnp.float32)
        here = slice(u * tile, (u + 1) * tile)
        applied = total[: members * tile, :].astype(jnp.bfloat16)
        right[:, here] = applied
        smooth = lax.dot_general(applied, dinv_ref[u], NT, preferred_element_type=jnp.float32)
        total[: members * tile, :] = -smoothing * smooth
        total[lane_tiles(own_member, tile), :] += tent[g].astype(jnp.float32)
        left[:, here] = total[: members * tile, :].astype(jnp.bfloat16)
    found[0] = listed
    ends[step] = listed


def own_slots(a_tiles, columns, dinv, tent, agg, place, count_y, members):
    rows, taps, tile = a_tiles.shape[0], a_tiles.shape[1], a_tiles.shape[-1]
    steps = rows // ROWS_PER_STEP
    span = ROWS_PER_STEP * tile
    scalars = pl.BlockSpec(memory_space=pltpu.SMEM)
    return pl.pallas_call(
        functools.partial(own_kernel, count_y, rows, members, taps),
        grid_spec=pltpu.PrefetchScalarGridSpec(
            num_scalar_prefetch=3,
            grid=(steps,),
            in_specs=[
                pl.BlockSpec((ROWS_PER_STEP, taps, tile, tile), lambda s, *_: (s, 0, 0, 0)),
                pl.BlockSpec((ROWS_PER_STEP, tile, tile), lambda s, *_: (s, 0, 0)),
                pl.BlockSpec((rows, tile, tile), lambda s, *_: (0, 0, 0)),
            ],
            out_specs=[pl.BlockSpec((members * tile, span), lambda s, *_: (0, s))] * 2
            + [scalars] * 4,
            scratch_shapes=[pltpu.SMEM((1,), jnp.int32)]
            + [pltpu.VMEM(((members + 1) * tile, tile), jnp.float32)] * ROWS_PER_STEP,
        ),
        out_shape=[jax.ShapeDtypeStruct((members * tile, rows * tile), jnp.bfloat16)] * 2
        + [jax.ShapeDtypeStruct((rows * taps,), jnp.int32)] * 3
        + [jax.ShapeDtypeStruct((steps,), jnp.int32)],
        compiler_params=pltpu.CompilerParams(vmem_limit_bytes=52 * 1024 * 1024),
        cost_estimate=pl.CostEstimate(
            flops=2 * tile**3 * rows * (taps + members),
            bytes_accessed=2 * (a_tiles.size + dinv.size * 6),
            transcendentals=0,
        ),
        name="own_slots",
    )(columns, agg, place, a_tiles, dinv, tent)


def product(left, right, outs, members, tile):
    width = members * tile

    def one(d2, carry):
        value = lax.dot_general(
            left[...],
            right[lane_tiles(d2, width), :],
            NT,
            preferred_element_type=jnp.float32,
        )
        for d1, out in enumerate(outs):
            for m in range(members):
                for m2 in range(members):
                    row = (d1 * members + m) * tile
                    block = value[row : row + tile, m2 * tile : (m2 + 1) * tile]
                    out[d2, m, m2] = block.astype(out.dtype)
        return carry

    lax.fori_loop(0, 5, one, 0)


def smoothed_rows(left, right, first, count, dinv, g, tile):
    lanes = lane_tiles(g, tile)
    smooth = lax.dot_general(
        right[first : first + count, lanes], dinv[g], NT, preferred_element_type=jnp.float32
    )
    left[:count, lanes] = (-smoothing * smooth).astype(jnp.bfloat16)


def partial_kernel(members, taps, tiles, sources, slots, ends, *refs):
    a_tiles, dinv_hbm, *tents = refs[:6]
    right_own, *outs, right_out = refs[6:12]
    a_held, dinv, tent, right, left, sums, sems = refs[12:]
    tile = dinv.shape[-1]
    rows = dinv.shape[0]
    chunks = rows // ROWS_PER_STEP
    outer = 4 * members
    per = ROWS_PER_STEP * taps

    def a_copy(c):
        part = pl.ds(c * per, per)
        return pltpu.make_async_copy(a_tiles.at[part], a_held.at[part], sems.at[c])

    others = [
        pltpu.make_async_copy(source, tent.at[pl.ds(d * rows, rows)], sems.at[chunks + d])
        for d, source in enumerate(tents)
    ]
    others.append(pltpu.make_async_copy(dinv_hbm, dinv, sems.at[chunks + 4]))
    own_part = (pl.ds(outer * tile, members * tile), slice(None))
    own_copy = pltpu.make_async_copy(right_own, right.at[own_part], sems.at[chunks + 5])
    out_copy = pltpu.make_async_copy(right, right_out, sems.at[chunks + 6])
    for copy in others:
        copy.start()
    for c in range(chunks):
        a_copy(c).start()
    own_copy.start()
    for copy in others:
        copy.wait()

    def one_chunk(c, first):
        sums[...] = jnp.zeros_like(sums)
        a_copy(c).wait()
        last = ends[c]

        def some(n, carry):
            found = []
            for u in range(UNROLL):
                at = first + UNROLL * n + u
                index = jnp.minimum(at, last - 1)
                number = tiles[index]
                slot = jnp.where(at < last, slots[index], outer)
                z = lax.dot_general(
                    tent[sources[index]], a_held[number], NT, preferred_element_type=jnp.float32
                )
                found.append((slot, number // taps - c * ROWS_PER_STEP, z))
            for slot, row, z in found:
                at = (lane_tiles(slot, tile), lane_tiles(row, tile))
                sums[at] += z.astype(jnp.bfloat16).astype(jnp.float32)
            return carry

        lax.fori_loop(0, (last - first + UNROLL - 1) // UNROLL, some, 0)
        lanes = lane_tiles(c, ROWS_PER_STEP * tile)
        right[: outer * tile, lanes] = sums[: outer * tile, :].astype(jnp.bfloat16)
        for u in range(ROWS_PER_STEP):
            g = c * ROWS_PER_STEP + u
            lanes = lane_tiles(g, tile)
            smooth = lax.dot_general(
                right[: outer * tile, lanes], dinv[g], NT, preferred_element_type=jnp.float32
            )
            left[: outer * tile, lanes] = (-smoothing * smooth).astype(jnp.bfloat16)
        return last

    lax.fori_loop(0, chunks, one_chunk, 0)
    own_copy.wait()
    out_copy.start()
    product(left, right, outs, members, tile)
    out_copy.wait()


def partial_blocks(a_tiles, dinv, tents, own_right, lists, members):
    rows, taps, tile = a_tiles.shape[0], a_tiles.shape[1], a_tiles.shape[-1]
    block = (5, members, members, tile, tile)
    whole = pl.BlockSpec(block, lambda s, *_: (0,) * 5)
    outer = 4 * members * tile
    slots = outer + members * tile
    return pl.pallas_call(
        functools.partial(partial_kernel, members, taps),
        grid_spec=pltpu.PrefetchScalarGridSpec(
            num_scalar_prefetch=4,
            grid=(1,),
            in_specs=[pl.BlockSpec(memory_space=pl.ANY)] * 7,
            out_specs=[whole] * 4 + [pl.BlockSpec(memory_space=pl.ANY)],
            scratch_shapes=[
                pltpu.VMEM((rows * taps, tile, tile), jnp.bfloat16),
                pltpu.VMEM((rows, tile, tile), jnp.bfloat16),
                pltpu.VMEM((4 * rows, tile, tile), jnp.bfloat16),
                pltpu.VMEM((slots, rows * tile), jnp.bfloat16),
                pltpu.VMEM((outer, rows * tile), jnp.bfloat16),
                pltpu.VMEM((outer + tile, ROWS_PER_STEP * tile), jnp.float32),
                pltpu.SemaphoreType.DMA((rows // ROWS_PER_STEP + 7,)),
            ],
        ),
        out_shape=[jax.ShapeDtypeStruct(block, jnp.bfloat16)] * 4
        + [jax.ShapeDtypeStruct((slots, rows * tile), jnp.bfloat16)],
        compiler_params=pltpu.CompilerParams(vmem_limit_bytes=48 * 1024 * 1024),
        cost_estimate=pl.CostEstimate(
            flops=2 * tile**3 * rows * members * (4 + 20 * members),
            bytes_accessed=2 * (a_tiles.size + 20 * dinv.size),
            transcendentals=0,
        ),
        name="partial_blocks",
    )(*lists, a_tiles.reshape(rows * taps, tile, tile), dinv, *tents, own_right)


def own_rows_kernel(members, left_own, right_all, own, left, right, sems):
    copies = [
        pltpu.make_async_copy(left_own, left, sems.at[0]),
        pltpu.make_async_copy(right_all, right, sems.at[1]),
    ]
    for copy in copies:
        copy.start()
    for copy in copies:
        copy.wait()
    product(left, right, (own,), members, own.shape[-1])


def own_rows(left, right, members):
    tile = left.shape[0] // members
    block = (5, members, members, tile, tile)
    return pl.pallas_call(
        functools.partial(own_rows_kernel, members),
        grid=(1,),
        in_specs=[pl.BlockSpec(memory_space=pl.ANY)] * 2,
        out_specs=pl.BlockSpec(block, lambda s: (0,) * 5),
        out_shape=jax.ShapeDtypeStruct(block, jnp.float32),
        scratch_shapes=[
            pltpu.VMEM(left.shape, left.dtype),
            pltpu.VMEM(right.shape, right.dtype),
            pltpu.SemaphoreType.DMA((2,)),
        ],
        compiler_params=pltpu.CompilerParams(vmem_limit_bytes=32 * 1024 * 1024),
        cost_estimate=pl.CostEstimate(
            flops=2 * left.size * right.shape[0],
            bytes_accessed=2 * (left.size + right.size),
            transcendentals=0,
        ),
        name="own_rows",
    )(left, right)


def window_kernel(*refs):
    for out, half in zip(refs[5:], HALVES):
        for position, offset in enumerate(half):
            total = None
            for shift, values in zip(CROSS_SHIFTS, refs):
                for d, member in enumerate(CROSS_SHIFTS):
                    if (shift[0] + member[0], shift[1] + member[1]) == WINDOW_SHIFTS[offset]:
                        term = values[d].astype(jnp.float32)
                        total = term if total is None else total + term
            out[position] = total.astype(out.dtype)


def finished_window(blocks):
    _, members, _, tile, _ = blocks[0].shape
    spec = lambda lead: pl.BlockSpec(
        (lead, 1, members, tile, tile), lambda m: (0, m, 0, 0, 0)
    )
    return pl.pallas_call(
        window_kernel,
        grid=(members,),
        in_specs=[spec(5)] * 5,
        out_specs=[spec(len(half)) for half in HALVES],
        out_shape=[
            jax.ShapeDtypeStruct((len(half), members, members, tile, tile), jnp.bfloat16)
            for half in HALVES
        ],
        compiler_params=pltpu.CompilerParams(vmem_limit_bytes=32 * 1024 * 1024),
        cost_estimate=pl.CostEstimate(
            flops=5 * blocks[0].size, bytes_accessed=16 * blocks[0].size, transcendentals=0
        ),
        name="finished_window",
    )(*blocks)


def place_kernel(lists, members, row, valid, *refs):
    arrays, (out, nothing, sems) = refs[: len(lists)], refs[-3:]
    nothing[...] = jnp.zeros_like(nothing)

    def each(act):
        for index, (array, (held, written)) in enumerate(zip(arrays, lists)):

            @pl.when(valid[index] == 1)
            def _():
                for offset in written:
                    for m in range(members):
                        source = array.at[held.index(offset), m] if offset in held else nothing
                        act(
                            pltpu.make_async_copy(
                                source,
                                out.at[row[index], m, offset],
                                sems.at[(index * 13 + offset) * members + m],
                            )
                        )

    each(lambda copy: copy.start())
    each(lambda copy: copy.wait())


def placed(out, pieces, count):
    arrays = [piece[0] for piece in pieces]
    members, _, tile, _ = arrays[0].shape[1:]
    scalars = pl.BlockSpec(memory_space=pltpu.SMEM)
    in_specs = [scalars] * 2 + [pl.BlockSpec(memory_space=pltpu.VMEM)] * len(arrays)
    operands = list(arrays)
    if out is not None:
        in_specs.append(pl.BlockSpec(memory_space=pl.ANY))
        operands.append(out)
    rows = jnp.stack([jnp.asarray(jnp.where(p[4], p[3], 0), jnp.int32) for p in pieces])
    valid = jnp.stack([jnp.asarray(p[4], jnp.int32) for p in pieces])
    return pl.pallas_call(
        functools.partial(place_kernel, tuple(p[1:3] for p in pieces), members),
        in_specs=in_specs,
        out_specs=pl.BlockSpec(memory_space=pl.ANY),
        scratch_shapes=[
            pltpu.VMEM((members, tile, tile), jnp.bfloat16),
            pltpu.SemaphoreType.DMA((len(pieces) * 13 * members,)),
        ],
        out_shape=jax.ShapeDtypeStruct(
            (count, members, 13, members, tile, tile), jnp.bfloat16
        ),
        input_output_aliases={2 + len(arrays): 0} if out is not None else {},
        compiler_params=pltpu.CompilerParams(vmem_limit_bytes=24 * 1024 * 1024),
        cost_estimate=pl.CostEstimate(
            flops=0, bytes_accessed=6 * 13 * members * members * tile * tile, transcendentals=0
        ),
        name="placed",
    )(rows, valid, *operands)


def hopped(shard, lists, hop, count_y):
    limit = count_y - 1 - hop
    lower = tuple(o for o in lists[0] if -WINDOW_SHIFTS[o][1] <= limit)
    upper = tuple(o for o in lists[1] if WINDOW_SHIFTS[o][1] <= limit)
    cut = len(lists[0]) - len(lower)
    arrived = (
        shifted(shard[0][cut:], "sy", 1),
        shifted(shard[1][: len(upper)], "sy", -1),
    )
    return arrived, (lower, upper)


def end_to_end(halves, grid_y, count_y):
    lower = tuple(o for o in TRAVEL if WINDOW_SHIFTS[o][1] >= 0)
    upper = tuple(o for o in TRAVEL if WINDOW_SHIFTS[o][1] <= 0)
    start = jnp.where(grid_y == 0, len(TRAVEL) - len(lower), 0)
    sent = lax.dynamic_slice_in_dim(jnp.concatenate(halves, axis=0), start, len(lower), axis=0)
    last = count_y - 1
    moved = lax.ppermute(sent, "sy", [(0, last), (last, 0)])
    return [
        (moved, lower, TRAVEL, 0, grid_y == last),
        (moved, upper, TRAVEL, last, grid_y == 0),
    ]


def gathered_rows(halves, grid_y, count_y):
    chains = [((half, half), (group, group)) for half, group in zip(halves, HALVES)]
    pieces = [(half, group, group, grid_y, True) for half, group in zip(halves, HALVES)]
    out = None
    for hop in range(1, count_y - 1):
        chains = [hopped(*chain, hop, count_y) for chain in chains]
        if hop == 1:
            direct = end_to_end(halves, grid_y, count_y)
        out = placed(out, pieces, count_y)
        (first, lists), second = chains
        second, out = (second[0], out) if hop > 1 else lax.optimization_barrier((second[0], out))
        chains = [(first, lists), (second, chains[1][1])]
        pieces = []
        for (arrived, lists), group in zip(chains, HALVES):
            has_lower, has_upper = grid_y >= hop, grid_y + hop < count_y
            pieces += [
                (arrived[0], lists[0], group, grid_y - hop, has_lower),
                (arrived[1], lists[1], group, grid_y + hop, has_upper),
            ]
    out = placed(out, direct + pieces[:2], count_y)
    return placed(out, pieces[2:], count_y)


def local(a_tiles, columns, ptent, dinv, agg):
    grid_x = lax.axis_index("sx")
    grid_y = lax.axis_index("sy")
    count_y = lax.axis_size("sy")
    rows, taps, tile = a_tiles.shape[2], a_tiles.shape[3], a_tiles.shape[-1]
    coupling = a_tiles.reshape(rows, taps, tile, tile)
    inverse = dinv.reshape(rows, tile, tile)
    tent = jnp.swapaxes(ptent.reshape(rows, tile, tile), 1, 2)
    tents = (
        shifted(tent, "sy", 1),
        shifted(tent, "sx", 1),
        shifted(tent, "sy", -1),
        shifted(tent, "sx", -1),
    )
    own_right, own_left, *lists = own_slots(
        coupling,
        columns.reshape(rows * taps),
        inverse,
        tent,
        agg,
        jnp.stack([grid_x, grid_y]).astype(jnp.int32),
        count_y,
        MEMBERS,
    )
    to_lower_y, to_lower_x, to_upper_y, to_upper_x, right = partial_blocks(
        coupling, inverse, tents, own_right, lists, MEMBERS
    )
    halves = finished_window(
        (
            shifted(to_upper_y, "sy", 1),
            shifted(to_upper_x, "sx", 1),
            shifted(to_lower_y, "sy", -1),
            shifted(to_lower_x, "sx", -1),
            own_rows(own_left, right, MEMBERS),
        )
    )
    return gathered_rows(halves, grid_y, count_y)[None]


def solution(mesh):
    return jax.shard_map(
        local,
        mesh=mesh,
        in_specs=(
            P("sx", "sy", None, None, None, None),
            P("sx", "sy", None, None),
            P("sx", "sy", None, None, None),
            P("sx", "sy", None, None, None),
            P(),
        ),
        out_specs=P("sx", None, None, None, None, None, None),
        check_vma=False,
    )
```

```python
import functools

import jax
import jax.numpy as jnp
from jax import lax
from jax.experimental import pallas as pl
from jax.experimental.pallas import tpu as pltpu
from jax.sharding import PartitionSpec as P

CROSS_SHIFTS = ((0, -1), (0, 1), (-1, 0), (1, 0), (0, 0))
OWN = 4
DOWN, UP = CROSS_SHIFTS[:2]
WINDOW_SHIFTS = (
    (-2, 0),
    (-1, -1),
    (-1, 0),
    (-1, 1),
    (0, -2),
    (0, -1),
    (0, 0),
    (0, 1),
    (0, 2),
    (1, -1),
    (1, 0),
    (1, 1),
    (2, 0),
)
AHEAD, BEHIND = 4, 8
TRAVEL = (4, 1, 5, 9, 0, 2, 6, 10, 12, 3, 7, 11, 8)
HALVES = (TRAVEL[:6], TRAVEL[6:])
smoothing = 2.0 / 3.0
MEMBERS = 2
ROWS_PER_STEP = 4
UNROLL = 8
NT = (((1,), (1,)), ((), ()))


def shifted(x, axis, by):
    length = lax.axis_size(axis)
    pairs = [(i, i + by) for i in range(length) if 0 <= i + by < length]
    return lax.ppermute(x, axis, pairs)


def lane_tiles(g, tile):
    return pl.ds(pl.multiple_of(g * tile, tile), tile)


def own_kernel(count_y, rows, members, taps, columns, agg, place, a_ref, dinv_ref, tent, *refs):
    right, left, tiles, sources, slots, ends, found = refs[:7]
    sums = refs[7:]
    tile = a_ref.shape[-1]
    step = pl.program_id(0)

    @pl.when(step == 0)
    def _():
        found[0] = 0

    listed = found[0]
    for u in range(ROWS_PER_STEP):
        g = step * ROWS_PER_STEP + u
        total = sums[u]
        total[...] = jnp.zeros_like(total)
        own_member = 0
        for k in range(taps):
            target = columns[g * taps + k]
            holder = target // rows
            step_x = holder // count_y - place[0]
            step_y = holder % count_y - place[1]
            direction = jnp.where(
                step_y == -1,
                0,
                jnp.where(step_y == 1, 1, jnp.where(step_x == -1, 2, jnp.where(step_x == 1, 3, OWN))),
            )
            member = agg[target] % members
            if k == 0:
                own_member = member
            else:
                tiles[listed] = g * taps + k
                sources[listed] = direction * rows + target % rows
                slots[listed] = direction * members + member
                listed += jnp.where(direction == OWN, 0, 1)
            z = lax.dot_general(
                tent[target % rows], a_ref[u, k], NT, preferred_element_type=jnp.float32
            )
            slot = jnp.where(direction == OWN, member, members)
            total[lane_tiles(slot, tile), :] += z.astype(jnp.bfloat16).astype(jnp.float32)
        here = slice(u * tile, (u + 1) * tile)
        applied = total[: members * tile, :].astype(jnp.bfloat16)
        right[:, here] = applied
        smooth = lax.dot_general(applied, dinv_ref[u], NT, preferred_element_type=jnp.float32)
        total[: members * tile, :] = -smoothing * smooth
        total[lane_tiles(own_member, tile), :] += tent[g].astype(jnp.float32)
        left[:, here] = total[: members * tile, :].astype(jnp.bfloat16)
    found[0] = listed
    ends[step] = listed


def own_slots(a_tiles, columns, dinv, tent, agg, place, count_y, members):
    rows, taps, tile = a_tiles.shape[0], a_tiles.shape[1], a_tiles.shape[-1]
    steps = rows // ROWS_PER_STEP
    span = ROWS_PER_STEP * tile
    scalars = pl.BlockSpec(memory_space=pltpu.SMEM)
    return pl.pallas_call(
        functools.partial(own_kernel, count_y, rows, members, taps),
        grid_spec=pltpu.PrefetchScalarGridSpec(
            num_scalar_prefetch=3,
            grid=(steps,),
            in_specs=[
                pl.BlockSpec((ROWS_PER_STEP, taps, tile, tile), lambda s, *_: (s, 0, 0, 0)),
                pl.BlockSpec((ROWS_PER_STEP, tile, tile), lambda s, *_: (s, 0, 0)),
                pl.BlockSpec((rows, tile, tile), lambda s, *_: (0, 0, 0)),
            ],
            out_specs=[pl.BlockSpec((members * tile, span), lambda s, *_: (0, s))] * 2
            + [scalars] * 4,
            scratch_shapes=[pltpu.SMEM((1,), jnp.int32)]
            + [pltpu.VMEM(((members + 1) * tile, tile), jnp.float32)] * ROWS_PER_STEP,
        ),
        out_shape=[jax.ShapeDtypeStruct((members * tile, rows * tile), jnp.bfloat16)] * 2
        + [jax.ShapeDtypeStruct((rows * taps,), jnp.int32)] * 3
        + [jax.ShapeDtypeStruct((steps,), jnp.int32)],
        compiler_params=pltpu.CompilerParams(vmem_limit_bytes=44 * 1024 * 1024),
        cost_estimate=pl.CostEstimate(
            flops=2 * tile**3 * rows * (taps + members),
            bytes_accessed=2 * (a_tiles.size + dinv.size * 6),
            transcendentals=0,
        ),
        name="own_slots",
    )(columns, agg, place, a_tiles, dinv, tent)


def kept_members(shift):
    lone = CROSS_SHIFTS.index(shift)
    return tuple((lone + 1 + p) % 5 for p in range(4))


def product(left, right, outs, lone, members, tile):
    width = members * tile

    def one(d2, carry):
        value = lax.dot_general(
            left[...],
            right[lane_tiles(d2, width), :],
            NT,
            preferred_element_type=jnp.float32,
        )

        def write(out, at, d1):
            for m in range(members):
                for m2 in range(members):
                    row = (d1 * members + m) * tile
                    block = value[row : row + tile, m2 * tile : (m2 + 1) * tile]
                    out[at, m, m2] = block.astype(out.dtype)

        for d1, out in enumerate(outs):
            if d1 not in lone:
                write(out, d2, d1)
                continue
            direction, single = lone[d1]

            @pl.when(d2 == direction)
            def _():
                write(single, 0, d1)

            @pl.when(d2 != direction)
            def _():
                write(out, (d2 + 4 - direction) % 5, d1)

        return carry

    lax.fori_loop(0, 5, one, 0)


def smoothed_rows(left, right, first, count, dinv, g, tile):
    lanes = lane_tiles(g, tile)
    smooth = lax.dot_general(
        right[first : first + count, lanes], dinv[g], NT, preferred_element_type=jnp.float32
    )
    left[:count, lanes] = (-smoothing * smooth).astype(jnp.bfloat16)


def partial_kernel(members, taps, tiles, sources, slots, ends, *refs):
    a_tiles, dinv_hbm, *tents = refs[:6]
    right_own, *outs, behind, ahead, right_out = refs[6:14]
    a_held, dinv, tent, right, left, sums, sems = refs[14:]
    tile = dinv.shape[-1]
    rows = dinv.shape[0]
    chunks = rows // ROWS_PER_STEP
    outer = 4 * members
    per = ROWS_PER_STEP * taps

    def a_copy(c):
        part = pl.ds(c * per, per)
        return pltpu.make_async_copy(a_tiles.at[part], a_held.at[part], sems.at[c])

    others = [
        pltpu.make_async_copy(source, tent.at[pl.ds(d * rows, rows)], sems.at[chunks + d])
        for d, source in enumerate(tents)
    ]
    others.append(pltpu.make_async_copy(dinv_hbm, dinv, sems.at[chunks + 4]))
    own_part = (pl.ds(outer * tile, members * tile), slice(None))
    own_copy = pltpu.make_async_copy(right_own, right.at[own_part], sems.at[chunks + 5])
    out_copy = pltpu.make_async_copy(right, right_out, sems.at[chunks + 6])
    for copy in others:
        copy.start()
    for c in range(chunks):
        a_copy(c).start()
    own_copy.start()
    sums[...] = jnp.zeros_like(sums)
    for copy in others:
        copy.wait()

    def one_chunk(c, first):
        a_copy(c).wait()
        last = ends[c]

        def some(n, carry):
            found = []
            for u in range(UNROLL):
                at = first + UNROLL * n + u
                index = jnp.minimum(at, last - 1)
                number = tiles[index]
                slot = jnp.where(at < last, slots[index], outer)
                z = lax.dot_general(
                    tent[sources[index]], a_held[number], NT, preferred_element_type=jnp.float32
                )
                found.append((slot, number // taps - c * ROWS_PER_STEP, z))
            for slot, row, z in found:
                at = (lane_tiles(slot, tile), lane_tiles(row, tile))
                sums[at] += z.astype(jnp.bfloat16).astype(jnp.float32)
            return carry

        lax.fori_loop(0, (last - first + UNROLL - 1) // UNROLL, some, 0)
        lanes = lane_tiles(c, ROWS_PER_STEP * tile)
        right[: outer * tile, lanes] = sums[: outer * tile, :].astype(jnp.bfloat16)
        sums[...] = jnp.zeros_like(sums)
        for u in range(ROWS_PER_STEP):
            g = c * ROWS_PER_STEP + u
            lanes = lane_tiles(g, tile)
            smooth = lax.dot_general(
                right[: outer * tile, lanes], dinv[g], NT, preferred_element_type=jnp.float32
            )
            left[: outer * tile, lanes] = (-smoothing * smooth).astype(jnp.bfloat16)
        return last

    lax.fori_loop(0, chunks, one_chunk, 0)
    own_copy.wait()
    out_copy.start()
    lone = {d: (CROSS_SHIFTS.index(t), out) for d, t, out in ((0, UP, behind), (1, DOWN, ahead))}
    product(left, right, outs, lone, members, tile)
    out_copy.wait()


def partial_blocks(a_tiles, dinv, tents, own_right, lists, members):
    rows, taps, tile = a_tiles.shape[0], a_tiles.shape[1], a_tiles.shape[-1]
    whole = lambda lead: pl.BlockSpec((lead, members, members, tile, tile), lambda s, *_: (0,) * 5)
    leads = (4, 4, 5, 5, 1, 1)
    outer = 4 * members * tile
    slots = outer + members * tile
    return pl.pallas_call(
        functools.partial(partial_kernel, members, taps),
        grid_spec=pltpu.PrefetchScalarGridSpec(
            num_scalar_prefetch=4,
            grid=(1,),
            in_specs=[pl.BlockSpec(memory_space=pl.ANY)] * 7,
            out_specs=[whole(lead) for lead in leads] + [pl.BlockSpec(memory_space=pl.ANY)],
            scratch_shapes=[
                pltpu.VMEM((rows * taps, tile, tile), jnp.bfloat16),
                pltpu.VMEM((rows, tile, tile), jnp.bfloat16),
                pltpu.VMEM((4 * rows, tile, tile), jnp.bfloat16),
                pltpu.VMEM((slots, rows * tile), jnp.bfloat16),
                pltpu.VMEM((outer, rows * tile), jnp.bfloat16),
                pltpu.VMEM((outer + tile, ROWS_PER_STEP * tile), jnp.float32),
                pltpu.SemaphoreType.DMA((rows // ROWS_PER_STEP + 7,)),
            ],
        ),
        out_shape=[
            jax.ShapeDtypeStruct((lead, members, members, tile, tile), jnp.bfloat16)
            for lead in leads
        ]
        + [jax.ShapeDtypeStruct((slots, rows * tile), jnp.bfloat16)],
        compiler_params=pltpu.CompilerParams(vmem_limit_bytes=48 * 1024 * 1024),
        cost_estimate=pl.CostEstimate(
            flops=2 * tile**3 * rows * members * (4 + 20 * members),
            bytes_accessed=2 * (a_tiles.size + 20 * dinv.size),
            transcendentals=0,
        ),
        name="partial_blocks",
    )(*lists, a_tiles.reshape(rows * taps, tile, tile), dinv, *tents, own_right)


def own_rows_kernel(members, left_own, right_all, own, left, right, sems):
    copies = [
        pltpu.make_async_copy(left_own, left, sems.at[0]),
        pltpu.make_async_copy(right_all, right, sems.at[1]),
    ]
    for copy in copies:
        copy.start()
    for copy in copies:
        copy.wait()
    product(left, right, (own,), {}, members, own.shape[-1])


def own_rows(left, right, members):
    tile = left.shape[0] // members
    block = (5, members, members, tile, tile)
    return pl.pallas_call(
        functools.partial(own_rows_kernel, members),
        grid=(1,),
        in_specs=[pl.BlockSpec(memory_space=pl.ANY)] * 2,
        out_specs=pl.BlockSpec(block, lambda s: (0,) * 5),
        out_shape=jax.ShapeDtypeStruct(block, jnp.float32),
        scratch_shapes=[
            pltpu.VMEM(left.shape, left.dtype),
            pltpu.VMEM(right.shape, right.dtype),
            pltpu.SemaphoreType.DMA((2,)),
        ],
        compiler_params=pltpu.CompilerParams(vmem_limit_bytes=32 * 1024 * 1024),
        cost_estimate=pl.CostEstimate(
            flops=2 * left.size * right.shape[0],
            bytes_accessed=2 * (left.size + right.size),
            transcendentals=0,
        ),
        name="own_rows",
    )(left, right)


def window_kernel(*refs):
    every = tuple(range(5))
    held = (kept_members(DOWN), kept_members(UP), every, every, every)
    behind, ahead = refs[5:7]
    for out, half in zip(refs[7:], HALVES):
        for position, offset in enumerate(half):
            if offset in (AHEAD, BEHIND):
                out[position] = (ahead if offset == AHEAD else behind)[0]
                continue
            total = None
            for shift, values, directions in zip(CROSS_SHIFTS, refs, held):
                for d, direction in enumerate(directions):
                    member = CROSS_SHIFTS[direction]
                    if (shift[0] + member[0], shift[1] + member[1]) == WINDOW_SHIFTS[offset]:
                        term = values[d].astype(jnp.float32)
                        total = term if total is None else total + term
            out[position] = total.astype(out.dtype)


def finished_window(blocks):
    _, members, _, tile, _ = blocks[0].shape
    spec = lambda lead: pl.BlockSpec(
        (lead, 1, members, tile, tile), lambda m: (0, m, 0, 0, 0)
    )
    return pl.pallas_call(
        window_kernel,
        grid=(members,),
        in_specs=[spec(block.shape[0]) for block in blocks],
        out_specs=[spec(len(half)) for half in HALVES],
        out_shape=[
            jax.ShapeDtypeStruct((len(half), members, members, tile, tile), jnp.bfloat16)
            for half in HALVES
        ],
        compiler_params=pltpu.CompilerParams(vmem_limit_bytes=32 * 1024 * 1024),
        cost_estimate=pl.CostEstimate(
            flops=5 * blocks[4].size, bytes_accessed=16 * blocks[4].size, transcendentals=0
        ),
        name="finished_window",
    )(*blocks)


def place_kernel(lists, edges, row, valid, *refs):
    arrays, (out, nothing, sems) = refs[: len(lists)], refs[-3:]
    count = out.shape[0]
    nothing[...] = jnp.zeros_like(nothing)

    def each(act):
        def move(source, target, offset, sem):
            act(pltpu.make_async_copy(source, out.at[target, :, offset], sems.at[sem]))

        for index, (array, (held, written)) in enumerate(zip(arrays, lists)):

            def write(offset, target):
                source = array.at[held.index(offset)] if offset in held else nothing
                move(source, target, offset, index * 13 + offset)

            here = row[index]

            @pl.when(valid[index] == 1)
            def _():
                for offset in written:
                    if offset not in (AHEAD, BEHIND):
                        write(offset, here)

            if AHEAD in written:

                @pl.when((valid[index] == 1) & (here + 1 < count))
                def _():
                    write(AHEAD, here + 1)

            if BEHIND in written:

                @pl.when((valid[index] == 1) & (here > 0))
                def _():
                    write(BEHIND, here - 1)

        if edges:
            move(nothing, 0, AHEAD, 13 * len(lists))
            move(nothing, count - 1, BEHIND, 13 * len(lists) + 1)

    each(lambda copy: copy.start())
    each(lambda copy: copy.wait())


def placed(out, pieces, count):
    arrays = [piece[0] for piece in pieces]
    members, _, tile, _ = arrays[0].shape[1:]
    scalars = pl.BlockSpec(memory_space=pltpu.SMEM)
    in_specs = [scalars] * 2 + [pl.BlockSpec(memory_space=pltpu.VMEM)] * len(arrays)
    operands = list(arrays)
    if out is not None:
        in_specs.append(pl.BlockSpec(memory_space=pl.ANY))
        operands.append(out)
    rows = jnp.stack([jnp.asarray(jnp.where(p[4], p[3], 0), jnp.int32) for p in pieces])
    valid = jnp.stack([jnp.asarray(p[4], jnp.int32) for p in pieces])
    return pl.pallas_call(
        functools.partial(place_kernel, tuple(p[1:3] for p in pieces), out is None),
        in_specs=in_specs,
        out_specs=pl.BlockSpec(memory_space=pl.ANY),
        scratch_shapes=[
            pltpu.VMEM((members, members, tile, tile), jnp.bfloat16),
            pltpu.SemaphoreType.DMA((len(pieces) * 13 + 2,)),
        ],
        out_shape=jax.ShapeDtypeStruct(
            (count, members, 13, members, tile, tile), jnp.bfloat16
        ),
        input_output_aliases={2 + len(arrays): 0} if out is not None else {},
        compiler_params=pltpu.CompilerParams(vmem_limit_bytes=24 * 1024 * 1024),
        cost_estimate=pl.CostEstimate(
            flops=0, bytes_accessed=6 * 13 * members * members * tile * tile, transcendentals=0
        ),
        name="placed",
    )(rows, valid, *operands)


def end_to_end(halves, grid_y, count_y):
    lower = tuple(o for o in TRAVEL if WINDOW_SHIFTS[o][1] in (0, 1))
    upper = tuple(o for o in TRAVEL if WINDOW_SHIFTS[o][1] in (-1, 0))
    start = jnp.where(grid_y == 0, TRAVEL.index(lower[0]), TRAVEL.index(upper[0]))
    sent = lax.dynamic_slice_in_dim(jnp.concatenate(halves, axis=0), start, len(lower), axis=0)
    last = count_y - 1
    moved = lax.ppermute(sent, "sy", [(0, last), (last, 0)])
    return [
        (moved, lower, TRAVEL, 0, grid_y == last),
        (moved, upper, TRAVEL, last, grid_y == 0),
    ]


def gathered_rows(halves, grid_y, count_y):
    chains = [(half, half) for half in halves]
    pieces = [(half, group, group, grid_y, True) for half, group in zip(halves, HALVES)]
    out = None
    for hop in range(1, count_y - 1):
        chains = [(shifted(a, "sy", 1), shifted(b, "sy", -1)) for a, b in chains]
        if hop == 1:
            direct = end_to_end(halves, grid_y, count_y)
        out = placed(out, pieces, count_y)
        if hop == 1:
            chains[1], out = lax.optimization_barrier((chains[1], out))
        pieces = []
        for (from_lower, from_upper), group in zip(chains, HALVES):
            pieces += [
                (from_lower, group, group, grid_y - hop, grid_y >= hop),
                (from_upper, group, group, grid_y + hop, grid_y + hop < count_y),
            ]
    out = placed(out, direct + pieces[:2], count_y)
    return placed(out, pieces[2:], count_y)


def local(a_tiles, columns, ptent, dinv, agg):
    grid_x = lax.axis_index("sx")
    grid_y = lax.axis_index("sy")
    count_y = lax.axis_size("sy")
    rows, taps, tile = a_tiles.shape[2], a_tiles.shape[3], a_tiles.shape[-1]
    coupling = a_tiles.reshape(rows, taps, tile, tile)
    inverse = dinv.reshape(rows, tile, tile)
    tent = jnp.swapaxes(ptent.reshape(rows, tile, tile), 1, 2)
    tents = (
        shifted(tent, "sy", 1),
        shifted(tent, "sy", -1),
        shifted(tent, "sx", 1),
        shifted(tent, "sx", -1),
    )
    own_right, own_left, *lists = own_slots(
        coupling,
        columns.reshape(rows * taps),
        inverse,
        tent,
        agg,
        jnp.stack([grid_x, grid_y]).astype(jnp.int32),
        count_y,
        MEMBERS,
    )
    to_lower_y, to_upper_y, to_lower_x, to_upper_x, behind, ahead, right = partial_blocks(
        coupling, inverse, tents, own_right, lists, MEMBERS
    )
    halves = finished_window(
        (
            shifted(to_upper_y, "sy", 1),
            shifted(to_lower_y, "sy", -1),
            shifted(to_upper_x, "sx", 1),
            shifted(to_lower_x, "sx", -1),
            own_rows(own_left, right, MEMBERS),
            behind,
            ahead,
        )
    )
    return gathered_rows(halves, grid_y, count_y)[None]


def solution(mesh):
    return jax.shard_map(
        local,
        mesh=mesh,
        in_specs=(
            P("sx", "sy", None, None, None, None),
            P("sx", "sy", None, None),
            P("sx", "sy", None, None, None),
            P("sx", "sy", None, None, None),
            P(),
        ),
        out_specs=P("sx", None, None, None, None, None, None),
        check_vma=False,
    )
```

```python
import functools

import jax
import jax.numpy as jnp
from jax import lax
from jax.experimental import pallas as pl
from jax.experimental.pallas import tpu as pltpu
from jax.sharding import PartitionSpec as P

CROSS_SHIFTS = ((0, -1), (0, 1), (-1, 0), (1, 0), (0, 0))
OWN = 4
DOWN, UP = CROSS_SHIFTS[:2]
WINDOW_SHIFTS = (
    (-2, 0),
    (-1, -1),
    (-1, 0),
    (-1, 1),
    (0, -2),
    (0, -1),
    (0, 0),
    (0, 1),
    (0, 2),
    (1, -1),
    (1, 0),
    (1, 1),
    (2, 0),
)
AHEAD, BEHIND = 4, 8
TRAVEL = (4, 1, 5, 9, 0, 2, 6, 10, 12, 3, 7, 11, 8)
HALVES = (TRAVEL[:6], TRAVEL[6:])
smoothing = 2.0 / 3.0
MEMBERS = 2
ROWS_PER_STEP = 4
ROWS_PER_CHUNK = 8
UNROLL = 8
NT = (((1,), (1,)), ((), ()))


def shifted(x, axis, by):
    length = lax.axis_size(axis)
    pairs = [(i, i + by) for i in range(length) if 0 <= i + by < length]
    return lax.ppermute(x, axis, pairs)


def lane_tiles(g, tile):
    return pl.ds(pl.multiple_of(g * tile, tile), tile)


def own_kernel(count_y, rows, members, taps, columns, agg, place, a_ref, dinv_ref, tent, *refs):
    right, left, tiles, sources, slots, ends, found = refs[:7]
    sums = refs[7:]
    tile = a_ref.shape[-1]
    step = pl.program_id(0)

    @pl.when(step == 0)
    def _():
        found[0] = 0

    listed = found[0]
    for u in range(ROWS_PER_STEP):
        g = step * ROWS_PER_STEP + u
        total = sums[u]
        total[...] = jnp.zeros_like(total)
        own_member = 0
        for k in range(taps):
            target = columns[g * taps + k]
            holder = target // rows
            step_x = holder // count_y - place[0]
            step_y = holder % count_y - place[1]
            direction = jnp.where(
                step_y == -1,
                0,
                jnp.where(step_y == 1, 1, jnp.where(step_x == -1, 2, jnp.where(step_x == 1, 3, OWN))),
            )
            member = agg[target] % members
            if k == 0:
                own_member = member
            else:
                tiles[listed] = g * taps + k
                sources[listed] = direction * rows + target % rows
                slots[listed] = direction * members + member
                listed += jnp.where(direction == OWN, 0, 1)
            z = lax.dot_general(
                tent[target % rows], a_ref[u, k], NT, preferred_element_type=jnp.float32
            )
            slot = jnp.where(direction == OWN, member, members)
            total[lane_tiles(slot, tile), :] += z.astype(jnp.bfloat16).astype(jnp.float32)
        here = slice(u * tile, (u + 1) * tile)
        applied = total[: members * tile, :].astype(jnp.bfloat16)
        right[:, here] = applied
        smooth = lax.dot_general(applied, dinv_ref[u], NT, preferred_element_type=jnp.float32)
        total[: members * tile, :] = -smoothing * smooth
        total[lane_tiles(own_member, tile), :] += tent[g].astype(jnp.float32)
        left[:, here] = total[: members * tile, :].astype(jnp.bfloat16)
    found[0] = listed
    ends[step] = listed


def own_slots(a_tiles, columns, dinv, tent, agg, place, count_y, members):
    rows, taps, tile = a_tiles.shape[0], a_tiles.shape[1], a_tiles.shape[-1]
    steps = rows // ROWS_PER_STEP
    span = ROWS_PER_STEP * tile
    scalars = pl.BlockSpec(memory_space=pltpu.SMEM)
    return pl.pallas_call(
        functools.partial(own_kernel, count_y, rows, members, taps),
        grid_spec=pltpu.PrefetchScalarGridSpec(
            num_scalar_prefetch=3,
            grid=(steps,),
            in_specs=[
                pl.BlockSpec((ROWS_PER_STEP, taps, tile, tile), lambda s, *_: (s, 0, 0, 0)),
                pl.BlockSpec((ROWS_PER_STEP, tile, tile), lambda s, *_: (s, 0, 0)),
                pl.BlockSpec((rows, tile, tile), lambda s, *_: (0, 0, 0)),
            ],
            out_specs=[pl.BlockSpec((members * tile, span), lambda s, *_: (0, s))] * 2
            + [scalars] * 4,
            scratch_shapes=[pltpu.SMEM((1,), jnp.int32)]
            + [pltpu.VMEM(((members + 1) * tile, tile), jnp.float32)] * ROWS_PER_STEP,
        ),
        out_shape=[jax.ShapeDtypeStruct((members * tile, rows * tile), jnp.bfloat16)] * 2
        + [jax.ShapeDtypeStruct((rows * taps,), jnp.int32)] * 3
        + [jax.ShapeDtypeStruct((steps,), jnp.int32)],
        compiler_params=pltpu.CompilerParams(vmem_limit_bytes=44 * 1024 * 1024),
        cost_estimate=pl.CostEstimate(
            flops=2 * tile**3 * rows * (taps + members),
            bytes_accessed=2 * (a_tiles.size + dinv.size * 6),
            transcendentals=0,
        ),
        name="own_slots",
    )(columns, agg, place, a_tiles, dinv, tent)


def kept_members(shift):
    lone = CROSS_SHIFTS.index(shift)
    return tuple((lone + 1 + p) % 5 for p in range(4))


def product(left, right, outs, lone, members, tile):
    width = members * tile

    def one(d2, carry):
        value = lax.dot_general(
            left[...],
            right[lane_tiles(d2, width), :],
            NT,
            preferred_element_type=jnp.float32,
        )

        def write(out, at, d1):
            for m in range(members):
                for m2 in range(members):
                    row = (d1 * members + m) * tile
                    block = value[row : row + tile, m2 * tile : (m2 + 1) * tile]
                    out[at, m, m2] = block.astype(out.dtype)

        for d1, out in enumerate(outs):
            if d1 not in lone:
                write(out, d2, d1)
                continue
            direction, single = lone[d1]

            @pl.when(d2 == direction)
            def _():
                write(single, 0, d1)

            @pl.when(d2 != direction)
            def _():
                write(out, (d2 + 4 - direction) % 5, d1)

        return carry

    lax.fori_loop(0, 5, one, 0)


def smoothed_rows(left, right, first, count, dinv, g, tile):
    lanes = lane_tiles(g, tile)
    smooth = lax.dot_general(
        right[first : first + count, lanes], dinv[g], NT, preferred_element_type=jnp.float32
    )
    left[:count, lanes] = (-smoothing * smooth).astype(jnp.bfloat16)


def partial_kernel(members, taps, tiles, sources, slots, ends, *refs):
    a_tiles, dinv_hbm, *tents = refs[:6]
    right_own, *outs, behind, ahead, right_out = refs[6:14]
    a_held, dinv, tent, right, left, sums, sems = refs[14:]
    tile = dinv.shape[-1]
    rows = dinv.shape[0]
    chunks = rows // ROWS_PER_CHUNK
    outer = 4 * members
    per = ROWS_PER_CHUNK * taps

    def a_copy(c):
        part = pl.ds(c * per, per)
        return pltpu.make_async_copy(a_tiles.at[part], a_held.at[part], sems.at[c])

    tent_copies = [
        pltpu.make_async_copy(source, tent.at[pl.ds(d * rows, rows)], sems.at[chunks + d])
        for d, source in enumerate(tents)
    ]
    dinv_copy = pltpu.make_async_copy(dinv_hbm, dinv, sems.at[chunks + 4])
    own_part = (pl.ds(outer * tile, members * tile), slice(None))
    own_copy = pltpu.make_async_copy(right_own, right.at[own_part], sems.at[chunks + 5])
    out_copy = pltpu.make_async_copy(right, right_out, sems.at[chunks + 6])
    for copy in tent_copies:
        copy.start()
    a_copy(0).start()
    sums[...] = jnp.zeros_like(sums)
    for copy in tent_copies:
        copy.wait()
    dinv_copy.start()
    for c in range(1, chunks):
        a_copy(c).start()
    own_copy.start()

    def one_chunk(c, first):
        a_copy(c).wait()
        last = ends[(c + 1) * (ROWS_PER_CHUNK // ROWS_PER_STEP) - 1]

        def some(n, carry):
            found = []
            for u in range(UNROLL):
                at = first + UNROLL * n + u
                index = jnp.minimum(at, last - 1)
                number = tiles[index]
                slot = jnp.where(at < last, slots[index], outer)
                z = lax.dot_general(
                    tent[sources[index]], a_held[number], NT, preferred_element_type=jnp.float32
                )
                found.append((slot, number // taps - c * ROWS_PER_CHUNK, z))
            for slot, row, z in found:
                at = (lane_tiles(slot, tile), lane_tiles(row, tile))
                sums[at] += z.astype(jnp.bfloat16).astype(jnp.float32)
            return carry

        lax.fori_loop(0, (last - first + UNROLL - 1) // UNROLL, some, 0)
        lanes = lane_tiles(c, ROWS_PER_CHUNK * tile)
        right[: outer * tile, lanes] = sums[: outer * tile, :].astype(jnp.bfloat16)
        sums[...] = jnp.zeros_like(sums)

        @pl.when(c == 0)
        def _():
            dinv_copy.wait()

        for u in range(ROWS_PER_CHUNK):
            g = c * ROWS_PER_CHUNK + u
            lanes = lane_tiles(g, tile)
            smooth = lax.dot_general(
                right[: outer * tile, lanes], dinv[g], NT, preferred_element_type=jnp.float32
            )
            left[: outer * tile, lanes] = (-smoothing * smooth).astype(jnp.bfloat16)
        return last

    lax.fori_loop(0, chunks, one_chunk, 0)
    own_copy.wait()
    out_copy.start()
    lone = {d: (CROSS_SHIFTS.index(t), out) for d, t, out in ((0, UP, behind), (1, DOWN, ahead))}
    product(left, right, outs, lone, members, tile)
    out_copy.wait()


def partial_blocks(a_tiles, dinv, tents, own_right, lists, members):
    rows, taps, tile = a_tiles.shape[0], a_tiles.shape[1], a_tiles.shape[-1]
    whole = lambda lead: pl.BlockSpec((lead, members, members, tile, tile), lambda s, *_: (0,) * 5)
    leads = (4, 4, 5, 5, 1, 1)
    outer = 4 * members * tile
    slots = outer + members * tile
    return pl.pallas_call(
        functools.partial(partial_kernel, members, taps),
        grid_spec=pltpu.PrefetchScalarGridSpec(
            num_scalar_prefetch=4,
            grid=(1,),
            in_specs=[pl.BlockSpec(memory_space=pl.ANY)] * 7,
            out_specs=[whole(lead) for lead in leads] + [pl.BlockSpec(memory_space=pl.ANY)],
            scratch_shapes=[
                pltpu.VMEM((rows * taps, tile, tile), jnp.bfloat16),
                pltpu.VMEM((rows, tile, tile), jnp.bfloat16),
                pltpu.VMEM((4 * rows, tile, tile), jnp.bfloat16),
                pltpu.VMEM((slots, rows * tile), jnp.bfloat16),
                pltpu.VMEM((outer, rows * tile), jnp.bfloat16),
                pltpu.VMEM((outer + tile, ROWS_PER_CHUNK * tile), jnp.float32),
                pltpu.SemaphoreType.DMA((rows // ROWS_PER_CHUNK + 7,)),
            ],
        ),
        out_shape=[
            jax.ShapeDtypeStruct((lead, members, members, tile, tile), jnp.bfloat16)
            for lead in leads
        ]
        + [jax.ShapeDtypeStruct((slots, rows * tile), jnp.bfloat16)],
        compiler_params=pltpu.CompilerParams(vmem_limit_bytes=48 * 1024 * 1024),
        cost_estimate=pl.CostEstimate(
            flops=2 * tile**3 * rows * members * (4 + 20 * members),
            bytes_accessed=2 * (a_tiles.size + 20 * dinv.size),
            transcendentals=0,
        ),
        name="partial_blocks",
    )(*lists, a_tiles.reshape(rows * taps, tile, tile), dinv, *tents, own_right)


def own_rows_kernel(members, left_own, right_all, own, left, right, sems):
    copies = [
        pltpu.make_async_copy(left_own, left, sems.at[0]),
        pltpu.make_async_copy(right_all, right, sems.at[1]),
    ]
    for copy in copies:
        copy.start()
    for copy in copies:
        copy.wait()
    product(left, right, (own,), {}, members, own.shape[-1])


def own_rows(left, right, members):
    tile = left.shape[0] // members
    block = (5, members, members, tile, tile)
    return pl.pallas_call(
        functools.partial(own_rows_kernel, members),
        grid=(1,),
        in_specs=[pl.BlockSpec(memory_space=pl.ANY)] * 2,
        out_specs=pl.BlockSpec(block, lambda s: (0,) * 5),
        out_shape=jax.ShapeDtypeStruct(block, jnp.float32),
        scratch_shapes=[
            pltpu.VMEM(left.shape, left.dtype),
            pltpu.VMEM(right.shape, right.dtype),
            pltpu.SemaphoreType.DMA((2,)),
        ],
        compiler_params=pltpu.CompilerParams(vmem_limit_bytes=32 * 1024 * 1024),
        cost_estimate=pl.CostEstimate(
            flops=2 * left.size * right.shape[0],
            bytes_accessed=2 * (left.size + right.size),
            transcendentals=0,
        ),
        name="own_rows",
    )(left, right)


def window_kernel(*refs):
    every = tuple(range(5))
    held = (kept_members(DOWN), kept_members(UP), every, every, every)
    behind, ahead = refs[5:7]
    for out, half in zip(refs[7:], HALVES):
        for position, offset in enumerate(half):
            if offset in (AHEAD, BEHIND):
                out[position] = (ahead if offset == AHEAD else behind)[0]
                continue
            total = None
            for shift, values, directions in zip(CROSS_SHIFTS, refs, held):
                for d, direction in enumerate(directions):
                    member = CROSS_SHIFTS[direction]
                    if (shift[0] + member[0], shift[1] + member[1]) == WINDOW_SHIFTS[offset]:
                        term = values[d].astype(jnp.float32)
                        total = term if total is None else total + term
            out[position] = total.astype(out.dtype)


def finished_window(blocks):
    _, members, _, tile, _ = blocks[0].shape
    spec = lambda lead: pl.BlockSpec(
        (lead, 1, members, tile, tile), lambda m: (0, m, 0, 0, 0)
    )
    return pl.pallas_call(
        window_kernel,
        grid=(members,),
        in_specs=[spec(block.shape[0]) for block in blocks],
        out_specs=[spec(len(half)) for half in HALVES],
        out_shape=[
            jax.ShapeDtypeStruct((len(half), members, members, tile, tile), jnp.bfloat16)
            for half in HALVES
        ],
        compiler_params=pltpu.CompilerParams(vmem_limit_bytes=32 * 1024 * 1024),
        cost_estimate=pl.CostEstimate(
            flops=5 * blocks[4].size, bytes_accessed=16 * blocks[4].size, transcendentals=0
        ),
        name="finished_window",
    )(*blocks)


def place_kernel(lists, edges, row, valid, *refs):
    arrays, (out, nothing, sems) = refs[: len(lists)], refs[-3:]
    count = out.shape[0]
    nothing[...] = jnp.zeros_like(nothing)

    def each(act):
        def move(source, target, offset, sem):
            act(pltpu.make_async_copy(source, out.at[target, :, offset], sems.at[sem]))

        for index, (array, (held, written)) in enumerate(zip(arrays, lists)):

            def write(offset, target):
                source = array.at[held.index(offset)] if offset in held else nothing
                move(source, target, offset, index * 13 + offset)

            here = row[index]

            @pl.when(valid[index] == 1)
            def _():
                for offset in written:
                    if offset not in (AHEAD, BEHIND):
                        write(offset, here)

            if AHEAD in written:

                @pl.when((valid[index] == 1) & (here + 1 < count))
                def _():
                    write(AHEAD, here + 1)

            if BEHIND in written:

                @pl.when((valid[index] == 1) & (here > 0))
                def _():
                    write(BEHIND, here - 1)

        if edges:
            move(nothing, 0, AHEAD, 13 * len(lists))
            move(nothing, count - 1, BEHIND, 13 * len(lists) + 1)

    each(lambda copy: copy.start())
    each(lambda copy: copy.wait())


def placed(out, pieces, count):
    arrays = [piece[0] for piece in pieces]
    members, _, tile, _ = arrays[0].shape[1:]
    scalars = pl.BlockSpec(memory_space=pltpu.SMEM)
    in_specs = [scalars] * 2 + [pl.BlockSpec(memory_space=pltpu.VMEM)] * len(arrays)
    operands = list(arrays)
    if out is not None:
        in_specs.append(pl.BlockSpec(memory_space=pl.ANY))
        operands.append(out)
    rows = jnp.stack([jnp.asarray(jnp.where(p[4], p[3], 0), jnp.int32) for p in pieces])
    valid = jnp.stack([jnp.asarray(p[4], jnp.int32) for p in pieces])
    return pl.pallas_call(
        functools.partial(place_kernel, tuple(p[1:3] for p in pieces), out is None),
        in_specs=in_specs,
        out_specs=pl.BlockSpec(memory_space=pl.ANY),
        scratch_shapes=[
            pltpu.VMEM((members, members, tile, tile), jnp.bfloat16),
            pltpu.SemaphoreType.DMA((len(pieces) * 13 + 2,)),
        ],
        out_shape=jax.ShapeDtypeStruct(
            (count, members, 13, members, tile, tile), jnp.bfloat16
        ),
        input_output_aliases={2 + len(arrays): 0} if out is not None else {},
        compiler_params=pltpu.CompilerParams(vmem_limit_bytes=24 * 1024 * 1024),
        cost_estimate=pl.CostEstimate(
            flops=0, bytes_accessed=6 * 13 * members * members * tile * tile, transcendentals=0
        ),
        name="placed",
    )(rows, valid, *operands)


def end_to_end(halves, grid_y, count_y):
    lower = tuple(o for o in TRAVEL if WINDOW_SHIFTS[o][1] in (0, 1))
    upper = tuple(o for o in TRAVEL if WINDOW_SHIFTS[o][1] in (-1, 0))
    start = jnp.where(grid_y == 0, TRAVEL.index(lower[0]), TRAVEL.index(upper[0]))
    sent = lax.dynamic_slice_in_dim(jnp.concatenate(halves, axis=0), start, len(lower), axis=0)
    last = count_y - 1
    moved = lax.ppermute(sent, "sy", [(0, last), (last, 0)])
    return [
        (moved, lower, TRAVEL, 0, grid_y == last),
        (moved, upper, TRAVEL, last, grid_y == 0),
    ]


def gathered_rows(halves, grid_y, count_y):
    chains = [(half, half) for half in halves]
    pieces = [(half, group, group, grid_y, True) for half, group in zip(halves, HALVES)]
    out = None
    for hop in range(1, count_y - 1):
        chains = [(shifted(a, "sy", 1), shifted(b, "sy", -1)) for a, b in chains]
        if hop == 1:
            direct = end_to_end(halves, grid_y, count_y)
        out = placed(out, pieces, count_y)
        if hop == 1:
            chains[1], out = lax.optimization_barrier((chains[1], out))
        pieces = []
        for (from_lower, from_upper), group in zip(chains, HALVES):
            pieces += [
                (from_lower, group, group, grid_y - hop, grid_y >= hop),
                (from_upper, group, group, grid_y + hop, grid_y + hop < count_y),
            ]
    out = placed(out, direct + pieces[2:], count_y)
    return placed(out, pieces[:2], count_y)


def local(a_tiles, columns, ptent, dinv, agg):
    grid_x = lax.axis_index("sx")
    grid_y = lax.axis_index("sy")
    count_y = lax.axis_size("sy")
    rows, taps, tile = a_tiles.shape[2], a_tiles.shape[3], a_tiles.shape[-1]
    coupling = a_tiles.reshape(rows, taps, tile, tile)
    inverse = dinv.reshape(rows, tile, tile)
    tent = jnp.swapaxes(ptent.reshape(rows, tile, tile), 1, 2)
    tents = (
        shifted(tent, "sy", 1),
        shifted(tent, "sy", -1),
        shifted(tent, "sx", 1),
        shifted(tent, "sx", -1),
    )
    own_right, own_left, *lists = own_slots(
        coupling,
        columns.reshape(rows * taps),
        inverse,
        tent,
        agg,
        jnp.stack([grid_x, grid_y]).astype(jnp.int32),
        count_y,
        MEMBERS,
    )
    to_lower_y, to_upper_y, to_lower_x, to_upper_x, behind, ahead, right = partial_blocks(
        coupling, inverse, tents, own_right, lists, MEMBERS
    )
    halves = finished_window(
        (
            shifted(to_upper_y, "sy", 1),
            shifted(to_lower_y, "sy", -1),
            shifted(to_upper_x, "sx", 1),
            shifted(to_lower_x, "sx", -1),
            own_rows(own_left, right, MEMBERS),
            behind,
            ahead,
        )
    )
    return gathered_rows(halves, grid_y, count_y)[None]


def solution(mesh):
    return jax.shard_map(
        local,
        mesh=mesh,
        in_specs=(
            P("sx", "sy", None, None, None, None),
            P("sx", "sy", None, None),
            P("sx", "sy", None, None, None),
            P("sx", "sy", None, None, None),
            P(),
        ),
        out_specs=P("sx", None, None, None, None, None, None),
        check_vma=False,
    )
```

```python
import functools

import jax
import jax.numpy as jnp
from jax import lax
from jax.experimental import pallas as pl
from jax.experimental.pallas import tpu as pltpu
from jax.sharding import PartitionSpec as P

CROSS_SHIFTS = ((0, -1), (0, 1), (-1, 0), (1, 0), (0, 0))
OWN = 4
DOWN, UP = CROSS_SHIFTS[:2]
HALO_ORDER = (2, 0, 1, 3)
WINDOW_SHIFTS = (
    (-2, 0),
    (-1, -1),
    (-1, 0),
    (-1, 1),
    (0, -2),
    (0, -1),
    (0, 0),
    (0, 1),
    (0, 2),
    (1, -1),
    (1, 0),
    (1, 1),
    (2, 0),
)
AHEAD, BEHIND = 4, 8
TRAVEL = (4, 1, 5, 9, 0, 2, 6, 10, 12, 3, 7, 11, 8)
HALVES = (TRAVEL[:6], TRAVEL[6:])
smoothing = 2.0 / 3.0
MEMBERS = 2
ROWS_PER_STEP = 4
ROWS_PER_CHUNK = 8
UNROLL = 8
NT = (((1,), (1,)), ((), ()))


def shifted(x, axis, by):
    length = lax.axis_size(axis)
    pairs = [(i, i + by) for i in range(length) if 0 <= i + by < length]
    return lax.ppermute(x, axis, pairs)


def lane_tiles(g, tile):
    return pl.ds(pl.multiple_of(g * tile, tile), tile)


def own_kernel(count_y, rows, members, taps, columns, agg, place, a_ref, dinv_ref, tent, *refs):
    right, left, tiles, sources, slots, ends, found = refs[:7]
    sums = refs[7:]
    tile = a_ref.shape[-1]
    step = pl.program_id(0)

    @pl.when(step == 0)
    def _():
        found[0] = 0

    listed = found[0]
    for u in range(ROWS_PER_STEP):
        g = step * ROWS_PER_STEP + u
        total = sums[u]
        total[...] = jnp.zeros_like(total)
        own_member = 0
        for k in range(taps):
            target = columns[g * taps + k]
            holder = target // rows
            step_x = holder // count_y - place[0]
            step_y = holder % count_y - place[1]
            direction = jnp.where(
                step_y == -1,
                0,
                jnp.where(step_y == 1, 1, jnp.where(step_x == -1, 2, jnp.where(step_x == 1, 3, OWN))),
            )
            member = agg[target] % members
            if k == 0:
                own_member = member
            else:
                tiles[listed] = g * taps + k
                sources[listed] = direction * rows + target % rows
                slots[listed] = direction * members + member
                listed += jnp.where(direction == OWN, 0, 1)
            z = lax.dot_general(
                tent[target % rows], a_ref[u, k], NT, preferred_element_type=jnp.float32
            )
            slot = jnp.where(direction == OWN, member, members)
            total[lane_tiles(slot, tile), :] += z.astype(jnp.bfloat16).astype(jnp.float32)
        here = slice(u * tile, (u + 1) * tile)
        applied = total[: members * tile, :].astype(jnp.bfloat16)
        right[:, here] = applied
        smooth = lax.dot_general(applied, dinv_ref[u], NT, preferred_element_type=jnp.float32)
        total[: members * tile, :] = -smoothing * smooth
        total[lane_tiles(own_member, tile), :] += tent[g].astype(jnp.float32)
        left[:, here] = total[: members * tile, :].astype(jnp.bfloat16)
    found[0] = listed
    ends[step] = listed


def own_slots(a_tiles, columns, dinv, tent, agg, place, count_y, members):
    rows, taps, tile = a_tiles.shape[0], a_tiles.shape[1], a_tiles.shape[-1]
    steps = rows // ROWS_PER_STEP
    span = ROWS_PER_STEP * tile
    scalars = pl.BlockSpec(memory_space=pltpu.SMEM)
    return pl.pallas_call(
        functools.partial(own_kernel, count_y, rows, members, taps),
        grid_spec=pltpu.PrefetchScalarGridSpec(
            num_scalar_prefetch=3,
            grid=(steps,),
            in_specs=[
                pl.BlockSpec((ROWS_PER_STEP, taps, tile, tile), lambda s, *_: (s, 0, 0, 0)),
                pl.BlockSpec((ROWS_PER_STEP, tile, tile), lambda s, *_: (s, 0, 0)),
                pl.BlockSpec((rows, tile, tile), lambda s, *_: (0, 0, 0)),
            ],
            out_specs=[pl.BlockSpec((members * tile, span), lambda s, *_: (0, s))] * 2
            + [scalars] * 4,
            scratch_shapes=[pltpu.SMEM((1,), jnp.int32)]
            + [pltpu.VMEM(((members + 1) * tile, tile), jnp.float32)] * ROWS_PER_STEP,
        ),
        out_shape=[jax.ShapeDtypeStruct((members * tile, rows * tile), jnp.bfloat16)] * 2
        + [jax.ShapeDtypeStruct((rows * taps,), jnp.int32)] * 3
        + [jax.ShapeDtypeStruct((steps,), jnp.int32)],
        compiler_params=pltpu.CompilerParams(vmem_limit_bytes=44 * 1024 * 1024),
        cost_estimate=pl.CostEstimate(
            flops=2 * tile**3 * rows * (taps + members),
            bytes_accessed=2 * (a_tiles.size + dinv.size * 6),
            transcendentals=0,
        ),
        name="own_slots",
    )(columns, agg, place, a_tiles, dinv, tent)


def kept_members(shift):
    lone = CROSS_SHIFTS.index(shift)
    return tuple((lone + 1 + p) % 5 for p in range(4))


def product(left, right, outs, lone, members, tile):
    width = members * tile

    def one(d2, carry):
        value = lax.dot_general(
            left[...],
            right[lane_tiles(d2, width), :],
            NT,
            preferred_element_type=jnp.float32,
        )

        def write(out, at, d1):
            for m in range(members):
                for m2 in range(members):
                    row = (d1 * members + m) * tile
                    block = value[row : row + tile, m2 * tile : (m2 + 1) * tile]
                    out[at, m, m2] = block.astype(out.dtype)

        for d1, out in enumerate(outs):
            if d1 not in lone:
                write(out, d2, d1)
                continue
            direction, single = lone[d1]

            @pl.when(d2 == direction)
            def _():
                write(single, 0, d1)

            @pl.when(d2 != direction)
            def _():
                write(out, (d2 + 4 - direction) % 5, d1)

        return carry

    lax.fori_loop(0, 5, one, 0)


def smoothed_rows(left, right, first, count, dinv, g, tile):
    lanes = lane_tiles(g, tile)
    smooth = lax.dot_general(
        right[first : first + count, lanes], dinv[g], NT, preferred_element_type=jnp.float32
    )
    left[:count, lanes] = (-smoothing * smooth).astype(jnp.bfloat16)


def partial_kernel(members, taps, tiles, sources, slots, ends, *refs):
    a_tiles, dinv_hbm, *tents = refs[:6]
    right_own, *outs, behind, ahead, right_out = refs[6:14]
    a_held, dinv, tent, right, left, sums, sems = refs[14:]
    tile = dinv.shape[-1]
    rows = dinv.shape[0]
    chunks = rows // ROWS_PER_CHUNK
    outer = 4 * members
    per = ROWS_PER_CHUNK * taps

    def a_copy(c):
        part = pl.ds(c * per, per)
        return pltpu.make_async_copy(a_tiles.at[part], a_held.at[part], sems.at[c])

    tent_copies = [
        pltpu.make_async_copy(source, tent.at[pl.ds(d * rows, rows)], sems.at[chunks + d])
        for d, source in zip(HALO_ORDER, tents)
    ]
    dinv_copy = pltpu.make_async_copy(dinv_hbm, dinv, sems.at[chunks + 4])
    own_part = (pl.ds(outer * tile, members * tile), slice(None))
    own_copy = pltpu.make_async_copy(right_own, right.at[own_part], sems.at[chunks + 5])
    out_copy = pltpu.make_async_copy(right, right_out, sems.at[chunks + 6])
    for copy in tent_copies:
        copy.start()
    a_copy(0).start()
    sums[...] = jnp.zeros_like(sums)
    for copy in tent_copies:
        copy.wait()
    dinv_copy.start()
    for c in range(1, chunks):
        a_copy(c).start()
    own_copy.start()

    def one_chunk(c, first):
        a_copy(c).wait()
        last = ends[(c + 1) * (ROWS_PER_CHUNK // ROWS_PER_STEP) - 1]

        def some(n, carry):
            found = []
            for u in range(UNROLL):
                at = first + UNROLL * n + u
                index = jnp.minimum(at, last - 1)
                number = tiles[index]
                slot = jnp.where(at < last, slots[index], outer)
                z = lax.dot_general(
                    tent[sources[index]], a_held[number], NT, preferred_element_type=jnp.float32
                )
                found.append((slot, number // taps - c * ROWS_PER_CHUNK, z))
            for slot, row, z in found:
                at = (lane_tiles(slot, tile), lane_tiles(row, tile))
                sums[at] += z.astype(jnp.bfloat16).astype(jnp.float32)
            return carry

        lax.fori_loop(0, (last - first + UNROLL - 1) // UNROLL, some, 0)
        lanes = lane_tiles(c, ROWS_PER_CHUNK * tile)
        right[: outer * tile, lanes] = sums[: outer * tile, :].astype(jnp.bfloat16)
        sums[...] = jnp.zeros_like(sums)

        @pl.when(c == 0)
        def _():
            dinv_copy.wait()

        for u in range(ROWS_PER_CHUNK):
            g = c * ROWS_PER_CHUNK + u
            lanes = lane_tiles(g, tile)
            smooth = lax.dot_general(
                right[: outer * tile, lanes], dinv[g], NT, preferred_element_type=jnp.float32
            )
            left[: outer * tile, lanes] = (-smoothing * smooth).astype(jnp.bfloat16)
        return last

    lax.fori_loop(0, chunks, one_chunk, 0)
    own_copy.wait()
    out_copy.start()
    lone = {d: (CROSS_SHIFTS.index(t), out) for d, t, out in ((0, UP, behind), (1, DOWN, ahead))}
    product(left, right, outs, lone, members, tile)
    out_copy.wait()


def partial_blocks(a_tiles, dinv, tents, own_right, lists, members):
    rows, taps, tile = a_tiles.shape[0], a_tiles.shape[1], a_tiles.shape[-1]
    whole = lambda lead: pl.BlockSpec((lead, members, members, tile, tile), lambda s, *_: (0,) * 5)
    leads = (4, 4, 5, 5, 1, 1)
    outer = 4 * members * tile
    slots = outer + members * tile
    return pl.pallas_call(
        functools.partial(partial_kernel, members, taps),
        grid_spec=pltpu.PrefetchScalarGridSpec(
            num_scalar_prefetch=4,
            grid=(1,),
            in_specs=[pl.BlockSpec(memory_space=pl.ANY)] * 7,
            out_specs=[whole(lead) for lead in leads] + [pl.BlockSpec(memory_space=pl.ANY)],
            scratch_shapes=[
                pltpu.VMEM((rows * taps, tile, tile), jnp.bfloat16),
                pltpu.VMEM((rows, tile, tile), jnp.bfloat16),
                pltpu.VMEM((4 * rows, tile, tile), jnp.bfloat16),
                pltpu.VMEM((slots, rows * tile), jnp.bfloat16),
                pltpu.VMEM((outer, rows * tile), jnp.bfloat16),
                pltpu.VMEM((outer + tile, ROWS_PER_CHUNK * tile), jnp.float32),
                pltpu.SemaphoreType.DMA((rows // ROWS_PER_CHUNK + 7,)),
            ],
        ),
        out_shape=[
            jax.ShapeDtypeStruct((lead, members, members, tile, tile), jnp.bfloat16)
            for lead in leads
        ]
        + [jax.ShapeDtypeStruct((slots, rows * tile), jnp.bfloat16)],
        compiler_params=pltpu.CompilerParams(vmem_limit_bytes=48 * 1024 * 1024),
        cost_estimate=pl.CostEstimate(
            flops=2 * tile**3 * rows * members * (4 + 20 * members),
            bytes_accessed=2 * (a_tiles.size + 20 * dinv.size),
            transcendentals=0,
        ),
        name="partial_blocks",
    )(*lists, a_tiles.reshape(rows * taps, tile, tile), dinv, *tents, own_right)


def own_rows_kernel(members, left_own, right_all, own, left, right, sems):
    copies = [
        pltpu.make_async_copy(left_own, left, sems.at[0]),
        pltpu.make_async_copy(right_all, right, sems.at[1]),
    ]
    for copy in copies:
        copy.start()
    for copy in copies:
        copy.wait()
    product(left, right, (own,), {}, members, own.shape[-1])


def own_rows(left, right, members):
    tile = left.shape[0] // members
    block = (5, members, members, tile, tile)
    return pl.pallas_call(
        functools.partial(own_rows_kernel, members),
        grid=(1,),
        in_specs=[pl.BlockSpec(memory_space=pl.ANY)] * 2,
        out_specs=pl.BlockSpec(block, lambda s: (0,) * 5),
        out_shape=jax.ShapeDtypeStruct(block, jnp.float32),
        scratch_shapes=[
            pltpu.VMEM(left.shape, left.dtype),
            pltpu.VMEM(right.shape, right.dtype),
            pltpu.SemaphoreType.DMA((2,)),
        ],
        compiler_params=pltpu.CompilerParams(vmem_limit_bytes=32 * 1024 * 1024),
        cost_estimate=pl.CostEstimate(
            flops=2 * left.size * right.shape[0],
            bytes_accessed=2 * (left.size + right.size),
            transcendentals=0,
        ),
        name="own_rows",
    )(left, right)


def window_kernel(*refs):
    every = tuple(range(5))
    held = (kept_members(DOWN), kept_members(UP), every, every, every)
    behind, ahead = refs[5:7]
    for out, half in zip(refs[7:], HALVES):
        for position, offset in enumerate(half):
            if offset in (AHEAD, BEHIND):
                out[position] = (ahead if offset == AHEAD else behind)[0]
                continue
            total = None
            for shift, values, directions in zip(CROSS_SHIFTS, refs, held):
                for d, direction in enumerate(directions):
                    member = CROSS_SHIFTS[direction]
                    if (shift[0] + member[0], shift[1] + member[1]) == WINDOW_SHIFTS[offset]:
                        term = values[d].astype(jnp.float32)
                        total = term if total is None else total + term
            out[position] = total.astype(out.dtype)


def finished_window(blocks):
    _, members, _, tile, _ = blocks[0].shape
    spec = lambda lead: pl.BlockSpec(
        (lead, 1, members, tile, tile), lambda m: (0, m, 0, 0, 0)
    )
    return pl.pallas_call(
        window_kernel,
        grid=(members,),
        in_specs=[spec(block.shape[0]) for block in blocks],
        out_specs=[spec(len(half)) for half in HALVES],
        out_shape=[
            jax.ShapeDtypeStruct((len(half), members, members, tile, tile), jnp.bfloat16)
            for half in HALVES
        ],
        compiler_params=pltpu.CompilerParams(vmem_limit_bytes=32 * 1024 * 1024),
        cost_estimate=pl.CostEstimate(
            flops=5 * blocks[4].size, bytes_accessed=16 * blocks[4].size, transcendentals=0
        ),
        name="finished_window",
    )(*blocks)


def place_kernel(lists, edges, row, valid, *refs):
    arrays, (out, nothing, sems) = refs[: len(lists)], refs[-3:]
    count = out.shape[0]
    nothing[...] = jnp.zeros_like(nothing)

    def each(act):
        def move(source, target, offset, sem):
            act(pltpu.make_async_copy(source, out.at[target, :, offset], sems.at[sem]))

        for index, (array, (held, written)) in enumerate(zip(arrays, lists)):

            def write(offset, target):
                source = array.at[held.index(offset)] if offset in held else nothing
                move(source, target, offset, index * 13 + offset)

            here = row[index]

            @pl.when(valid[index] == 1)
            def _():
                for offset in written:
                    if offset not in (AHEAD, BEHIND):
                        write(offset, here)

            if AHEAD in written:

                @pl.when((valid[index] == 1) & (here + 1 < count))
                def _():
                    write(AHEAD, here + 1)

            if BEHIND in written:

                @pl.when((valid[index] == 1) & (here > 0))
                def _():
                    write(BEHIND, here - 1)

        if edges:
            move(nothing, 0, AHEAD, 13 * len(lists))
            move(nothing, count - 1, BEHIND, 13 * len(lists) + 1)

    each(lambda copy: copy.start())
    each(lambda copy: copy.wait())


def placed(out, pieces, count):
    arrays = [piece[0] for piece in pieces]
    members, _, tile, _ = arrays[0].shape[1:]
    scalars = pl.BlockSpec(memory_space=pltpu.SMEM)
    in_specs = [scalars] * 2 + [pl.BlockSpec(memory_space=pltpu.VMEM)] * len(arrays)
    operands = list(arrays)
    if out is not None:
        in_specs.append(pl.BlockSpec(memory_space=pl.ANY))
        operands.append(out)
    rows = jnp.stack([jnp.asarray(jnp.where(p[4], p[3], 0), jnp.int32) for p in pieces])
    valid = jnp.stack([jnp.asarray(p[4], jnp.int32) for p in pieces])
    return pl.pallas_call(
        functools.partial(place_kernel, tuple(p[1:3] for p in pieces), out is None),
        in_specs=in_specs,
        out_specs=pl.BlockSpec(memory_space=pl.ANY),
        scratch_shapes=[
            pltpu.VMEM((members, members, tile, tile), jnp.bfloat16),
            pltpu.SemaphoreType.DMA((len(pieces) * 13 + 2,)),
        ],
        out_shape=jax.ShapeDtypeStruct(
            (count, members, 13, members, tile, tile), jnp.bfloat16
        ),
        input_output_aliases={2 + len(arrays): 0} if out is not None else {},
        compiler_params=pltpu.CompilerParams(vmem_limit_bytes=24 * 1024 * 1024),
        cost_estimate=pl.CostEstimate(
            flops=0, bytes_accessed=6 * 13 * members * members * tile * tile, transcendentals=0
        ),
        name="placed",
    )(rows, valid, *operands)


def end_to_end(halves, grid_y, count_y):
    lower = tuple(o for o in TRAVEL if WINDOW_SHIFTS[o][1] in (0, 1))
    upper = tuple(o for o in TRAVEL if WINDOW_SHIFTS[o][1] in (-1, 0))
    start = jnp.where(grid_y == 0, TRAVEL.index(lower[0]), TRAVEL.index(upper[0]))
    sent = lax.dynamic_slice_in_dim(jnp.concatenate(halves, axis=0), start, len(lower), axis=0)
    last = count_y - 1
    moved = lax.ppermute(sent, "sy", [(0, last), (last, 0)])
    return [
        (moved, lower, TRAVEL, 0, grid_y == last),
        (moved, upper, TRAVEL, last, grid_y == 0),
    ]


def gathered_rows(halves, grid_y, count_y):
    chains = [(half, half) for half in halves]
    pieces = [(half, group, group, grid_y, True) for half, group in zip(halves, HALVES)]
    out = None
    for hop in range(1, count_y - 1):
        chains = [(shifted(a, "sy", 1), shifted(b, "sy", -1)) for a, b in chains]
        if hop == 1:
            direct = end_to_end(halves, grid_y, count_y)
        out = placed(out, pieces, count_y)
        if hop == 1:
            chains[1], out = lax.optimization_barrier((chains[1], out))
        pieces = []
        for (from_lower, from_upper), group in zip(chains, HALVES):
            pieces += [
                (from_lower, group, group, grid_y - hop, grid_y >= hop),
                (from_upper, group, group, grid_y + hop, grid_y + hop < count_y),
            ]
    out = placed(out, direct + pieces[2:], count_y)
    return placed(out, pieces[:2], count_y)


def local(a_tiles, columns, ptent, dinv, agg):
    grid_x = lax.axis_index("sx")
    grid_y = lax.axis_index("sy")
    count_y = lax.axis_size("sy")
    rows, taps, tile = a_tiles.shape[2], a_tiles.shape[3], a_tiles.shape[-1]
    coupling = a_tiles.reshape(rows, taps, tile, tile)
    inverse = dinv.reshape(rows, tile, tile)
    tent = jnp.swapaxes(ptent.reshape(rows, tile, tile), 1, 2)
    tents = (
        shifted(tent, "sx", 1),
        shifted(tent, "sy", 1),
        shifted(tent, "sy", -1),
        shifted(tent, "sx", -1),
    )
    own_right, own_left, *lists = own_slots(
        coupling,
        columns.reshape(rows * taps),
        inverse,
        tent,
        agg,
        jnp.stack([grid_x, grid_y]).astype(jnp.int32),
        count_y,
        MEMBERS,
    )
    to_lower_y, to_upper_y, to_lower_x, to_upper_x, behind, ahead, right = partial_blocks(
        coupling, inverse, tents, own_right, lists, MEMBERS
    )
    halves = finished_window(
        (
            shifted(to_upper_y, "sy", 1),
            shifted(to_lower_y, "sy", -1),
            shifted(to_upper_x, "sx", 1),
            shifted(to_lower_x, "sx", -1),
            own_rows(own_left, right, MEMBERS),
            behind,
            ahead,
        )
    )
    return gathered_rows(halves, grid_y, count_y)[None]


def solution(mesh):
    return jax.shard_map(
        local,
        mesh=mesh,
        in_specs=(
            P("sx", "sy", None, None, None, None),
            P("sx", "sy", None, None),
            P("sx", "sy", None, None, None),
            P("sx", "sy", None, None, None),
            P(),
        ),
        out_specs=P("sx", None, None, None, None, None, None),
        check_vma=False,
    )
```

```python
import functools

import jax
import jax.numpy as jnp
from jax import lax
from jax.experimental import pallas as pl
from jax.experimental.pallas import tpu as pltpu
from jax.sharding import PartitionSpec as P

CROSS_SHIFTS = ((0, -1), (0, 1), (-1, 0), (1, 0), (0, 0))
OWN = 4
DOWN, UP = CROSS_SHIFTS[:2]
HALO_ORDER = (2, 0, 1, 3)
WINDOW_SHIFTS = (
    (-2, 0),
    (-1, -1),
    (-1, 0),
    (-1, 1),
    (0, -2),
    (0, -1),
    (0, 0),
    (0, 1),
    (0, 2),
    (1, -1),
    (1, 0),
    (1, 1),
    (2, 0),
)
AHEAD, BEHIND = 4, 8
TRAVEL = (4, 1, 5, 9, 0, 2, 6, 10, 12, 3, 7, 11, 8)
HALVES = (TRAVEL[:6], TRAVEL[6:])
smoothing = 2.0 / 3.0
MEMBERS = 2
ROWS_PER_STEP = 4
ROWS_PER_CHUNK = 8
UNROLL = 8
NT = (((1,), (1,)), ((), ()))


def shifted(x, axis, by):
    length = lax.axis_size(axis)
    pairs = [(i, i + by) for i in range(length) if 0 <= i + by < length]
    return lax.ppermute(x, axis, pairs)


def lane_tiles(g, tile):
    return pl.ds(pl.multiple_of(g * tile, tile), tile)


def own_kernel(count_y, rows, members, taps, columns, agg, place, a_ref, dinv_ref, tent, *refs):
    right, left, tiles, sources, slots, ends, found = refs[:7]
    sums = refs[7:]
    tile = a_ref.shape[-1]
    step = pl.program_id(0)

    @pl.when(step == 0)
    def _():
        found[0] = 0

    listed = found[0]
    for u in range(ROWS_PER_STEP):
        g = step * ROWS_PER_STEP + u
        total = sums[u]
        total[...] = jnp.zeros_like(total)
        own_member = 0
        for k in range(taps):
            target = columns[g * taps + k]
            holder = target // rows
            step_x = holder // count_y - place[0]
            step_y = holder % count_y - place[1]
            direction = jnp.where(
                step_y == -1,
                0,
                jnp.where(step_y == 1, 1, jnp.where(step_x == -1, 2, jnp.where(step_x == 1, 3, OWN))),
            )
            member = agg[target] % members
            if k == 0:
                own_member = member
            else:
                tiles[listed] = g * taps + k
                sources[listed] = direction * rows + target % rows
                slots[listed] = direction * members + member
                listed += jnp.where(direction == OWN, 0, 1)
            z = lax.dot_general(
                tent[target % rows], a_ref[u, k], NT, preferred_element_type=jnp.float32
            )
            slot = jnp.where(direction == OWN, member, members)
            total[lane_tiles(slot, tile), :] += z.astype(jnp.bfloat16).astype(jnp.float32)
        here = slice(u * tile, (u + 1) * tile)
        applied = total[: members * tile, :].astype(jnp.bfloat16)
        right[:, here] = applied
        smooth = lax.dot_general(applied, dinv_ref[u], NT, preferred_element_type=jnp.float32)
        total[: members * tile, :] = -smoothing * smooth
        total[lane_tiles(own_member, tile), :] += tent[g].astype(jnp.float32)
        left[:, here] = total[: members * tile, :].astype(jnp.bfloat16)
    found[0] = listed
    ends[step] = listed


def own_slots(a_tiles, columns, dinv, tent, agg, place, count_y, members):
    rows, taps, tile = a_tiles.shape[0], a_tiles.shape[1], a_tiles.shape[-1]
    steps = rows // ROWS_PER_STEP
    span = ROWS_PER_STEP * tile
    scalars = pl.BlockSpec(memory_space=pltpu.SMEM)
    return pl.pallas_call(
        functools.partial(own_kernel, count_y, rows, members, taps),
        grid_spec=pltpu.PrefetchScalarGridSpec(
            num_scalar_prefetch=3,
            grid=(steps,),
            in_specs=[
                pl.BlockSpec((ROWS_PER_STEP, taps, tile, tile), lambda s, *_: (s, 0, 0, 0)),
                pl.BlockSpec((ROWS_PER_STEP, tile, tile), lambda s, *_: (s, 0, 0)),
                pl.BlockSpec((rows, tile, tile), lambda s, *_: (0, 0, 0)),
            ],
            out_specs=[pl.BlockSpec((members * tile, span), lambda s, *_: (0, s))] * 2
            + [scalars] * 4,
            scratch_shapes=[pltpu.SMEM((1,), jnp.int32)]
            + [pltpu.VMEM(((members + 1) * tile, tile), jnp.float32)] * ROWS_PER_STEP,
        ),
        out_shape=[jax.ShapeDtypeStruct((members * tile, rows * tile), jnp.bfloat16)] * 2
        + [jax.ShapeDtypeStruct((rows * taps,), jnp.int32)] * 3
        + [jax.ShapeDtypeStruct((steps,), jnp.int32)],
        compiler_params=pltpu.CompilerParams(vmem_limit_bytes=44 * 1024 * 1024),
        cost_estimate=pl.CostEstimate(
            flops=2 * tile**3 * rows * (taps + members),
            bytes_accessed=2 * (a_tiles.size + dinv.size * 6),
            transcendentals=0,
        ),
        name="own_slots",
    )(columns, agg, place, a_tiles, dinv, tent)


def kept_members(shift):
    lone = CROSS_SHIFTS.index(shift)
    return tuple((lone + 1 + p) % 5 for p in range(4))


def product(left, right, outs, lone, members, tile):
    value = lax.dot_general(left[...], right[...], NT, preferred_element_type=jnp.float32)
    for d1, out in enumerate(outs):
        for d2 in range(5):
            target, at = out, d2
            if d1 in lone:
                direction, single = lone[d1]
                target, at = (single, 0) if d2 == direction else (out, (d2 + 4 - direction) % 5)
            for m in range(members):
                for m2 in range(members):
                    row, column = (d1 * members + m) * tile, (d2 * members + m2) * tile
                    block = value[row : row + tile, column : column + tile]
                    target[at, m, m2] = block.astype(target.dtype)


def partial_kernel(members, taps, tiles, sources, slots, ends, *refs):
    a_tiles, dinv_hbm, *tents = refs[:6]
    right_own, *outs, behind, ahead, right_out = refs[6:14]
    a_held, dinv, tent, right, left, sums, sems = refs[14:]
    tile = dinv.shape[-1]
    rows = dinv.shape[0]
    chunks = rows // ROWS_PER_CHUNK
    outer = 4 * members
    per = ROWS_PER_CHUNK * taps

    def a_copy(c):
        part = pl.ds(c * per, per)
        return pltpu.make_async_copy(a_tiles.at[part], a_held.at[part], sems.at[c])

    tent_copies = [
        pltpu.make_async_copy(source, tent.at[pl.ds(d * rows, rows)], sems.at[chunks + d])
        for d, source in zip(HALO_ORDER, tents)
    ]
    dinv_copy = pltpu.make_async_copy(dinv_hbm, dinv, sems.at[chunks + 4])
    own_part = (pl.ds(outer * tile, members * tile), slice(None))
    own_copy = pltpu.make_async_copy(right_own, right.at[own_part], sems.at[chunks + 5])
    out_copy = pltpu.make_async_copy(right, right_out, sems.at[chunks + 6])
    for copy in tent_copies:
        copy.start()
    a_copy(0).start()
    sums[...] = jnp.zeros_like(sums)
    for copy in tent_copies:
        copy.wait()
    dinv_copy.start()
    for c in range(1, chunks):
        a_copy(c).start()
    own_copy.start()

    def one_chunk(c, first):
        a_copy(c).wait()
        last = ends[(c + 1) * (ROWS_PER_CHUNK // ROWS_PER_STEP) - 1]

        def some(n, carry):
            found = []
            for u in range(UNROLL):
                at = first + UNROLL * n + u
                index = jnp.minimum(at, last - 1)
                number = tiles[index]
                slot = jnp.where(at < last, slots[index], outer)
                z = lax.dot_general(
                    tent[sources[index]], a_held[number], NT, preferred_element_type=jnp.float32
                )
                found.append((slot, number // taps - c * ROWS_PER_CHUNK, z))
            for slot, row, z in found:
                at = (lane_tiles(slot, tile), lane_tiles(row, tile))
                sums[at] += z.astype(jnp.bfloat16).astype(jnp.float32)
            return carry

        lax.fori_loop(0, (last - first + UNROLL - 1) // UNROLL, some, 0)
        lanes = lane_tiles(c, ROWS_PER_CHUNK * tile)
        right[: outer * tile, lanes] = sums[: outer * tile, :].astype(jnp.bfloat16)
        sums[...] = jnp.zeros_like(sums)

        @pl.when(c == 0)
        def _():
            dinv_copy.wait()

        for u in range(ROWS_PER_CHUNK):
            g = c * ROWS_PER_CHUNK + u
            lanes = lane_tiles(g, tile)
            smooth = lax.dot_general(
                right[: outer * tile, lanes], dinv[g], NT, preferred_element_type=jnp.float32
            )
            left[: outer * tile, lanes] = (-smoothing * smooth).astype(jnp.bfloat16)
        return last

    lax.fori_loop(0, chunks, one_chunk, 0)
    own_copy.wait()
    out_copy.start()
    lone = {d: (CROSS_SHIFTS.index(t), out) for d, t, out in ((0, UP, behind), (1, DOWN, ahead))}
    product(left, right, outs, lone, members, tile)
    out_copy.wait()


def partial_blocks(a_tiles, dinv, tents, own_right, lists, members):
    rows, taps, tile = a_tiles.shape[0], a_tiles.shape[1], a_tiles.shape[-1]
    whole = lambda lead: pl.BlockSpec((lead, members, members, tile, tile), lambda s, *_: (0,) * 5)
    leads = (4, 4, 5, 5, 1, 1)
    outer = 4 * members * tile
    slots = outer + members * tile
    return pl.pallas_call(
        functools.partial(partial_kernel, members, taps),
        grid_spec=pltpu.PrefetchScalarGridSpec(
            num_scalar_prefetch=4,
            grid=(1,),
            in_specs=[pl.BlockSpec(memory_space=pl.ANY)] * 7,
            out_specs=[whole(lead) for lead in leads] + [pl.BlockSpec(memory_space=pl.ANY)],
            scratch_shapes=[
                pltpu.VMEM((rows * taps, tile, tile), jnp.bfloat16),
                pltpu.VMEM((rows, tile, tile), jnp.bfloat16),
                pltpu.VMEM((4 * rows, tile, tile), jnp.bfloat16),
                pltpu.VMEM((slots, rows * tile), jnp.bfloat16),
                pltpu.VMEM((outer, rows * tile), jnp.bfloat16),
                pltpu.VMEM((outer + tile, ROWS_PER_CHUNK * tile), jnp.float32),
                pltpu.SemaphoreType.DMA((rows // ROWS_PER_CHUNK + 7,)),
            ],
        ),
        out_shape=[
            jax.ShapeDtypeStruct((lead, members, members, tile, tile), jnp.bfloat16)
            for lead in leads
        ]
        + [jax.ShapeDtypeStruct((slots, rows * tile), jnp.bfloat16)],
        compiler_params=pltpu.CompilerParams(vmem_limit_bytes=48 * 1024 * 1024),
        cost_estimate=pl.CostEstimate(
            flops=2 * tile**3 * rows * members * (4 + 20 * members),
            bytes_accessed=2 * (a_tiles.size + 20 * dinv.size),
            transcendentals=0,
        ),
        name="partial_blocks",
    )(*lists, a_tiles.reshape(rows * taps, tile, tile), dinv, *tents, own_right)


def own_rows_kernel(members, left_own, right_all, own, left, right, sems):
    copies = [
        pltpu.make_async_copy(left_own, left, sems.at[0]),
        pltpu.make_async_copy(right_all, right, sems.at[1]),
    ]
    for copy in copies:
        copy.start()
    for copy in copies:
        copy.wait()
    product(left, right, (own,), {}, members, own.shape[-1])


def own_rows(left, right, members):
    tile = left.shape[0] // members
    block = (5, members, members, tile, tile)
    return pl.pallas_call(
        functools.partial(own_rows_kernel, members),
        grid=(1,),
        in_specs=[pl.BlockSpec(memory_space=pl.ANY)] * 2,
        out_specs=pl.BlockSpec(block, lambda s: (0,) * 5),
        out_shape=jax.ShapeDtypeStruct(block, jnp.float32),
        scratch_shapes=[
            pltpu.VMEM(left.shape, left.dtype),
            pltpu.VMEM(right.shape, right.dtype),
            pltpu.SemaphoreType.DMA((2,)),
        ],
        compiler_params=pltpu.CompilerParams(vmem_limit_bytes=32 * 1024 * 1024),
        cost_estimate=pl.CostEstimate(
            flops=2 * left.size * right.shape[0],
            bytes_accessed=2 * (left.size + right.size),
            transcendentals=0,
        ),
        name="own_rows",
    )(left, right)


def window_kernel(*refs):
    every = tuple(range(5))
    held = (kept_members(DOWN), kept_members(UP), every, every, every)
    behind, ahead = refs[5:7]
    for out, half in zip(refs[7:], HALVES):
        for position, offset in enumerate(half):
            if offset in (AHEAD, BEHIND):
                out[position] = (ahead if offset == AHEAD else behind)[0]
                continue
            total = None
            for shift, values, directions in zip(CROSS_SHIFTS, refs, held):
                for d, direction in enumerate(directions):
                    member = CROSS_SHIFTS[direction]
                    if (shift[0] + member[0], shift[1] + member[1]) == WINDOW_SHIFTS[offset]:
                        term = values[d].astype(jnp.float32)
                        total = term if total is None else total + term
            out[position] = total.astype(out.dtype)


def finished_window(blocks):
    _, members, _, tile, _ = blocks[0].shape
    spec = lambda lead: pl.BlockSpec(
        (lead, 1, members, tile, tile), lambda m: (0, m, 0, 0, 0)
    )
    return pl.pallas_call(
        window_kernel,
        grid=(members,),
        in_specs=[spec(block.shape[0]) for block in blocks],
        out_specs=[spec(len(half)) for half in HALVES],
        out_shape=[
            jax.ShapeDtypeStruct((len(half), members, members, tile, tile), jnp.bfloat16)
            for half in HALVES
        ],
        compiler_params=pltpu.CompilerParams(vmem_limit_bytes=32 * 1024 * 1024),
        cost_estimate=pl.CostEstimate(
            flops=5 * blocks[4].size, bytes_accessed=16 * blocks[4].size, transcendentals=0
        ),
        name="finished_window",
    )(*blocks)


def place_kernel(lists, edges, row, valid, *refs):
    arrays, (out, nothing, sems) = refs[: len(lists)], refs[-3:]
    count = out.shape[0]
    nothing[...] = jnp.zeros_like(nothing)

    def each(act):
        def move(source, target, offset, sem):
            act(pltpu.make_async_copy(source, out.at[target, :, offset], sems.at[sem]))

        for index, (array, (held, written)) in enumerate(zip(arrays, lists)):

            def write(offset, target):
                source = array.at[held.index(offset)] if offset in held else nothing
                move(source, target, offset, index * 13 + offset)

            here = row[index]

            @pl.when(valid[index] == 1)
            def _():
                for offset in written:
                    if offset not in (AHEAD, BEHIND):
                        write(offset, here)

            if AHEAD in written:

                @pl.when((valid[index] == 1) & (here + 1 < count))
                def _():
                    write(AHEAD, here + 1)

            if BEHIND in written:

                @pl.when((valid[index] == 1) & (here > 0))
                def _():
                    write(BEHIND, here - 1)

        if edges:
            move(nothing, 0, AHEAD, 13 * len(lists))
            move(nothing, count - 1, BEHIND, 13 * len(lists) + 1)

    each(lambda copy: copy.start())
    each(lambda copy: copy.wait())


def placed(out, pieces, count):
    arrays = [piece[0] for piece in pieces]
    members, _, tile, _ = arrays[0].shape[1:]
    scalars = pl.BlockSpec(memory_space=pltpu.SMEM)
    in_specs = [scalars] * 2 + [pl.BlockSpec(memory_space=pltpu.VMEM)] * len(arrays)
    operands = list(arrays)
    if out is not None:
        in_specs.append(pl.BlockSpec(memory_space=pl.ANY))
        operands.append(out)
    rows = jnp.stack([jnp.asarray(jnp.where(p[4], p[3], 0), jnp.int32) for p in pieces])
    valid = jnp.stack([jnp.asarray(p[4], jnp.int32) for p in pieces])
    return pl.pallas_call(
        functools.partial(place_kernel, tuple(p[1:3] for p in pieces), out is None),
        in_specs=in_specs,
        out_specs=pl.BlockSpec(memory_space=pl.ANY),
        scratch_shapes=[
            pltpu.VMEM((members, members, tile, tile), jnp.bfloat16),
            pltpu.SemaphoreType.DMA((len(pieces) * 13 + 2,)),
        ],
        out_shape=jax.ShapeDtypeStruct(
            (count, members, 13, members, tile, tile), jnp.bfloat16
        ),
        input_output_aliases={2 + len(arrays): 0} if out is not None else {},
        compiler_params=pltpu.CompilerParams(vmem_limit_bytes=24 * 1024 * 1024),
        cost_estimate=pl.CostEstimate(
            flops=0, bytes_accessed=6 * 13 * members * members * tile * tile, transcendentals=0
        ),
        name="placed",
    )(rows, valid, *operands)


def end_to_end(halves, grid_y, count_y):
    lower = tuple(o for o in TRAVEL if WINDOW_SHIFTS[o][1] in (0, 1))
    upper = tuple(o for o in TRAVEL if WINDOW_SHIFTS[o][1] in (-1, 0))
    start = jnp.where(grid_y == 0, TRAVEL.index(lower[0]), TRAVEL.index(upper[0]))
    sent = lax.dynamic_slice_in_dim(jnp.concatenate(halves, axis=0), start, len(lower), axis=0)
    last = count_y - 1
    moved = lax.ppermute(sent, "sy", [(0, last), (last, 0)])
    return [
        (moved, lower, TRAVEL, 0, grid_y == last),
        (moved, upper, TRAVEL, last, grid_y == 0),
    ]


def gathered_rows(halves, grid_y, count_y):
    chains = [(half, half) for half in halves]
    pieces = [(half, group, group, grid_y, True) for half, group in zip(halves, HALVES)]
    out = None
    for hop in range(1, count_y - 1):
        chains = [(shifted(a, "sy", 1), shifted(b, "sy", -1)) for a, b in chains]
        if hop == 1:
            direct = end_to_end(halves, grid_y, count_y)
        out = placed(out, pieces, count_y)
        if hop == 1:
            chains[1], out = lax.optimization_barrier((chains[1], out))
        pieces = []
        for (from_lower, from_upper), group in zip(chains, HALVES):
            pieces += [
                (from_lower, group, group, grid_y - hop, grid_y >= hop),
                (from_upper, group, group, grid_y + hop, grid_y + hop < count_y),
            ]
    out = placed(out, direct + pieces[2:], count_y)
    return placed(out, pieces[:2], count_y)


def local(a_tiles, columns, ptent, dinv, agg):
    grid_x = lax.axis_index("sx")
    grid_y = lax.axis_index("sy")
    count_y = lax.axis_size("sy")
    rows, taps, tile = a_tiles.shape[2], a_tiles.shape[3], a_tiles.shape[-1]
    coupling = a_tiles.reshape(rows, taps, tile, tile)
    inverse = dinv.reshape(rows, tile, tile)
    tent = jnp.swapaxes(ptent.reshape(rows, tile, tile), 1, 2)
    tents = (
        shifted(tent, "sx", 1),
        shifted(tent, "sy", 1),
        shifted(tent, "sy", -1),
        shifted(tent, "sx", -1),
    )
    own_right, own_left, *lists = own_slots(
        coupling,
        columns.reshape(rows * taps),
        inverse,
        tent,
        agg,
        jnp.stack([grid_x, grid_y]).astype(jnp.int32),
        count_y,
        MEMBERS,
    )
    to_lower_y, to_upper_y, to_lower_x, to_upper_x, behind, ahead, right = partial_blocks(
        coupling, inverse, tents, own_right, lists, MEMBERS
    )
    halves = finished_window(
        (
            shifted(to_upper_y, "sy", 1),
            shifted(to_lower_y, "sy", -1),
            shifted(to_upper_x, "sx", 1),
            shifted(to_lower_x, "sx", -1),
            own_rows(own_left, right, MEMBERS),
            behind,
            ahead,
        )
    )
    return gathered_rows(halves, grid_y, count_y)[None]


def solution(mesh):
    return jax.shard_map(
        local,
        mesh=mesh,
        in_specs=(
            P("sx", "sy", None, None, None, None),
            P("sx", "sy", None, None),
            P("sx", "sy", None, None, None),
            P("sx", "sy", None, None, None),
            P(),
        ),
        out_specs=P("sx", None, None, None, None, None, None),
        check_vma=False,
    )
```

```python
import functools

import jax
import jax.numpy as jnp
from jax import lax
from jax.experimental import pallas as pl
from jax.experimental.pallas import tpu as pltpu
from jax.sharding import PartitionSpec as P

CROSS_SHIFTS = ((0, -1), (0, 1), (-1, 0), (1, 0), (0, 0))
OWN = 4
DOWN, UP = CROSS_SHIFTS[:2]
HALO_ORDER = (2, 0, 1, 3)
WINDOW_SHIFTS = (
    (-2, 0),
    (-1, -1),
    (-1, 0),
    (-1, 1),
    (0, -2),
    (0, -1),
    (0, 0),
    (0, 1),
    (0, 2),
    (1, -1),
    (1, 0),
    (1, 1),
    (2, 0),
)
AHEAD, BEHIND = 4, 8
TRAVEL = (4, 1, 5, 9, 0, 2, 6, 10, 12, 3, 7, 11, 8)
HALVES = (TRAVEL[:6], TRAVEL[6:])
smoothing = 2.0 / 3.0
MEMBERS = 2
ROWS_PER_STEP = 4
ROWS_PER_CHUNK = 8
UNROLL = 8
NT = (((1,), (1,)), ((), ()))


def shifted(x, axis, by):
    length = lax.axis_size(axis)
    pairs = [(i, i + by) for i in range(length) if 0 <= i + by < length]
    return lax.ppermute(x, axis, pairs)


def lane_tiles(g, tile):
    return pl.ds(pl.multiple_of(g * tile, tile), tile)


def own_kernel(count_y, rows, members, taps, columns, agg, place, a_ref, dinv_ref, tent, *refs):
    right, left, tiles, sources, slots, ends, found = refs[:7]
    sums = refs[7:]
    tile = a_ref.shape[-1]
    step = pl.program_id(0)

    @pl.when(step == 0)
    def _():
        found[0] = 0

    listed = found[0]
    for u in range(ROWS_PER_STEP):
        g = step * ROWS_PER_STEP + u
        total = sums[u]
        total[...] = jnp.zeros_like(total)
        own_member = 0
        for k in range(taps):
            target = columns[g * taps + k]
            holder = target // rows
            step_x = holder // count_y - place[0]
            step_y = holder % count_y - place[1]
            direction = jnp.where(
                step_y == -1,
                0,
                jnp.where(step_y == 1, 1, jnp.where(step_x == -1, 2, jnp.where(step_x == 1, 3, OWN))),
            )
            member = agg[target] % members
            if k == 0:
                own_member = member
            else:
                tiles[listed] = g * taps + k
                sources[listed] = direction * rows + target % rows
                slots[listed] = direction * members + member
                listed += jnp.where(direction == OWN, 0, 1)
            z = lax.dot_general(
                tent[target % rows], a_ref[u, k], NT, preferred_element_type=jnp.float32
            )
            slot = jnp.where(direction == OWN, member, members)
            total[lane_tiles(slot, tile), :] += z.astype(jnp.bfloat16).astype(jnp.float32)
        here = slice(u * tile, (u + 1) * tile)
        applied = total[: members * tile, :].astype(jnp.bfloat16)
        right[:, here] = applied
        smooth = lax.dot_general(applied, dinv_ref[u], NT, preferred_element_type=jnp.float32)
        total[: members * tile, :] = -smoothing * smooth
        total[lane_tiles(own_member, tile), :] += tent[g].astype(jnp.float32)
        left[:, here] = total[: members * tile, :].astype(jnp.bfloat16)
    found[0] = listed
    ends[step] = listed


def own_slots(a_tiles, columns, dinv, tent, agg, place, count_y, members):
    rows, taps, tile = a_tiles.shape[0], a_tiles.shape[1], a_tiles.shape[-1]
    steps = rows // ROWS_PER_STEP
    span = ROWS_PER_STEP * tile
    scalars = pl.BlockSpec(memory_space=pltpu.SMEM)
    return pl.pallas_call(
        functools.partial(own_kernel, count_y, rows, members, taps),
        grid_spec=pltpu.PrefetchScalarGridSpec(
            num_scalar_prefetch=3,
            grid=(steps,),
            in_specs=[
                pl.BlockSpec((ROWS_PER_STEP, taps, tile, tile), lambda s, *_: (s, 0, 0, 0)),
                pl.BlockSpec((ROWS_PER_STEP, tile, tile), lambda s, *_: (s, 0, 0)),
                pl.BlockSpec((rows, tile, tile), lambda s, *_: (0, 0, 0)),
            ],
            out_specs=[pl.BlockSpec((members * tile, span), lambda s, *_: (0, s))] * 2
            + [scalars] * 4,
            scratch_shapes=[pltpu.SMEM((1,), jnp.int32)]
            + [pltpu.VMEM(((members + 1) * tile, tile), jnp.float32)] * ROWS_PER_STEP,
        ),
        out_shape=[jax.ShapeDtypeStruct((members * tile, rows * tile), jnp.bfloat16)] * 2
        + [jax.ShapeDtypeStruct((rows * taps,), jnp.int32)] * 3
        + [jax.ShapeDtypeStruct((steps,), jnp.int32)],
        compiler_params=pltpu.CompilerParams(vmem_limit_bytes=44 * 1024 * 1024),
        cost_estimate=pl.CostEstimate(
            flops=2 * tile**3 * rows * (taps + members),
            bytes_accessed=2 * (a_tiles.size + dinv.size * 6),
            transcendentals=0,
        ),
        name="own_slots",
    )(columns, agg, place, a_tiles, dinv, tent)


def kept_members(shift):
    lone = CROSS_SHIFTS.index(shift)
    return tuple((lone + 1 + p) % 5 for p in range(4))


def product(left, right, outs, lone, members, tile):
    value = lax.dot_general(left, right, NT, preferred_element_type=jnp.float32)
    for d1, out in enumerate(outs):
        for d2 in range(5):
            target, at = out, d2
            if d1 in lone:
                direction, single = lone[d1]
                target, at = (single, 0) if d2 == direction else (out, (d2 + 4 - direction) % 5)
            for m in range(members):
                for m2 in range(members):
                    row, column = (d1 * members + m) * tile, (d2 * members + m2) * tile
                    block = value[row : row + tile, column : column + tile]
                    target[at, m, m2] = block.astype(target.dtype)


def partial_kernel(members, taps, tiles, sources, slots, ends, *refs):
    a_tiles, dinv_hbm, *tents = refs[:6]
    right_own, *outs, behind, ahead, right_out = refs[6:14]
    a_held, dinv, tent, right, left, sems = refs[14:]
    tile = dinv.shape[-1]
    rows = dinv.shape[0]
    chunks = rows // ROWS_PER_CHUNK
    outer = 4 * members
    per = ROWS_PER_CHUNK * taps
    depth = rows * tile

    def a_copy(c):
        part = pl.ds(c * per, per)
        return pltpu.make_async_copy(a_tiles.at[part], a_held.at[part], sems.at[c])

    tent_copies = [
        pltpu.make_async_copy(source, tent.at[pl.ds(d * rows, rows)], sems.at[chunks + d])
        for d, source in zip(HALO_ORDER, tents)
    ]
    dinv_copy = pltpu.make_async_copy(dinv_hbm, dinv, sems.at[chunks + 4])
    own_part = (pl.ds(outer * tile, members * tile), pl.ds(0, depth))
    own_copy = pltpu.make_async_copy(right_own, right.at[own_part], sems.at[chunks + 5])
    out_copy = pltpu.make_async_copy(
        right.at[:, pl.ds(0, depth)], right_out, sems.at[chunks + 6]
    )
    for copy in tent_copies:
        copy.start()
    dinv_copy.start()
    for c in range(chunks):
        a_copy(c).start()
    own_copy.start()
    right[: outer * tile, :] = jnp.zeros((outer * tile, right.shape[1]), right.dtype)
    left[...] = jnp.zeros_like(left)
    for copy in tent_copies:
        copy.wait()
    dinv_copy.wait()

    def one_chunk(c, first):
        a_copy(c).wait()
        last = ends[(c + 1) * (ROWS_PER_CHUNK // ROWS_PER_STEP) - 1]

        def some(n, carry):
            found = []
            for u in range(UNROLL):
                at = first + UNROLL * n + u
                index = jnp.minimum(at, last - 1)
                number = tiles[index]
                row = number // taps
                z = lax.dot_general(
                    tent[sources[index]], a_held[number], NT, preferred_element_type=jnp.float32
                ).astype(jnp.bfloat16)
                smooth = lax.dot_general(z, dinv[row], NT, preferred_element_type=jnp.float32)
                lanes = lane_tiles(jnp.where(at < last, row, rows), tile)
                found.append(((lane_tiles(slots[index], tile), lanes), z, smooth))
            for at, z, smooth in found:
                right[at] = (right[at].astype(jnp.float32) + z.astype(jnp.float32)).astype(
                    jnp.bfloat16
                )
                left[at] = (left[at].astype(jnp.float32) - smoothing * smooth).astype(jnp.bfloat16)
            return carry

        lax.fori_loop(0, (last - first + UNROLL - 1) // UNROLL, some, 0)
        return last

    lax.fori_loop(0, chunks, one_chunk, 0)
    own_copy.wait()
    out_copy.start()
    lone = {d: (CROSS_SHIFTS.index(t), out) for d, t, out in ((0, UP, behind), (1, DOWN, ahead))}
    product(left[:, :depth], right[:, :depth], outs, lone, members, tile)
    out_copy.wait()


def partial_blocks(a_tiles, dinv, tents, own_right, lists, members):
    rows, taps, tile = a_tiles.shape[0], a_tiles.shape[1], a_tiles.shape[-1]
    whole = lambda lead: pl.BlockSpec((lead, members, members, tile, tile), lambda s, *_: (0,) * 5)
    leads = (4, 4, 5, 5, 1, 1)
    outer = 4 * members * tile
    slots = outer + members * tile
    return pl.pallas_call(
        functools.partial(partial_kernel, members, taps),
        grid_spec=pltpu.PrefetchScalarGridSpec(
            num_scalar_prefetch=4,
            grid=(1,),
            in_specs=[pl.BlockSpec(memory_space=pl.ANY)] * 7,
            out_specs=[whole(lead) for lead in leads] + [pl.BlockSpec(memory_space=pl.ANY)],
            scratch_shapes=[
                pltpu.VMEM((rows * taps, tile, tile), jnp.bfloat16),
                pltpu.VMEM((rows, tile, tile), jnp.bfloat16),
                pltpu.VMEM((4 * rows, tile, tile), jnp.bfloat16),
                pltpu.VMEM((slots, (rows + 1) * tile), jnp.bfloat16),
                pltpu.VMEM((outer, (rows + 1) * tile), jnp.bfloat16),
                pltpu.SemaphoreType.DMA((rows // ROWS_PER_CHUNK + 7,)),
            ],
        ),
        out_shape=[
            jax.ShapeDtypeStruct((lead, members, members, tile, tile), jnp.bfloat16)
            for lead in leads
        ]
        + [jax.ShapeDtypeStruct((slots, rows * tile), jnp.bfloat16)],
        compiler_params=pltpu.CompilerParams(vmem_limit_bytes=48 * 1024 * 1024),
        cost_estimate=pl.CostEstimate(
            flops=2 * tile**3 * rows * (taps + 20 * members * members),
            bytes_accessed=2 * (a_tiles.size + 20 * dinv.size),
            transcendentals=0,
        ),
        name="partial_blocks",
    )(*lists, a_tiles.reshape(rows * taps, tile, tile), dinv, *tents, own_right)


def own_rows_kernel(members, left_own, right_all, own, left, right, sems):
    copies = [
        pltpu.make_async_copy(left_own, left, sems.at[0]),
        pltpu.make_async_copy(right_all, right, sems.at[1]),
    ]
    for copy in copies:
        copy.start()
    for copy in copies:
        copy.wait()
    product(left[...], right[...], (own,), {}, members, own.shape[-1])


def own_rows(left, right, members):
    tile = left.shape[0] // members
    block = (5, members, members, tile, tile)
    return pl.pallas_call(
        functools.partial(own_rows_kernel, members),
        grid=(1,),
        in_specs=[pl.BlockSpec(memory_space=pl.ANY)] * 2,
        out_specs=pl.BlockSpec(block, lambda s: (0,) * 5),
        out_shape=jax.ShapeDtypeStruct(block, jnp.float32),
        scratch_shapes=[
            pltpu.VMEM(left.shape, left.dtype),
            pltpu.VMEM(right.shape, right.dtype),
            pltpu.SemaphoreType.DMA((2,)),
        ],
        compiler_params=pltpu.CompilerParams(vmem_limit_bytes=32 * 1024 * 1024),
        cost_estimate=pl.CostEstimate(
            flops=2 * left.size * right.shape[0],
            bytes_accessed=2 * (left.size + right.size),
            transcendentals=0,
        ),
        name="own_rows",
    )(left, right)


def window_kernel(*refs):
    every = tuple(range(5))
    held = (kept_members(DOWN), kept_members(UP), every, every, every)
    behind, ahead = refs[5:7]
    for out, half in zip(refs[7:], HALVES):
        for position, offset in enumerate(half):
            if offset in (AHEAD, BEHIND):
                out[position] = (ahead if offset == AHEAD else behind)[0]
                continue
            total = None
            for shift, values, directions in zip(CROSS_SHIFTS, refs, held):
                for d, direction in enumerate(directions):
                    member = CROSS_SHIFTS[direction]
                    if (shift[0] + member[0], shift[1] + member[1]) == WINDOW_SHIFTS[offset]:
                        term = values[d].astype(jnp.float32)
                        total = term if total is None else total + term
            out[position] = total.astype(out.dtype)


def finished_window(blocks):
    _, members, _, tile, _ = blocks[0].shape
    spec = lambda lead: pl.BlockSpec(
        (lead, 1, members, tile, tile), lambda m: (0, m, 0, 0, 0)
    )
    return pl.pallas_call(
        window_kernel,
        grid=(members,),
        in_specs=[spec(block.shape[0]) for block in blocks],
        out_specs=[spec(len(half)) for half in HALVES],
        out_shape=[
            jax.ShapeDtypeStruct((len(half), members, members, tile, tile), jnp.bfloat16)
            for half in HALVES
        ],
        compiler_params=pltpu.CompilerParams(vmem_limit_bytes=32 * 1024 * 1024),
        cost_estimate=pl.CostEstimate(
            flops=5 * blocks[4].size, bytes_accessed=16 * blocks[4].size, transcendentals=0
        ),
        name="finished_window",
    )(*blocks)


def place_kernel(lists, edges, row, valid, *refs):
    arrays, (out, nothing, sems) = refs[: len(lists)], refs[-3:]
    count = out.shape[0]
    nothing[...] = jnp.zeros_like(nothing)

    def each(act):
        def move(source, target, offset, sem):
            act(pltpu.make_async_copy(source, out.at[target, :, offset], sems.at[sem]))

        for index, (array, (held, written)) in enumerate(zip(arrays, lists)):

            def write(offset, target):
                source = array.at[held.index(offset)] if offset in held else nothing
                move(source, target, offset, index * 13 + offset)

            here = row[index]

            @pl.when(valid[index] == 1)
            def _():
                for offset in written:
                    if offset not in (AHEAD, BEHIND):
                        write(offset, here)

            if AHEAD in written:

                @pl.when((valid[index] == 1) & (here + 1 < count))
                def _():
                    write(AHEAD, here + 1)

            if BEHIND in written:

                @pl.when((valid[index] == 1) & (here > 0))
                def _():
                    write(BEHIND, here - 1)

        if edges:
            move(nothing, 0, AHEAD, 13 * len(lists))
            move(nothing, count - 1, BEHIND, 13 * len(lists) + 1)

    each(lambda copy: copy.start())
    each(lambda copy: copy.wait())


def placed(out, pieces, count):
    arrays = [piece[0] for piece in pieces]
    members, _, tile, _ = arrays[0].shape[1:]
    scalars = pl.BlockSpec(memory_space=pltpu.SMEM)
    in_specs = [scalars] * 2 + [pl.BlockSpec(memory_space=pltpu.VMEM)] * len(arrays)
    operands = list(arrays)
    if out is not None:
        in_specs.append(pl.BlockSpec(memory_space=pl.ANY))
        operands.append(out)
    rows = jnp.stack([jnp.asarray(jnp.where(p[4], p[3], 0), jnp.int32) for p in pieces])
    valid = jnp.stack([jnp.asarray(p[4], jnp.int32) for p in pieces])
    return pl.pallas_call(
        functools.partial(place_kernel, tuple(p[1:3] for p in pieces), out is None),
        in_specs=in_specs,
        out_specs=pl.BlockSpec(memory_space=pl.ANY),
        scratch_shapes=[
            pltpu.VMEM((members, members, tile, tile), jnp.bfloat16),
            pltpu.SemaphoreType.DMA((len(pieces) * 13 + 2,)),
        ],
        out_shape=jax.ShapeDtypeStruct(
            (count, members, 13, members, tile, tile), jnp.bfloat16
        ),
        input_output_aliases={2 + len(arrays): 0} if out is not None else {},
        compiler_params=pltpu.CompilerParams(vmem_limit_bytes=24 * 1024 * 1024),
        cost_estimate=pl.CostEstimate(
            flops=0, bytes_accessed=6 * 13 * members * members * tile * tile, transcendentals=0
        ),
        name="placed",
    )(rows, valid, *operands)


def end_to_end(halves, grid_y, count_y):
    lower = tuple(o for o in TRAVEL if WINDOW_SHIFTS[o][1] in (0, 1))
    upper = tuple(o for o in TRAVEL if WINDOW_SHIFTS[o][1] in (-1, 0))
    start = jnp.where(grid_y == 0, TRAVEL.index(lower[0]), TRAVEL.index(upper[0]))
    sent = lax.dynamic_slice_in_dim(jnp.concatenate(halves, axis=0), start, len(lower), axis=0)
    last = count_y - 1
    moved = lax.ppermute(sent, "sy", [(0, last), (last, 0)])
    return [
        (moved, lower, TRAVEL, 0, grid_y == last),
        (moved, upper, TRAVEL, last, grid_y == 0),
    ]


def gathered_rows(halves, grid_y, count_y):
    chains = [(half, half) for half in halves]
    pieces = [(half, group, group, grid_y, True) for half, group in zip(halves, HALVES)]
    out = None
    for hop in range(1, count_y - 1):
        chains = [(shifted(a, "sy", 1), shifted(b, "sy", -1)) for a, b in chains]
        if hop == 1:
            direct = end_to_end(halves, grid_y, count_y)
        out = placed(out, pieces, count_y)
        if hop == 1:
            chains[1], out = lax.optimization_barrier((chains[1], out))
        pieces = []
        for (from_lower, from_upper), group in zip(chains, HALVES):
            pieces += [
                (from_lower, group, group, grid_y - hop, grid_y >= hop),
                (from_upper, group, group, grid_y + hop, grid_y + hop < count_y),
            ]
    out = placed(out, direct + pieces[2:], count_y)
    return placed(out, pieces[:2], count_y)


def local(a_tiles, columns, ptent, dinv, agg):
    grid_x = lax.axis_index("sx")
    grid_y = lax.axis_index("sy")
    count_y = lax.axis_size("sy")
    rows, taps, tile = a_tiles.shape[2], a_tiles.shape[3], a_tiles.shape[-1]
    coupling = a_tiles.reshape(rows, taps, tile, tile)
    inverse = dinv.reshape(rows, tile, tile)
    tent = jnp.swapaxes(ptent.reshape(rows, tile, tile), 1, 2)
    tents = (
        shifted(tent, "sx", 1),
        shifted(tent, "sy", 1),
        shifted(tent, "sy", -1),
        shifted(tent, "sx", -1),
    )
    own_right, own_left, *lists = own_slots(
        coupling,
        columns.reshape(rows * taps),
        inverse,
        tent,
        agg,
        jnp.stack([grid_x, grid_y]).astype(jnp.int32),
        count_y,
        MEMBERS,
    )
    to_lower_y, to_upper_y, to_lower_x, to_upper_x, behind, ahead, right = partial_blocks(
        coupling, inverse, tents, own_right, lists, MEMBERS
    )
    halves = finished_window(
        (
            shifted(to_upper_y, "sy", 1),
            shifted(to_lower_y, "sy", -1),
            shifted(to_upper_x, "sx", 1),
            shifted(to_lower_x, "sx", -1),
            own_rows(own_left, right, MEMBERS),
            behind,
            ahead,
        )
    )
    return gathered_rows(halves, grid_y, count_y)[None]


def solution(mesh):
    return jax.shard_map(
        local,
        mesh=mesh,
        in_specs=(
            P("sx", "sy", None, None, None, None),
            P("sx", "sy", None, None),
            P("sx", "sy", None, None, None),
            P("sx", "sy", None, None, None),
            P(),
        ),
        out_specs=P("sx", None, None, None, None, None, None),
        check_vma=False,
    )
```

```python
import functools

import jax
import jax.numpy as jnp
from jax import lax
from jax.experimental import pallas as pl
from jax.experimental.pallas import tpu as pltpu
from jax.sharding import PartitionSpec as P

CROSS_SHIFTS = ((0, -1), (0, 1), (-1, 0), (1, 0), (0, 0))
OWN = 4
DOWN, UP = CROSS_SHIFTS[:2]
HALO_ORDER = (2, 0, 1, 3)
WINDOW_SHIFTS = (
    (-2, 0),
    (-1, -1),
    (-1, 0),
    (-1, 1),
    (0, -2),
    (0, -1),
    (0, 0),
    (0, 1),
    (0, 2),
    (1, -1),
    (1, 0),
    (1, 1),
    (2, 0),
)
AHEAD, BEHIND = 4, 8
TRAVEL = (4, 1, 5, 9, 0, 2, 6, 10, 12, 3, 7, 11, 8)
HALVES = (TRAVEL[:6], TRAVEL[6:])
smoothing = 2.0 / 3.0
MEMBERS = 2
ROWS_PER_STEP = 4
ROWS_PER_CHUNK = 16
UNROLL = 8
NT = (((1,), (1,)), ((), ()))


def shifted(x, axis, by):
    length = lax.axis_size(axis)
    pairs = [(i, i + by) for i in range(length) if 0 <= i + by < length]
    return lax.ppermute(x, axis, pairs)


def lane_tiles(g, tile):
    return pl.ds(pl.multiple_of(g * tile, tile), tile)


def own_kernel(count_y, rows, members, taps, columns, agg, place, a_ref, dinv_ref, tent, *refs):
    right, left, tiles, sources, slots, ends, found = refs[:7]
    sums = refs[7:]
    tile = a_ref.shape[-1]
    step = pl.program_id(0)

    @pl.when(step == 0)
    def _():
        found[0] = 0

    listed = found[0]
    for u in range(ROWS_PER_STEP):
        g = step * ROWS_PER_STEP + u
        total = sums[u]
        total[...] = jnp.zeros_like(total)
        own_member = 0
        for k in range(taps):
            target = columns[g * taps + k]
            holder = target // rows
            step_x = holder // count_y - place[0]
            step_y = holder % count_y - place[1]
            direction = jnp.where(
                step_y == -1,
                0,
                jnp.where(step_y == 1, 1, jnp.where(step_x == -1, 2, jnp.where(step_x == 1, 3, OWN))),
            )
            member = agg[target] % members
            if k == 0:
                own_member = member
            else:
                tiles[listed] = g * taps + k
                sources[listed] = direction * rows + target % rows
                slots[listed] = direction * members + member
                listed += jnp.where(direction == OWN, 0, 1)
            z = lax.dot_general(
                tent[target % rows], a_ref[u, k], NT, preferred_element_type=jnp.float32
            )
            slot = jnp.where(direction == OWN, member, members)
            total[lane_tiles(slot, tile), :] += z.astype(jnp.bfloat16).astype(jnp.float32)
        here = slice(u * tile, (u + 1) * tile)
        applied = total[: members * tile, :].astype(jnp.bfloat16)
        right[:, here] = applied
        smooth = lax.dot_general(applied, dinv_ref[u], NT, preferred_element_type=jnp.float32)
        total[: members * tile, :] = -smoothing * smooth
        total[lane_tiles(own_member, tile), :] += tent[g].astype(jnp.float32)
        left[:, here] = total[: members * tile, :].astype(jnp.bfloat16)
    found[0] = listed
    ends[step] = listed


def own_slots(a_tiles, columns, dinv, tent, agg, place, count_y, members):
    rows, taps, tile = a_tiles.shape[0], a_tiles.shape[1], a_tiles.shape[-1]
    steps = rows // ROWS_PER_STEP
    span = ROWS_PER_STEP * tile
    scalars = pl.BlockSpec(memory_space=pltpu.SMEM)
    return pl.pallas_call(
        functools.partial(own_kernel, count_y, rows, members, taps),
        grid_spec=pltpu.PrefetchScalarGridSpec(
            num_scalar_prefetch=3,
            grid=(steps,),
            in_specs=[
                pl.BlockSpec((ROWS_PER_STEP, taps, tile, tile), lambda s, *_: (s, 0, 0, 0)),
                pl.BlockSpec((ROWS_PER_STEP, tile, tile), lambda s, *_: (s, 0, 0)),
                pl.BlockSpec((rows, tile, tile), lambda s, *_: (0, 0, 0)),
            ],
            out_specs=[pl.BlockSpec((members * tile, span), lambda s, *_: (0, s))] * 2
            + [scalars] * 4,
            scratch_shapes=[pltpu.SMEM((1,), jnp.int32)]
            + [pltpu.VMEM(((members + 1) * tile, tile), jnp.float32)] * ROWS_PER_STEP,
        ),
        out_shape=[jax.ShapeDtypeStruct((members * tile, rows * tile), jnp.bfloat16)] * 2
        + [jax.ShapeDtypeStruct((rows * taps,), jnp.int32)] * 3
        + [jax.ShapeDtypeStruct((steps,), jnp.int32)],
        compiler_params=pltpu.CompilerParams(vmem_limit_bytes=44 * 1024 * 1024),
        cost_estimate=pl.CostEstimate(
            flops=2 * tile**3 * rows * (taps + members),
            bytes_accessed=2 * (a_tiles.size + dinv.size * 6),
            transcendentals=0,
        ),
        name="own_slots",
    )(columns, agg, place, a_tiles, dinv, tent)


def kept_members(shift):
    lone = CROSS_SHIFTS.index(shift)
    return tuple((lone + 1 + p) % 5 for p in range(4))


def product(left, right, outs, lone, members, tile):
    value = lax.dot_general(left, right, NT, preferred_element_type=jnp.float32)
    for d1, out in enumerate(outs):
        for d2 in range(5):
            target, at = out, d2
            if d1 in lone:
                direction, single = lone[d1]
                target, at = (single, 0) if d2 == direction else (out, (d2 + 4 - direction) % 5)
            for m in range(members):
                for m2 in range(members):
                    row, column = (d1 * members + m) * tile, (d2 * members + m2) * tile
                    block = value[row : row + tile, column : column + tile]
                    target[at, m, m2] = block.astype(target.dtype)


def partial_kernel(members, taps, tiles, sources, slots, ends, *refs):
    a_tiles, dinv_hbm, *tents = refs[:6]
    right_own, *outs, behind, ahead, right_out = refs[6:14]
    a_held, dinv, tent, right, left, held, sems = refs[14:]
    tile = dinv.shape[-1]
    rows = dinv.shape[0]
    chunks = rows // ROWS_PER_CHUNK
    outer = 4 * members
    per = ROWS_PER_CHUNK * taps
    depth = rows * tile

    def a_copy(c):
        part = pl.ds(c * per, per)
        return pltpu.make_async_copy(a_tiles.at[part], a_held.at[part], sems.at[c])

    tent_copies = [
        pltpu.make_async_copy(source, tent.at[pl.ds(d * rows, rows)], sems.at[chunks + d])
        for d, source in zip(HALO_ORDER, tents)
    ]
    dinv_copy = pltpu.make_async_copy(dinv_hbm, dinv, sems.at[chunks + 4])
    own_part = (pl.ds(outer * tile, members * tile), pl.ds(0, depth))
    own_copy = pltpu.make_async_copy(right_own, right.at[own_part], sems.at[chunks + 5])
    out_copy = pltpu.make_async_copy(
        right.at[:, pl.ds(0, depth)], right_out, sems.at[chunks + 6]
    )
    for copy in tent_copies:
        copy.start()
    a_copy(0).start()
    dinv_copy.start()
    right[: outer * tile, :] = jnp.zeros((outer * tile, right.shape[1]), right.dtype)
    left[...] = jnp.zeros_like(left)
    held[...] = jnp.zeros_like(held)
    for copy in tent_copies:
        copy.wait()
    for c in range(1, chunks):
        a_copy(c).start()
    own_copy.start()
    dinv_copy.wait()

    def one_chunk(c, first):
        a_copy(c).wait()
        last = ends[(c + 1) * (ROWS_PER_CHUNK // ROWS_PER_STEP) - 1]
        batches = (last - first + UNROLL - 1) // UNROLL

        def entry(at):
            index = jnp.clip(at, first, last - 1)
            row = tiles[index] // taps
            lanes = lane_tiles(jnp.where((at >= first) & (at < last), row, rows), tile)
            return index, row, (lane_tiles(slots[index], tile), lanes)

        def some(n, carry):
            fresh, older = [], []
            for u in range(UNROLL):
                index, _, at = entry(first + UNROLL * n + u)
                z = lax.dot_general(
                    tent[sources[index]],
                    a_held[tiles[index]],
                    NT,
                    preferred_element_type=jnp.float32,
                ).astype(jnp.bfloat16)
                fresh.append((at, z))
                _, row, at = entry(first + UNROLL * (n - 1) + u)
                smooth = lax.dot_general(
                    held[(n + 1) % 2, u], dinv[row], NT, preferred_element_type=jnp.float32
                )
                older.append((at, smooth))
            for u, ((at, z), (old_at, smooth)) in enumerate(zip(fresh, older)):
                held[n % 2, u] = z
                right[at] = (right[at].astype(jnp.float32) + z.astype(jnp.float32)).astype(
                    jnp.bfloat16
                )
                left[old_at] = (left[old_at].astype(jnp.float32) - smoothing * smooth).astype(
                    jnp.bfloat16
                )
            return carry

        lax.fori_loop(0, jnp.where(batches > 0, batches + 1, 0), some, 0)
        return last

    lax.fori_loop(0, chunks, one_chunk, 0)
    own_copy.wait()
    out_copy.start()
    lone = {d: (CROSS_SHIFTS.index(t), out) for d, t, out in ((0, UP, behind), (1, DOWN, ahead))}
    product(left[:, :depth], right[:, :depth], outs, lone, members, tile)
    out_copy.wait()


def partial_blocks(a_tiles, dinv, tents, own_right, lists, members):
    rows, taps, tile = a_tiles.shape[0], a_tiles.shape[1], a_tiles.shape[-1]
    whole = lambda lead: pl.BlockSpec((lead, members, members, tile, tile), lambda s, *_: (0,) * 5)
    leads = (4, 4, 5, 5, 1, 1)
    outer = 4 * members * tile
    slots = outer + members * tile
    return pl.pallas_call(
        functools.partial(partial_kernel, members, taps),
        grid_spec=pltpu.PrefetchScalarGridSpec(
            num_scalar_prefetch=4,
            grid=(1,),
            in_specs=[pl.BlockSpec(memory_space=pl.ANY)] * 7,
            out_specs=[whole(lead) for lead in leads] + [pl.BlockSpec(memory_space=pl.ANY)],
            scratch_shapes=[
                pltpu.VMEM((rows * taps, tile, tile), jnp.bfloat16),
                pltpu.VMEM((rows, tile, tile), jnp.bfloat16),
                pltpu.VMEM((4 * rows, tile, tile), jnp.bfloat16),
                pltpu.VMEM((slots, (rows + 1) * tile), jnp.bfloat16),
                pltpu.VMEM((outer, (rows + 1) * tile), jnp.bfloat16),
                pltpu.VMEM((2, UNROLL, tile, tile), jnp.bfloat16),
                pltpu.SemaphoreType.DMA((rows // ROWS_PER_CHUNK + 7,)),
            ],
        ),
        out_shape=[
            jax.ShapeDtypeStruct((lead, members, members, tile, tile), jnp.bfloat16)
            for lead in leads
        ]
        + [jax.ShapeDtypeStruct((slots, rows * tile), jnp.bfloat16)],
        compiler_params=pltpu.CompilerParams(vmem_limit_bytes=48 * 1024 * 1024),
        cost_estimate=pl.CostEstimate(
            flops=2 * tile**3 * rows * (taps + 20 * members * members),
            bytes_accessed=2 * (a_tiles.size + 20 * dinv.size),
            transcendentals=0,
        ),
        name="partial_blocks",
    )(*lists, a_tiles.reshape(rows * taps, tile, tile), dinv, *tents, own_right)


def own_rows_kernel(members, left_own, right_all, own, left, right, sems):
    copies = [
        pltpu.make_async_copy(left_own, left, sems.at[0]),
        pltpu.make_async_copy(right_all, right, sems.at[1]),
    ]
    for copy in copies:
        copy.start()
    for copy in copies:
        copy.wait()
    product(left[...], right[...], (own,), {}, members, own.shape[-1])


def own_rows(left, right, members):
    tile = left.shape[0] // members
    block = (5, members, members, tile, tile)
    return pl.pallas_call(
        functools.partial(own_rows_kernel, members),
        grid=(1,),
        in_specs=[pl.BlockSpec(memory_space=pl.ANY)] * 2,
        out_specs=pl.BlockSpec(block, lambda s: (0,) * 5),
        out_shape=jax.ShapeDtypeStruct(block, jnp.float32),
        scratch_shapes=[
            pltpu.VMEM(left.shape, left.dtype),
            pltpu.VMEM(right.shape, right.dtype),
            pltpu.SemaphoreType.DMA((2,)),
        ],
        compiler_params=pltpu.CompilerParams(vmem_limit_bytes=32 * 1024 * 1024),
        cost_estimate=pl.CostEstimate(
            flops=2 * left.size * right.shape[0],
            bytes_accessed=2 * (left.size + right.size),
            transcendentals=0,
        ),
        name="own_rows",
    )(left, right)


def window_kernel(*refs):
    every = tuple(range(5))
    held = (kept_members(DOWN), kept_members(UP), every, every, every)
    behind, ahead = refs[5:7]
    for out, half in zip(refs[7:], HALVES):
        for position, offset in enumerate(half):
            if offset in (AHEAD, BEHIND):
                out[position] = (ahead if offset == AHEAD else behind)[0]
                continue
            total = None
            for shift, values, directions in zip(CROSS_SHIFTS, refs, held):
                for d, direction in enumerate(directions):
                    member = CROSS_SHIFTS[direction]
                    if (shift[0] + member[0], shift[1] + member[1]) == WINDOW_SHIFTS[offset]:
                        term = values[d].astype(jnp.float32)
                        total = term if total is None else total + term
            out[position] = total.astype(out.dtype)


def finished_window(blocks):
    _, members, _, tile, _ = blocks[0].shape
    spec = lambda lead: pl.BlockSpec(
        (lead, 1, members, tile, tile), lambda m: (0, m, 0, 0, 0)
    )
    return pl.pallas_call(
        window_kernel,
        grid=(members,),
        in_specs=[spec(block.shape[0]) for block in blocks],
        out_specs=[spec(len(half)) for half in HALVES],
        out_shape=[
            jax.ShapeDtypeStruct((len(half), members, members, tile, tile), jnp.bfloat16)
            for half in HALVES
        ],
        compiler_params=pltpu.CompilerParams(vmem_limit_bytes=32 * 1024 * 1024),
        cost_estimate=pl.CostEstimate(
            flops=5 * blocks[4].size, bytes_accessed=16 * blocks[4].size, transcendentals=0
        ),
        name="finished_window",
    )(*blocks)


def place_kernel(lists, edges, row, valid, *refs):
    arrays, (out, nothing, sems) = refs[: len(lists)], refs[-3:]
    count = out.shape[0]
    nothing[...] = jnp.zeros_like(nothing)

    def each(act):
        def move(source, target, offset, sem):
            act(pltpu.make_async_copy(source, out.at[target, :, offset], sems.at[sem]))

        for index, (array, (held, written)) in enumerate(zip(arrays, lists)):

            def write(offset, target):
                source = array.at[held.index(offset)] if offset in held else nothing
                move(source, target, offset, index * 13 + offset)

            here = row[index]

            @pl.when(valid[index] == 1)
            def _():
                for offset in written:
                    if offset not in (AHEAD, BEHIND):
                        write(offset, here)

            if AHEAD in written:

                @pl.when((valid[index] == 1) & (here + 1 < count))
                def _():
                    write(AHEAD, here + 1)

            if BEHIND in written:

                @pl.when((valid[index] == 1) & (here > 0))
                def _():
                    write(BEHIND, here - 1)

        if edges:
            move(nothing, 0, AHEAD, 13 * len(lists))
            move(nothing, count - 1, BEHIND, 13 * len(lists) + 1)

    each(lambda copy: copy.start())
    each(lambda copy: copy.wait())


def placed(out, pieces, count):
    arrays = [piece[0] for piece in pieces]
    members, _, tile, _ = arrays[0].shape[1:]
    scalars = pl.BlockSpec(memory_space=pltpu.SMEM)
    in_specs = [scalars] * 2 + [pl.BlockSpec(memory_space=pltpu.VMEM)] * len(arrays)
    operands = list(arrays)
    if out is not None:
        in_specs.append(pl.BlockSpec(memory_space=pl.ANY))
        operands.append(out)
    rows = jnp.stack([jnp.asarray(jnp.where(p[4], p[3], 0), jnp.int32) for p in pieces])
    valid = jnp.stack([jnp.asarray(p[4], jnp.int32) for p in pieces])
    return pl.pallas_call(
        functools.partial(place_kernel, tuple(p[1:3] for p in pieces), out is None),
        in_specs=in_specs,
        out_specs=pl.BlockSpec(memory_space=pl.ANY),
        scratch_shapes=[
            pltpu.VMEM((members, members, tile, tile), jnp.bfloat16),
            pltpu.SemaphoreType.DMA((len(pieces) * 13 + 2,)),
        ],
        out_shape=jax.ShapeDtypeStruct(
            (count, members, 13, members, tile, tile), jnp.bfloat16
        ),
        input_output_aliases={2 + len(arrays): 0} if out is not None else {},
        compiler_params=pltpu.CompilerParams(vmem_limit_bytes=24 * 1024 * 1024),
        cost_estimate=pl.CostEstimate(
            flops=0, bytes_accessed=6 * 13 * members * members * tile * tile, transcendentals=0
        ),
        name="placed",
    )(rows, valid, *operands)


def end_to_end(halves, grid_y, count_y):
    lower = tuple(o for o in TRAVEL if WINDOW_SHIFTS[o][1] in (0, 1))
    upper = tuple(o for o in TRAVEL if WINDOW_SHIFTS[o][1] in (-1, 0))
    start = jnp.where(grid_y == 0, TRAVEL.index(lower[0]), TRAVEL.index(upper[0]))
    sent = lax.dynamic_slice_in_dim(jnp.concatenate(halves, axis=0), start, len(lower), axis=0)
    last = count_y - 1
    moved = lax.ppermute(sent, "sy", [(0, last), (last, 0)])
    return [
        (moved, lower, TRAVEL, 0, grid_y == last),
        (moved, upper, TRAVEL, last, grid_y == 0),
    ]


def gathered_rows(halves, grid_y, count_y):
    chains = [(half, half) for half in halves]
    pieces = [(half, group, group, grid_y, True) for half, group in zip(halves, HALVES)]
    out = None
    for hop in range(1, count_y - 1):
        chains = [(shifted(a, "sy", 1), shifted(b, "sy", -1)) for a, b in chains]
        if hop == 1:
            direct = end_to_end(halves, grid_y, count_y)
        out = placed(out, pieces, count_y)
        if hop == 1:
            chains[1], out = lax.optimization_barrier((chains[1], out))
        pieces = []
        for (from_lower, from_upper), group in zip(chains, HALVES):
            pieces += [
                (from_lower, group, group, grid_y - hop, grid_y >= hop),
                (from_upper, group, group, grid_y + hop, grid_y + hop < count_y),
            ]
    out = placed(out, direct + pieces[2:], count_y)
    return placed(out, pieces[:2], count_y)


def local(a_tiles, columns, ptent, dinv, agg):
    grid_x = lax.axis_index("sx")
    grid_y = lax.axis_index("sy")
    count_y = lax.axis_size("sy")
    rows, taps, tile = a_tiles.shape[2], a_tiles.shape[3], a_tiles.shape[-1]
    coupling = a_tiles.reshape(rows, taps, tile, tile)
    inverse = dinv.reshape(rows, tile, tile)
    tent = jnp.swapaxes(ptent.reshape(rows, tile, tile), 1, 2)
    tents = (
        shifted(tent, "sx", 1),
        shifted(tent, "sy", 1),
        shifted(tent, "sy", -1),
        shifted(tent, "sx", -1),
    )
    own_right, own_left, *lists = own_slots(
        coupling,
        columns.reshape(rows * taps),
        inverse,
        tent,
        agg,
        jnp.stack([grid_x, grid_y]).astype(jnp.int32),
        count_y,
        MEMBERS,
    )
    to_lower_y, to_upper_y, to_lower_x, to_upper_x, behind, ahead, right = partial_blocks(
        coupling, inverse, tents, own_right, lists, MEMBERS
    )
    halves = finished_window(
        (
            shifted(to_upper_y, "sy", 1),
            shifted(to_lower_y, "sy", -1),
            shifted(to_upper_x, "sx", 1),
            shifted(to_lower_x, "sx", -1),
            own_rows(own_left, right, MEMBERS),
            behind,
            ahead,
        )
    )
    return gathered_rows(halves, grid_y, count_y)[None]


def solution(mesh):
    return jax.shard_map(
        local,
        mesh=mesh,
        in_specs=(
            P("sx", "sy", None, None, None, None),
            P("sx", "sy", None, None),
            P("sx", "sy", None, None, None),
            P("sx", "sy", None, None, None),
            P(),
        ),
        out_specs=P("sx", None, None, None, None, None, None),
        check_vma=False,
    )
```

```python
import functools

import jax
import jax.numpy as jnp
from jax import lax
from jax.experimental import pallas as pl
from jax.experimental.pallas import tpu as pltpu
from jax.sharding import PartitionSpec as P

CROSS_SHIFTS = ((0, -1), (0, 1), (-1, 0), (1, 0), (0, 0))
OWN = 4
DOWN, UP = CROSS_SHIFTS[:2]
HALO_ORDER = (2, 0, 1, 3)
WINDOW_SHIFTS = (
    (-2, 0),
    (-1, -1),
    (-1, 0),
    (-1, 1),
    (0, -2),
    (0, -1),
    (0, 0),
    (0, 1),
    (0, 2),
    (1, -1),
    (1, 0),
    (1, 1),
    (2, 0),
)
AHEAD, BEHIND = 4, 8
TRAVEL = (4, 1, 5, 9, 0, 2, 6, 10, 12, 3, 7, 11, 8)
HALVES = (TRAVEL[:6], TRAVEL[6:])
smoothing = 2.0 / 3.0
MEMBERS = 2
ROWS_PER_STEP = 4
UNROLL = 8
NT = (((1,), (1,)), ((), ()))


def shifted(x, axis, by):
    length = lax.axis_size(axis)
    pairs = [(i, i + by) for i in range(length) if 0 <= i + by < length]
    return lax.ppermute(x, axis, pairs)


def lane_tiles(g, tile):
    return pl.ds(pl.multiple_of(g * tile, tile), tile)


def own_kernel(count_y, rows, members, taps, columns, agg, place, a_ref, dinv_ref, tent, *refs):
    right, left, tiles, sources, slots, ends, found = refs[:7]
    sums = refs[7:]
    tile = a_ref.shape[-1]
    step = pl.program_id(0)

    @pl.when(step == 0)
    def _():
        found[0] = 0

    listed = found[0]
    for u in range(ROWS_PER_STEP):
        g = step * ROWS_PER_STEP + u
        total = sums[u]
        total[...] = jnp.zeros_like(total)
        own_member = 0
        for k in range(taps):
            target = columns[g * taps + k]
            holder = target // rows
            step_x = holder // count_y - place[0]
            step_y = holder % count_y - place[1]
            direction = jnp.where(
                step_y == -1,
                0,
                jnp.where(step_y == 1, 1, jnp.where(step_x == -1, 2, jnp.where(step_x == 1, 3, OWN))),
            )
            member = agg[target] % members
            if k == 0:
                own_member = member
            else:
                tiles[listed] = g * taps + k
                sources[listed] = direction * rows + target % rows
                slots[listed] = direction * members + member
                listed += jnp.where(direction == OWN, 0, 1)
            z = lax.dot_general(
                tent[target % rows], a_ref[u, k], NT, preferred_element_type=jnp.float32
            )
            slot = jnp.where(direction == OWN, member, members)
            total[lane_tiles(slot, tile), :] += z.astype(jnp.bfloat16).astype(jnp.float32)
        here = slice(u * tile, (u + 1) * tile)
        applied = total[: members * tile, :].astype(jnp.bfloat16)
        right[:, here] = applied
        smooth = lax.dot_general(applied, dinv_ref[u], NT, preferred_element_type=jnp.float32)
        total[: members * tile, :] = -smoothing * smooth
        total[lane_tiles(own_member, tile), :] += tent[g].astype(jnp.float32)
        left[:, here] = total[: members * tile, :].astype(jnp.bfloat16)
    found[0] = listed
    ends[step] = listed


def own_slots(a_tiles, columns, dinv, tent, agg, place, count_y, members):
    rows, taps, tile = a_tiles.shape[0], a_tiles.shape[1], a_tiles.shape[-1]
    steps = rows // ROWS_PER_STEP
    span = ROWS_PER_STEP * tile
    scalars = pl.BlockSpec(memory_space=pltpu.SMEM)
    return pl.pallas_call(
        functools.partial(own_kernel, count_y, rows, members, taps),
        grid_spec=pltpu.PrefetchScalarGridSpec(
            num_scalar_prefetch=3,
            grid=(steps,),
            in_specs=[
                pl.BlockSpec((ROWS_PER_STEP, taps, tile, tile), lambda s, *_: (s, 0, 0, 0)),
                pl.BlockSpec((ROWS_PER_STEP, tile, tile), lambda s, *_: (s, 0, 0)),
                pl.BlockSpec((rows, tile, tile), lambda s, *_: (0, 0, 0)),
            ],
            out_specs=[pl.BlockSpec((members * tile, span), lambda s, *_: (0, s))] * 2
            + [scalars] * 4,
            scratch_shapes=[pltpu.SMEM((1,), jnp.int32)]
            + [pltpu.VMEM(((members + 1) * tile, tile), jnp.float32)] * ROWS_PER_STEP,
        ),
        out_shape=[jax.ShapeDtypeStruct((members * tile, rows * tile), jnp.bfloat16)] * 2
        + [jax.ShapeDtypeStruct((rows * taps,), jnp.int32)] * 3
        + [jax.ShapeDtypeStruct((steps,), jnp.int32)],
        compiler_params=pltpu.CompilerParams(vmem_limit_bytes=24 * 1024 * 1024),
        cost_estimate=pl.CostEstimate(
            flops=2 * tile**3 * rows * (taps + members),
            bytes_accessed=2 * (a_tiles.size + dinv.size * 6),
            transcendentals=0,
        ),
        name="own_slots",
    )(columns, agg, place, a_tiles, dinv, tent)


def kept_members(shift):
    lone = CROSS_SHIFTS.index(shift)
    return tuple((lone + 1 + p) % 5 for p in range(4))


def product(left, right, outs, lone, members, tile):
    value = lax.dot_general(left, right, NT, preferred_element_type=jnp.float32)
    for d1, out in enumerate(outs):
        for d2 in range(5):
            target, at = out, d2
            if d1 in lone:
                direction, single = lone[d1]
                target, at = (single, 0) if d2 == direction else (out, (d2 + 4 - direction) % 5)
            for m in range(members):
                for m2 in range(members):
                    row, column = (d1 * members + m) * tile, (d2 * members + m2) * tile
                    block = value[row : row + tile, column : column + tile]
                    target[at, m, m2] = block.astype(target.dtype)


def partial_kernel(members, taps, tiles, sources, slots, ends, *refs):
    a_tiles, dinv, *tents = refs[:6]
    right_own, *outs, behind, ahead, right_out = refs[6:14]
    tent, right, left, held, sems = refs[14:]
    tile = dinv.shape[-1]
    rows = dinv.shape[0]
    outer = 4 * members
    depth = rows * tile

    copies = [
        pltpu.make_async_copy(source, tent.at[pl.ds(d * rows, rows)], sems.at[d])
        for d, source in zip(HALO_ORDER, tents)
    ]
    own_part = (pl.ds(outer * tile, members * tile), pl.ds(0, depth))
    own_copy = pltpu.make_async_copy(right_own, right.at[own_part], sems.at[4])
    out_copy = pltpu.make_async_copy(right.at[:, pl.ds(0, depth)], right_out, sems.at[5])
    for copy in copies:
        copy.start()
    own_copy.start()
    right[: outer * tile, :] = jnp.zeros((outer * tile, right.shape[1]), right.dtype)
    left[...] = jnp.zeros_like(left)
    held[...] = jnp.zeros_like(held)
    for copy in copies:
        copy.wait()

    last = ends[rows // ROWS_PER_STEP - 1]
    batches = (last + UNROLL - 1) // UNROLL

    def entry(at):
        index = jnp.clip(at, 0, last - 1)
        row = tiles[index] // taps
        lanes = lane_tiles(jnp.where((at >= 0) & (at < last), row, rows), tile)
        return index, row, (lane_tiles(slots[index], tile), lanes)

    def some(n, carry):
        fresh, older = [], []
        for u in range(UNROLL):
            index, _, at = entry(UNROLL * n + u)
            z = lax.dot_general(
                tent[sources[index]],
                a_tiles[tiles[index]],
                NT,
                preferred_element_type=jnp.float32,
            ).astype(jnp.bfloat16)
            fresh.append((at, z))
            _, row, at = entry(UNROLL * (n - 1) + u)
            smooth = lax.dot_general(
                held[(n + 1) % 2, u], dinv[row], NT, preferred_element_type=jnp.float32
            )
            older.append((at, smooth))
        for u, ((at, z), (old_at, smooth)) in enumerate(zip(fresh, older)):
            held[n % 2, u] = z
            right[at] = (right[at].astype(jnp.float32) + z.astype(jnp.float32)).astype(
                jnp.bfloat16
            )
            left[old_at] = (left[old_at].astype(jnp.float32) - smoothing * smooth).astype(
                jnp.bfloat16
            )
        return carry

    lax.fori_loop(0, jnp.where(batches > 0, batches + 1, 0), some, 0)
    own_copy.wait()
    out_copy.start()
    lone = {d: (CROSS_SHIFTS.index(t), out) for d, t, out in ((0, UP, behind), (1, DOWN, ahead))}
    product(left[:, :depth], right[:, :depth], outs, lone, members, tile)
    out_copy.wait()


def partial_blocks(a_tiles, dinv, tents, own_right, lists, members):
    rows, taps, tile = a_tiles.shape[0], a_tiles.shape[1], a_tiles.shape[-1]
    leads = (4, 4, 5, 5, 1, 1)
    outer = 4 * members * tile
    slots = outer + members * tile
    scalars, inside, anywhere = (
        pl.BlockSpec(memory_space=space) for space in (pltpu.SMEM, pltpu.VMEM, pl.ANY)
    )
    return pl.pallas_call(
        functools.partial(partial_kernel, members, taps),
        in_specs=[scalars] * 4 + [inside] * 6 + [anywhere],
        out_specs=[inside] * 6 + [anywhere],
        scratch_shapes=[
            pltpu.VMEM((4 * rows, tile, tile), jnp.bfloat16),
            pltpu.VMEM((slots, (rows + 1) * tile), jnp.bfloat16),
            pltpu.VMEM((outer, (rows + 1) * tile), jnp.bfloat16),
            pltpu.VMEM((2, UNROLL, tile, tile), jnp.bfloat16),
            pltpu.SemaphoreType.DMA((6,)),
        ],
        out_shape=[
            jax.ShapeDtypeStruct((lead, members, members, tile, tile), jnp.bfloat16)
            for lead in leads
        ]
        + [jax.ShapeDtypeStruct((slots, rows * tile), jnp.bfloat16)],
        compiler_params=pltpu.CompilerParams(vmem_limit_bytes=36 * 1024 * 1024),
        cost_estimate=pl.CostEstimate(
            flops=2 * tile**3 * rows * (taps + 20 * members * members),
            bytes_accessed=2 * (a_tiles.size + 20 * dinv.size),
            transcendentals=0,
        ),
        name="partial_blocks",
    )(*lists, a_tiles.reshape(rows * taps, tile, tile), dinv, *tents, own_right)


def own_rows_kernel(members, left_own, right_all, own, left, right, sems):
    copies = [
        pltpu.make_async_copy(left_own, left, sems.at[0]),
        pltpu.make_async_copy(right_all, right, sems.at[1]),
    ]
    for copy in copies:
        copy.start()
    for copy in copies:
        copy.wait()
    product(left[...], right[...], (own,), {}, members, own.shape[-1])


def own_rows(left, right, members):
    tile = left.shape[0] // members
    block = (5, members, members, tile, tile)
    return pl.pallas_call(
        functools.partial(own_rows_kernel, members),
        grid=(1,),
        in_specs=[pl.BlockSpec(memory_space=pl.ANY)] * 2,
        out_specs=pl.BlockSpec(block, lambda s: (0,) * 5),
        out_shape=jax.ShapeDtypeStruct(block, jnp.float32),
        scratch_shapes=[
            pltpu.VMEM(left.shape, left.dtype),
            pltpu.VMEM(right.shape, right.dtype),
            pltpu.SemaphoreType.DMA((2,)),
        ],
        compiler_params=pltpu.CompilerParams(vmem_limit_bytes=32 * 1024 * 1024),
        cost_estimate=pl.CostEstimate(
            flops=2 * left.size * right.shape[0],
            bytes_accessed=2 * (left.size + right.size),
            transcendentals=0,
        ),
        name="own_rows",
    )(left, right)


def window_kernel(*refs):
    every = tuple(range(5))
    held = (kept_members(DOWN), kept_members(UP), every, every, every)
    behind, ahead = refs[5:7]
    for out, half in zip(refs[7:], HALVES):
        for position, offset in enumerate(half):
            if offset in (AHEAD, BEHIND):
                out[position] = (ahead if offset == AHEAD else behind)[0]
                continue
            total = None
            for shift, values, directions in zip(CROSS_SHIFTS, refs, held):
                for d, direction in enumerate(directions):
                    member = CROSS_SHIFTS[direction]
                    if (shift[0] + member[0], shift[1] + member[1]) == WINDOW_SHIFTS[offset]:
                        term = values[d].astype(jnp.float32)
                        total = term if total is None else total + term
            out[position] = total.astype(out.dtype)


def finished_window(blocks):
    _, members, _, tile, _ = blocks[0].shape
    spec = lambda lead: pl.BlockSpec(
        (lead, 1, members, tile, tile), lambda m: (0, m, 0, 0, 0)
    )
    return pl.pallas_call(
        window_kernel,
        grid=(members,),
        in_specs=[spec(block.shape[0]) for block in blocks],
        out_specs=[spec(len(half)) for half in HALVES],
        out_shape=[
            jax.ShapeDtypeStruct((len(half), members, members, tile, tile), jnp.bfloat16)
            for half in HALVES
        ],
        compiler_params=pltpu.CompilerParams(vmem_limit_bytes=32 * 1024 * 1024),
        cost_estimate=pl.CostEstimate(
            flops=5 * blocks[4].size, bytes_accessed=16 * blocks[4].size, transcendentals=0
        ),
        name="finished_window",
    )(*blocks)


def place_kernel(lists, edges, row, valid, *refs):
    arrays, (out, nothing, sems) = refs[: len(lists)], refs[-3:]
    count = out.shape[0]
    nothing[...] = jnp.zeros_like(nothing)

    def each(act):
        def move(source, target, offset, sem):
            act(pltpu.make_async_copy(source, out.at[target, :, offset], sems.at[sem]))

        for index, (array, (held, written)) in enumerate(zip(arrays, lists)):

            def write(offset, target):
                source = array.at[held.index(offset)] if offset in held else nothing
                move(source, target, offset, index * 13 + offset)

            here = row[index]

            @pl.when(valid[index] == 1)
            def _():
                for offset in written:
                    if offset not in (AHEAD, BEHIND):
                        write(offset, here)

            if AHEAD in written:

                @pl.when((valid[index] == 1) & (here + 1 < count))
                def _():
                    write(AHEAD, here + 1)

            if BEHIND in written:

                @pl.when((valid[index] == 1) & (here > 0))
                def _():
                    write(BEHIND, here - 1)

        if edges:
            move(nothing, 0, AHEAD, 13 * len(lists))
            move(nothing, count - 1, BEHIND, 13 * len(lists) + 1)

    each(lambda copy: copy.start())
    each(lambda copy: copy.wait())


def placed(out, pieces, count):
    arrays = [piece[0] for piece in pieces]
    members, _, tile, _ = arrays[0].shape[1:]
    scalars = pl.BlockSpec(memory_space=pltpu.SMEM)
    in_specs = [scalars] * 2 + [pl.BlockSpec(memory_space=pltpu.VMEM)] * len(arrays)
    operands = list(arrays)
    if out is not None:
        in_specs.append(pl.BlockSpec(memory_space=pl.ANY))
        operands.append(out)
    rows = jnp.stack([jnp.asarray(jnp.where(p[4], p[3], 0), jnp.int32) for p in pieces])
    valid = jnp.stack([jnp.asarray(p[4], jnp.int32) for p in pieces])
    return pl.pallas_call(
        functools.partial(place_kernel, tuple(p[1:3] for p in pieces), out is None),
        in_specs=in_specs,
        out_specs=pl.BlockSpec(memory_space=pl.ANY),
        scratch_shapes=[
            pltpu.VMEM((members, members, tile, tile), jnp.bfloat16),
            pltpu.SemaphoreType.DMA((len(pieces) * 13 + 2,)),
        ],
        out_shape=jax.ShapeDtypeStruct(
            (count, members, 13, members, tile, tile), jnp.bfloat16
        ),
        input_output_aliases={2 + len(arrays): 0} if out is not None else {},
        compiler_params=pltpu.CompilerParams(vmem_limit_bytes=24 * 1024 * 1024),
        cost_estimate=pl.CostEstimate(
            flops=0, bytes_accessed=6 * 13 * members * members * tile * tile, transcendentals=0
        ),
        name="placed",
    )(rows, valid, *operands)


def end_to_end(halves, grid_y, count_y):
    lower = tuple(o for o in TRAVEL if WINDOW_SHIFTS[o][1] in (0, 1))
    upper = tuple(o for o in TRAVEL if WINDOW_SHIFTS[o][1] in (-1, 0))
    start = jnp.where(grid_y == 0, TRAVEL.index(lower[0]), TRAVEL.index(upper[0]))
    sent = lax.dynamic_slice_in_dim(jnp.concatenate(halves, axis=0), start, len(lower), axis=0)
    last = count_y - 1
    moved = lax.ppermute(sent, "sy", [(0, last), (last, 0)])
    return [
        (moved, lower, TRAVEL, 0, grid_y == last),
        (moved, upper, TRAVEL, last, grid_y == 0),
    ]


def gathered_rows(halves, grid_y, count_y):
    chains = [(half, half) for half in halves]
    pieces = [(half, group, group, grid_y, True) for half, group in zip(halves, HALVES)]
    out = None
    for hop in range(1, count_y - 1):
        chains = [(shifted(a, "sy", 1), shifted(b, "sy", -1)) for a, b in chains]
        if hop == 1:
            direct = end_to_end(halves, grid_y, count_y)
        out = placed(out, pieces, count_y)
        if hop == 1:
            chains[1], out = lax.optimization_barrier((chains[1], out))
        pieces = []
        for (from_lower, from_upper), group in zip(chains, HALVES):
            pieces += [
                (from_lower, group, group, grid_y - hop, grid_y >= hop),
                (from_upper, group, group, grid_y + hop, grid_y + hop < count_y),
            ]
    out = placed(out, direct + pieces[2:], count_y)
    return placed(out, pieces[:2], count_y)


def local(a_tiles, columns, ptent, dinv, agg):
    grid_x = lax.axis_index("sx")
    grid_y = lax.axis_index("sy")
    count_y = lax.axis_size("sy")
    rows, taps, tile = a_tiles.shape[2], a_tiles.shape[3], a_tiles.shape[-1]
    coupling = a_tiles.reshape(rows, taps, tile, tile)
    inverse = dinv.reshape(rows, tile, tile)
    tent = jnp.swapaxes(ptent.reshape(rows, tile, tile), 1, 2)
    tents = (
        shifted(tent, "sx", 1),
        shifted(tent, "sy", 1),
        shifted(tent, "sy", -1),
        shifted(tent, "sx", -1),
    )
    own_right, own_left, *lists = own_slots(
        coupling,
        columns.reshape(rows * taps),
        inverse,
        tent,
        agg,
        jnp.stack([grid_x, grid_y]).astype(jnp.int32),
        count_y,
        MEMBERS,
    )
    to_lower_y, to_upper_y, to_lower_x, to_upper_x, behind, ahead, right = partial_blocks(
        coupling, inverse, tents, own_right, lists, MEMBERS
    )
    halves = finished_window(
        (
            shifted(to_upper_y, "sy", 1),
            shifted(to_lower_y, "sy", -1),
            shifted(to_upper_x, "sx", 1),
            shifted(to_lower_x, "sx", -1),
            own_rows(own_left, right, MEMBERS),
            behind,
            ahead,
        )
    )
    return gathered_rows(halves, grid_y, count_y)[None]


def solution(mesh):
    return jax.shard_map(
        local,
        mesh=mesh,
        in_specs=(
            P("sx", "sy", None, None, None, None),
            P("sx", "sy", None, None),
            P("sx", "sy", None, None, None),
            P("sx", "sy", None, None, None),
            P(),
        ),
        out_specs=P("sx", None, None, None, None, None, None),
        check_vma=False,
    )
```

```python
import functools

import jax
import jax.numpy as jnp
from jax import lax
from jax.experimental import pallas as pl
from jax.experimental.pallas import tpu as pltpu
from jax.sharding import PartitionSpec as P

CROSS_SHIFTS = ((0, -1), (0, 1), (-1, 0), (1, 0), (0, 0))
OWN = 4
DOWN, UP = CROSS_SHIFTS[:2]
HALO_ORDER = (0, 1, 3, 2)
WINDOW_SHIFTS = (
    (-2, 0),
    (-1, -1),
    (-1, 0),
    (-1, 1),
    (0, -2),
    (0, -1),
    (0, 0),
    (0, 1),
    (0, 2),
    (1, -1),
    (1, 0),
    (1, 1),
    (2, 0),
)
AHEAD, BEHIND = 4, 8
TRAVEL = (4, 1, 5, 9, 0, 2, 6, 10, 12, 3, 7, 11, 8)
HALVES = (TRAVEL[:6], TRAVEL[6:])
smoothing = 2.0 / 3.0
MEMBERS = 2
ROWS_PER_STEP = 4
UNROLL = 8
NT = (((1,), (1,)), ((), ()))


def shifted(x, axis, by):
    length = lax.axis_size(axis)
    pairs = [(i, i + by) for i in range(length) if 0 <= i + by < length]
    return lax.ppermute(x, axis, pairs)


def lane_tiles(g, tile):
    return pl.ds(pl.multiple_of(g * tile, tile), tile)


def swapped(x, axis, first):
    lows = range(first, lax.axis_size(axis) - 1, 2)
    return lax.ppermute(x, axis, [(i + a, i + 1 - a) for i in lows for a in (0, 1)])


def own_kernel(count_y, rows, members, taps, columns, agg, place, a_ref, dinv_ref, tent, *refs):
    right, left, tiles, sources, slots, ends, found = refs[:7]
    sums = refs[7:]
    tile = a_ref.shape[-1]
    step = pl.program_id(0)

    @pl.when(step == 0)
    def _():
        found[0] = 0

    listed = found[0]
    for u in range(ROWS_PER_STEP):
        g = step * ROWS_PER_STEP + u
        total = sums[u]
        total[...] = jnp.zeros_like(total)
        own_member = 0
        for k in range(taps):
            target = columns[g * taps + k]
            holder = target // rows
            step_x = holder // count_y - place[0]
            step_y = holder % count_y - place[1]
            direction = jnp.where(
                step_y == -1,
                0,
                jnp.where(step_y == 1, 1, jnp.where(step_x == -1, 2, jnp.where(step_x == 1, 3, OWN))),
            )
            member = agg[target] % members
            if k == 0:
                own_member = member
            else:
                tiles[listed] = g * taps + k
                seat = jnp.where(direction < 2, direction, 2 + (direction + place[0] + 1) % 2)
                sources[listed] = seat * rows + target % rows
                slots[listed] = direction * members + member
                listed += jnp.where(direction == OWN, 0, 1)
            z = lax.dot_general(
                tent[target % rows], a_ref[u, k], NT, preferred_element_type=jnp.float32
            )
            slot = jnp.where(direction == OWN, member, members)
            total[lane_tiles(slot, tile), :] += z.astype(jnp.bfloat16).astype(jnp.float32)
        here = slice(u * tile, (u + 1) * tile)
        applied = total[: members * tile, :].astype(jnp.bfloat16)
        right[:, here] = applied
        smooth = lax.dot_general(applied, dinv_ref[u], NT, preferred_element_type=jnp.float32)
        total[: members * tile, :] = -smoothing * smooth
        total[lane_tiles(own_member, tile), :] += tent[g].astype(jnp.float32)
        left[:, here] = total[: members * tile, :].astype(jnp.bfloat16)
    found[0] = listed
    ends[step] = listed


def own_slots(a_tiles, columns, dinv, tent, agg, place, count_y, members):
    rows, taps, tile = a_tiles.shape[0], a_tiles.shape[1], a_tiles.shape[-1]
    steps = rows // ROWS_PER_STEP
    span = ROWS_PER_STEP * tile
    scalars = pl.BlockSpec(memory_space=pltpu.SMEM)
    return pl.pallas_call(
        functools.partial(own_kernel, count_y, rows, members, taps),
        grid_spec=pltpu.PrefetchScalarGridSpec(
            num_scalar_prefetch=3,
            grid=(steps,),
            in_specs=[
                pl.BlockSpec((ROWS_PER_STEP, taps, tile, tile), lambda s, *_: (s, 0, 0, 0)),
                pl.BlockSpec((ROWS_PER_STEP, tile, tile), lambda s, *_: (s, 0, 0)),
                pl.BlockSpec((rows, tile, tile), lambda s, *_: (0, 0, 0)),
            ],
            out_specs=[pl.BlockSpec((members * tile, span), lambda s, *_: (0, s))] * 2
            + [scalars] * 4,
            scratch_shapes=[pltpu.SMEM((1,), jnp.int32)]
            + [pltpu.VMEM(((members + 1) * tile, tile), jnp.float32)] * ROWS_PER_STEP,
        ),
        out_shape=[jax.ShapeDtypeStruct((members * tile, rows * tile), jnp.bfloat16)] * 2
        + [jax.ShapeDtypeStruct((rows * taps,), jnp.int32)] * 3
        + [jax.ShapeDtypeStruct((steps,), jnp.int32)],
        compiler_params=pltpu.CompilerParams(vmem_limit_bytes=24 * 1024 * 1024),
        cost_estimate=pl.CostEstimate(
            flops=2 * tile**3 * rows * (taps + members),
            bytes_accessed=2 * (a_tiles.size + dinv.size * 6),
            transcendentals=0,
        ),
        name="own_slots",
    )(columns, agg, place, a_tiles, dinv, tent)


def kept_members(shift):
    lone = CROSS_SHIFTS.index(shift)
    return tuple((lone + 1 + p) % 5 for p in range(4))


def product(left, right, outs, lone, members, tile):
    value = lax.dot_general(left, right, NT, preferred_element_type=jnp.float32)
    for d1, out in enumerate(outs):
        for d2 in range(5):
            target, at = out, d2
            if d1 in lone:
                direction, single = lone[d1]
                target, at = (single, 0) if d2 == direction else (out, (d2 + 4 - direction) % 5)
            for m in range(members):
                for m2 in range(members):
                    row, column = (d1 * members + m) * tile, (d2 * members + m2) * tile
                    block = value[row : row + tile, column : column + tile]
                    target[at, m, m2] = block.astype(target.dtype)


def partial_kernel(members, taps, tiles, sources, slots, ends, *refs):
    a_tiles, dinv, *tents = refs[:6]
    right_own, *outs, behind, ahead, right_out = refs[6:14]
    tent, right, left, held, sems = refs[14:]
    tile = dinv.shape[-1]
    rows = dinv.shape[0]
    outer = 4 * members
    depth = rows * tile

    copies = [
        pltpu.make_async_copy(source, tent.at[pl.ds(d * rows, rows)], sems.at[d])
        for d, source in zip(HALO_ORDER, tents)
    ]
    own_part = (pl.ds(outer * tile, members * tile), pl.ds(0, depth))
    own_copy = pltpu.make_async_copy(right_own, right.at[own_part], sems.at[4])
    out_copy = pltpu.make_async_copy(right.at[:, pl.ds(0, depth)], right_out, sems.at[5])
    for copy in copies:
        copy.start()
    own_copy.start()
    right[: outer * tile, :] = jnp.zeros((outer * tile, right.shape[1]), right.dtype)
    left[...] = jnp.zeros_like(left)
    held[...] = jnp.zeros_like(held)
    for copy in copies:
        copy.wait()

    last = ends[rows // ROWS_PER_STEP - 1]
    batches = (last + UNROLL - 1) // UNROLL

    def entry(at):
        index = jnp.clip(at, 0, last - 1)
        row = tiles[index] // taps
        lanes = lane_tiles(jnp.where((at >= 0) & (at < last), row, rows), tile)
        return index, row, (lane_tiles(slots[index], tile), lanes)

    def some(n, carry):
        fresh, older = [], []
        for u in range(UNROLL):
            index, _, at = entry(UNROLL * n + u)
            z = lax.dot_general(
                tent[sources[index]],
                a_tiles[tiles[index]],
                NT,
                preferred_element_type=jnp.float32,
            ).astype(jnp.bfloat16)
            fresh.append((at, z))
            _, row, at = entry(UNROLL * (n - 1) + u)
            smooth = lax.dot_general(
                held[(n + 1) % 2, u], dinv[row], NT, preferred_element_type=jnp.float32
            )
            older.append((at, smooth))
        for u, ((at, z), (old_at, smooth)) in enumerate(zip(fresh, older)):
            held[n % 2, u] = z
            right[at] = (right[at].astype(jnp.float32) + z.astype(jnp.float32)).astype(
                jnp.bfloat16
            )
            left[old_at] = (left[old_at].astype(jnp.float32) - smoothing * smooth).astype(
                jnp.bfloat16
            )
        return carry

    lax.fori_loop(0, jnp.where(batches > 0, batches + 1, 0), some, 0)
    own_copy.wait()
    out_copy.start()
    lone = {d: (CROSS_SHIFTS.index(t), out) for d, t, out in ((0, UP, behind), (1, DOWN, ahead))}
    product(left[:, :depth], right[:, :depth], outs, lone, members, tile)
    out_copy.wait()


def partial_blocks(a_tiles, dinv, tents, own_right, lists, members):
    rows, taps, tile = a_tiles.shape[0], a_tiles.shape[1], a_tiles.shape[-1]
    leads = (4, 4, 5, 5, 1, 1)
    outer = 4 * members * tile
    slots = outer + members * tile
    scalars, inside, anywhere = (
        pl.BlockSpec(memory_space=space) for space in (pltpu.SMEM, pltpu.VMEM, pl.ANY)
    )
    return pl.pallas_call(
        functools.partial(partial_kernel, members, taps),
        in_specs=[scalars] * 4 + [inside] * 6 + [anywhere],
        out_specs=[inside] * 6 + [anywhere],
        scratch_shapes=[
            pltpu.VMEM((4 * rows, tile, tile), jnp.bfloat16),
            pltpu.VMEM((slots, (rows + 1) * tile), jnp.bfloat16),
            pltpu.VMEM((outer, (rows + 1) * tile), jnp.bfloat16),
            pltpu.VMEM((2, UNROLL, tile, tile), jnp.bfloat16),
            pltpu.SemaphoreType.DMA((6,)),
        ],
        out_shape=[
            jax.ShapeDtypeStruct((lead, members, members, tile, tile), jnp.bfloat16)
            for lead in leads
        ]
        + [jax.ShapeDtypeStruct((slots, rows * tile), jnp.bfloat16)],
        compiler_params=pltpu.CompilerParams(vmem_limit_bytes=36 * 1024 * 1024),
        cost_estimate=pl.CostEstimate(
            flops=2 * tile**3 * rows * (taps + 20 * members * members),
            bytes_accessed=2 * (a_tiles.size + 20 * dinv.size),
            transcendentals=0,
        ),
        name="partial_blocks",
    )(*lists, a_tiles.reshape(rows * taps, tile, tile), dinv, *tents, own_right)


def own_rows_kernel(members, left_own, right_all, own, left, right, sems):
    copies = [
        pltpu.make_async_copy(left_own, left, sems.at[0]),
        pltpu.make_async_copy(right_all, right, sems.at[1]),
    ]
    for copy in copies:
        copy.start()
    for copy in copies:
        copy.wait()
    product(left[...], right[...], (own,), {}, members, own.shape[-1])


def own_rows(left, right, members):
    tile = left.shape[0] // members
    block = (5, members, members, tile, tile)
    return pl.pallas_call(
        functools.partial(own_rows_kernel, members),
        grid=(1,),
        in_specs=[pl.BlockSpec(memory_space=pl.ANY)] * 2,
        out_specs=pl.BlockSpec(block, lambda s: (0,) * 5),
        out_shape=jax.ShapeDtypeStruct(block, jnp.float32),
        scratch_shapes=[
            pltpu.VMEM(left.shape, left.dtype),
            pltpu.VMEM(right.shape, right.dtype),
            pltpu.SemaphoreType.DMA((2,)),
        ],
        compiler_params=pltpu.CompilerParams(vmem_limit_bytes=32 * 1024 * 1024),
        cost_estimate=pl.CostEstimate(
            flops=2 * left.size * right.shape[0],
            bytes_accessed=2 * (left.size + right.size),
            transcendentals=0,
        ),
        name="own_rows",
    )(left, right)


def window_kernel(*refs):
    every = tuple(range(5))
    held = (kept_members(DOWN), kept_members(UP), every, every, every)
    behind, ahead = refs[5:7]
    for out, half in zip(refs[7:], HALVES):
        for position, offset in enumerate(half):
            if offset in (AHEAD, BEHIND):
                out[position] = (ahead if offset == AHEAD else behind)[0]
                continue
            total = None
            for shift, values, directions in zip(CROSS_SHIFTS, refs, held):
                for d, direction in enumerate(directions):
                    member = CROSS_SHIFTS[direction]
                    if (shift[0] + member[0], shift[1] + member[1]) == WINDOW_SHIFTS[offset]:
                        term = values[d].astype(jnp.float32)
                        total = term if total is None else total + term
            out[position] = total.astype(out.dtype)


def finished_window(blocks):
    _, members, _, tile, _ = blocks[0].shape
    spec = lambda lead: pl.BlockSpec(
        (lead, 1, members, tile, tile), lambda m: (0, m, 0, 0, 0)
    )
    return pl.pallas_call(
        window_kernel,
        grid=(members,),
        in_specs=[spec(block.shape[0]) for block in blocks],
        out_specs=[spec(len(half)) for half in HALVES],
        out_shape=[
            jax.ShapeDtypeStruct((len(half), members, members, tile, tile), jnp.bfloat16)
            for half in HALVES
        ],
        compiler_params=pltpu.CompilerParams(vmem_limit_bytes=32 * 1024 * 1024),
        cost_estimate=pl.CostEstimate(
            flops=5 * blocks[4].size, bytes_accessed=16 * blocks[4].size, transcendentals=0
        ),
        name="finished_window",
    )(*blocks)


def place_kernel(lists, edges, row, valid, *refs):
    arrays, (out, nothing, sems) = refs[: len(lists)], refs[-3:]
    count = out.shape[0]
    nothing[...] = jnp.zeros_like(nothing)

    def each(act):
        def move(source, target, offset, sem):
            act(pltpu.make_async_copy(source, out.at[target, :, offset], sems.at[sem]))

        for index, (array, (held, written)) in enumerate(zip(arrays, lists)):

            def write(offset, target):
                source = array.at[held.index(offset)] if offset in held else nothing
                move(source, target, offset, index * 13 + offset)

            here = row[index]

            @pl.when(valid[index] == 1)
            def _():
                for offset in written:
                    if offset not in (AHEAD, BEHIND):
                        write(offset, here)

            if AHEAD in written:

                @pl.when((valid[index] == 1) & (here + 1 < count))
                def _():
                    write(AHEAD, here + 1)

            if BEHIND in written:

                @pl.when((valid[index] == 1) & (here > 0))
                def _():
                    write(BEHIND, here - 1)

        if edges:
            move(nothing, 0, AHEAD, 13 * len(lists))
            move(nothing, count - 1, BEHIND, 13 * len(lists) + 1)

    each(lambda copy: copy.start())
    each(lambda copy: copy.wait())


def placed(out, pieces, count):
    arrays = [piece[0] for piece in pieces]
    members, _, tile, _ = arrays[0].shape[1:]
    scalars = pl.BlockSpec(memory_space=pltpu.SMEM)
    in_specs = [scalars] * 2 + [pl.BlockSpec(memory_space=pltpu.VMEM)] * len(arrays)
    operands = list(arrays)
    if out is not None:
        in_specs.append(pl.BlockSpec(memory_space=pl.ANY))
        operands.append(out)
    rows = jnp.stack([jnp.asarray(jnp.where(p[4], p[3], 0), jnp.int32) for p in pieces])
    valid = jnp.stack([jnp.asarray(p[4], jnp.int32) for p in pieces])
    return pl.pallas_call(
        functools.partial(place_kernel, tuple(p[1:3] for p in pieces), out is None),
        in_specs=in_specs,
        out_specs=pl.BlockSpec(memory_space=pl.ANY),
        scratch_shapes=[
            pltpu.VMEM((members, members, tile, tile), jnp.bfloat16),
            pltpu.SemaphoreType.DMA((len(pieces) * 13 + 2,)),
        ],
        out_shape=jax.ShapeDtypeStruct(
            (count, members, 13, members, tile, tile), jnp.bfloat16
        ),
        input_output_aliases={2 + len(arrays): 0} if out is not None else {},
        compiler_params=pltpu.CompilerParams(vmem_limit_bytes=24 * 1024 * 1024),
        cost_estimate=pl.CostEstimate(
            flops=0, bytes_accessed=6 * 13 * members * members * tile * tile, transcendentals=0
        ),
        name="placed",
    )(rows, valid, *operands)


def end_to_end(halves, grid_y, count_y):
    lower = tuple(o for o in TRAVEL if WINDOW_SHIFTS[o][1] in (0, 1))
    upper = tuple(o for o in TRAVEL if WINDOW_SHIFTS[o][1] in (-1, 0))
    start = jnp.where(grid_y == 0, TRAVEL.index(lower[0]), TRAVEL.index(upper[0]))
    sent = lax.dynamic_slice_in_dim(jnp.concatenate(halves, axis=0), start, len(lower), axis=0)
    last = count_y - 1
    moved = lax.ppermute(sent, "sy", [(0, last), (last, 0)])
    return [
        (moved, lower, TRAVEL, 0, grid_y == last),
        (moved, upper, TRAVEL, last, grid_y == 0),
    ]


def gathered_rows(halves, grid_y, count_y):
    chains = [(half, half) for half in halves]
    pieces = [(half, group, group, grid_y, True) for half, group in zip(halves, HALVES)]
    out = None
    for hop in range(1, count_y - 1):
        chains = [(shifted(a, "sy", 1), shifted(b, "sy", -1)) for a, b in chains]
        if hop == 1:
            direct = end_to_end(halves, grid_y, count_y)
        out = placed(out, pieces, count_y)
        if hop == 1:
            chains[1], out = lax.optimization_barrier((chains[1], out))
        pieces = []
        for (from_lower, from_upper), group in zip(chains, HALVES):
            pieces += [
                (from_lower, group, group, grid_y - hop, grid_y >= hop),
                (from_upper, group, group, grid_y + hop, grid_y + hop < count_y),
            ]
    out = placed(out, direct + pieces[2:], count_y)
    return placed(out, pieces[:2], count_y)


def local(a_tiles, columns, ptent, dinv, agg):
    grid_x = lax.axis_index("sx")
    grid_y = lax.axis_index("sy")
    count_y = lax.axis_size("sy")
    rows, taps, tile = a_tiles.shape[2], a_tiles.shape[3], a_tiles.shape[-1]
    coupling = a_tiles.reshape(rows, taps, tile, tile)
    inverse = dinv.reshape(rows, tile, tile)
    tent = jnp.swapaxes(ptent.reshape(rows, tile, tile), 1, 2)
    tents = (
        shifted(tent, "sy", 1),
        shifted(tent, "sy", -1),
        swapped(tent, "sx", 1),
        swapped(tent, "sx", 0),
    )
    own_right, own_left, *lists = own_slots(
        coupling,
        columns.reshape(rows * taps),
        inverse,
        tent,
        agg,
        jnp.stack([grid_x, grid_y]).astype(jnp.int32),
        count_y,
        MEMBERS,
    )
    to_lower_y, to_upper_y, to_lower_x, to_upper_x, behind, ahead, right = partial_blocks(
        coupling, inverse, tents, own_right, lists, MEMBERS
    )
    halves = finished_window(
        (
            shifted(to_upper_y, "sy", 1),
            shifted(to_lower_y, "sy", -1),
            shifted(to_upper_x, "sx", 1),
            shifted(to_lower_x, "sx", -1),
            own_rows(own_left, right, MEMBERS),
            behind,
            ahead,
        )
    )
    return gathered_rows(halves, grid_y, count_y)[None]


def solution(mesh):
    return jax.shard_map(
        local,
        mesh=mesh,
        in_specs=(
            P("sx", "sy", None, None, None, None),
            P("sx", "sy", None, None),
            P("sx", "sy", None, None, None),
            P("sx", "sy", None, None, None),
            P(),
        ),
        out_specs=P("sx", None, None, None, None, None, None),
        check_vma=False,
    )
```

```python
import functools

import jax
import jax.numpy as jnp
from jax import lax
from jax.experimental import pallas as pl
from jax.experimental.pallas import tpu as pltpu
from jax.sharding import PartitionSpec as P

CROSS_SHIFTS = ((0, -1), (0, 1), (-1, 0), (1, 0), (0, 0))
OWN = 4
DOWN, UP = CROSS_SHIFTS[:2]
HALO_ORDER = (0, 1, 3, 2)
WINDOW_SHIFTS = (
    (-2, 0),
    (-1, -1),
    (-1, 0),
    (-1, 1),
    (0, -2),
    (0, -1),
    (0, 0),
    (0, 1),
    (0, 2),
    (1, -1),
    (1, 0),
    (1, 1),
    (2, 0),
)
AHEAD, BEHIND = 4, 8
TRAVEL = (4, 1, 5, 9, 0, 2, 6, 10, 12, 3, 7, 11, 8)
HALVES = (TRAVEL[:6], TRAVEL[6:])
smoothing = 2.0 / 3.0
MEMBERS = 2
ROWS_PER_STEP = 4
UNROLL = 8
NT = (((1,), (1,)), ((), ()))


def shifted(x, axis, by):
    length = lax.axis_size(axis)
    pairs = [(i, i + by) for i in range(length) if 0 <= i + by < length]
    return lax.ppermute(x, axis, pairs)


def lane_tiles(g, tile):
    return pl.ds(pl.multiple_of(g * tile, tile), tile)


def swapped(x, axis, first):
    lows = range(first, lax.axis_size(axis) - 1, 2)
    return lax.ppermute(x, axis, [(i + a, i + 1 - a) for i in lows for a in (0, 1)])


def own_kernel(count_y, rows, members, taps, columns, agg, place, a_ref, dinv_ref, tent, *refs):
    right, left, tiles, sources, slots, ends, found = refs[:7]
    sums = refs[7:]
    tile = a_ref.shape[-1]
    step = pl.program_id(0)

    @pl.when(step == 0)
    def _():
        found[0] = 0

    listed = found[0]
    for u in range(ROWS_PER_STEP):
        g = step * ROWS_PER_STEP + u
        total = sums[u]
        total[...] = jnp.zeros_like(total)
        own_member = 0
        for k in range(taps):
            target = columns[g * taps + k]
            holder = target // rows
            step_x = holder // count_y - place[0]
            step_y = holder % count_y - place[1]
            direction = jnp.where(
                step_y == -1,
                0,
                jnp.where(step_y == 1, 1, jnp.where(step_x == -1, 2, jnp.where(step_x == 1, 3, OWN))),
            )
            member = agg[target] % members
            if k == 0:
                own_member = member
            else:
                tiles[listed] = g * taps + k
                seat = jnp.where(direction < 2, direction, 2 + (direction + place[0] + 1) % 2)
                sources[listed] = seat * rows + target % rows
                slots[listed] = direction * members + member
                listed += jnp.where(direction == OWN, 0, 1)
            z = lax.dot_general(
                tent[target % rows], a_ref[u, k], NT, preferred_element_type=jnp.float32
            )
            slot = jnp.where(direction == OWN, member, members)
            total[lane_tiles(slot, tile), :] += z.astype(jnp.bfloat16).astype(jnp.float32)
        here = slice(u * tile, (u + 1) * tile)
        applied = total[: members * tile, :].astype(jnp.bfloat16)
        right[:, here] = applied
        smooth = lax.dot_general(applied, dinv_ref[u], NT, preferred_element_type=jnp.float32)
        total[: members * tile, :] = -smoothing * smooth
        total[lane_tiles(own_member, tile), :] += tent[g].astype(jnp.float32)
        left[:, here] = total[: members * tile, :].astype(jnp.bfloat16)
    found[0] = listed
    ends[step] = listed


def own_slots(a_tiles, columns, dinv, tent, agg, place, count_y, members):
    rows, taps, tile = a_tiles.shape[0], a_tiles.shape[1], a_tiles.shape[-1]
    steps = rows // ROWS_PER_STEP
    span = ROWS_PER_STEP * tile
    scalars = pl.BlockSpec(memory_space=pltpu.SMEM)
    return pl.pallas_call(
        functools.partial(own_kernel, count_y, rows, members, taps),
        grid_spec=pltpu.PrefetchScalarGridSpec(
            num_scalar_prefetch=3,
            grid=(steps,),
            in_specs=[
                pl.BlockSpec((ROWS_PER_STEP, taps, tile, tile), lambda s, *_: (s, 0, 0, 0)),
                pl.BlockSpec((ROWS_PER_STEP, tile, tile), lambda s, *_: (s, 0, 0)),
                pl.BlockSpec((rows, tile, tile), lambda s, *_: (0, 0, 0)),
            ],
            out_specs=[pl.BlockSpec((members * tile, span), lambda s, *_: (0, s))] * 2
            + [scalars] * 4,
            scratch_shapes=[pltpu.SMEM((1,), jnp.int32)]
            + [pltpu.VMEM(((members + 1) * tile, tile), jnp.float32)] * ROWS_PER_STEP,
        ),
        out_shape=[jax.ShapeDtypeStruct((members * tile, rows * tile), jnp.bfloat16)] * 2
        + [jax.ShapeDtypeStruct((rows * taps,), jnp.int32)] * 3
        + [jax.ShapeDtypeStruct((steps,), jnp.int32)],
        compiler_params=pltpu.CompilerParams(vmem_limit_bytes=24 * 1024 * 1024),
        cost_estimate=pl.CostEstimate(
            flops=2 * tile**3 * rows * (taps + members),
            bytes_accessed=2 * (a_tiles.size + dinv.size * 6),
            transcendentals=0,
        ),
        name="own_slots",
    )(columns, agg, place, a_tiles, dinv, tent)


def kept_members(shift):
    lone = CROSS_SHIFTS.index(shift)
    return tuple((lone + 1 + p) % 5 for p in range(4))


def product(left, right, outs, lone, members, tile):
    width = members * tile
    for d1, out in enumerate(outs):
        value = lax.dot_general(
            left[d1 * width : (d1 + 1) * width],
            right,
            NT,
            preferred_element_type=jnp.float32,
        )
        for d2 in range(5):
            target, at = out, d2
            if d1 in lone:
                direction, single = lone[d1]
                target, at = (single, 0) if d2 == direction else (out, (d2 + 4 - direction) % 5)
            for m in range(members):
                for m2 in range(members):
                    row, column = m * tile, (d2 * members + m2) * tile
                    block = value[row : row + tile, column : column + tile]
                    target[at, m, m2] = block.astype(target.dtype)


def partial_kernel(members, taps, tiles, sources, slots, ends, *refs):
    a_tiles, dinv, *tents = refs[:6]
    right_own, *outs, behind, ahead, right_out = refs[6:14]
    tent, right, left, held, sems = refs[14:]
    tile = dinv.shape[-1]
    rows = dinv.shape[0]
    outer = 4 * members
    depth = rows * tile

    copies = [
        pltpu.make_async_copy(source, tent.at[pl.ds(d * rows, rows)], sems.at[d])
        for d, source in zip(HALO_ORDER, tents)
    ]
    own_part = (pl.ds(outer * tile, members * tile), pl.ds(0, depth))
    own_copy = pltpu.make_async_copy(right_own, right.at[own_part], sems.at[4])
    out_copy = pltpu.make_async_copy(right.at[:, pl.ds(0, depth)], right_out, sems.at[5])
    for copy in copies:
        copy.start()
    own_copy.start()
    right[: outer * tile, :] = jnp.zeros((outer * tile, right.shape[1]), right.dtype)
    left[...] = jnp.zeros_like(left)
    held[...] = jnp.zeros_like(held)
    for copy in copies:
        copy.wait()

    last = ends[rows // ROWS_PER_STEP - 1]
    batches = (last + UNROLL - 1) // UNROLL

    def entry(at):
        index = jnp.clip(at, 0, last - 1)
        row = tiles[index] // taps
        lanes = lane_tiles(jnp.where((at >= 0) & (at < last), row, rows), tile)
        return index, row, (lane_tiles(slots[index], tile), lanes)

    def some(n, carry):
        fresh, older = [], []
        for u in range(UNROLL):
            index, _, at = entry(UNROLL * n + u)
            z = lax.dot_general(
                tent[sources[index]],
                a_tiles[tiles[index]],
                NT,
                preferred_element_type=jnp.float32,
            ).astype(jnp.bfloat16)
            fresh.append((at, z))
            _, row, at = entry(UNROLL * (n - 1) + u)
            smooth = lax.dot_general(
                held[(n + 1) % 2, u], dinv[row], NT, preferred_element_type=jnp.float32
            )
            older.append((at, smooth))
        for u, ((at, z), (old_at, smooth)) in enumerate(zip(fresh, older)):
            held[n % 2, u] = z
            right[at] = (right[at].astype(jnp.float32) + z.astype(jnp.float32)).astype(
                jnp.bfloat16
            )
            left[old_at] = (left[old_at].astype(jnp.float32) - smoothing * smooth).astype(
                jnp.bfloat16
            )
        return carry

    lax.fori_loop(0, jnp.where(batches > 0, batches + 1, 0), some, 0)
    own_copy.wait()
    out_copy.start()
    lone = {d: (CROSS_SHIFTS.index(t), out) for d, t, out in ((0, UP, behind), (1, DOWN, ahead))}
    product(left[:, :depth], right[:, :depth], outs, lone, members, tile)
    out_copy.wait()


def partial_blocks(a_tiles, dinv, tents, own_right, lists, members):
    rows, taps, tile = a_tiles.shape[0], a_tiles.shape[1], a_tiles.shape[-1]
    leads = (4, 4, 5, 5, 1, 1)
    outer = 4 * members * tile
    slots = outer + members * tile
    scalars, inside, anywhere = (
        pl.BlockSpec(memory_space=space) for space in (pltpu.SMEM, pltpu.VMEM, pl.ANY)
    )
    return pl.pallas_call(
        functools.partial(partial_kernel, members, taps),
        in_specs=[scalars] * 4 + [inside] * 6 + [anywhere],
        out_specs=[inside] * 6 + [anywhere],
        scratch_shapes=[
            pltpu.VMEM((4 * rows, tile, tile), jnp.bfloat16),
            pltpu.VMEM((slots, (rows + 1) * tile), jnp.bfloat16),
            pltpu.VMEM((outer, (rows + 1) * tile), jnp.bfloat16),
            pltpu.VMEM((2, UNROLL, tile, tile), jnp.bfloat16),
            pltpu.SemaphoreType.DMA((6,)),
        ],
        out_shape=[
            jax.ShapeDtypeStruct((lead, members, members, tile, tile), jnp.bfloat16)
            for lead in leads
        ]
        + [jax.ShapeDtypeStruct((slots, rows * tile), jnp.bfloat16)],
        compiler_params=pltpu.CompilerParams(vmem_limit_bytes=36 * 1024 * 1024),
        cost_estimate=pl.CostEstimate(
            flops=2 * tile**3 * rows * (taps + 20 * members * members),
            bytes_accessed=2 * (a_tiles.size + 20 * dinv.size),
            transcendentals=0,
        ),
        name="partial_blocks",
    )(*lists, a_tiles.reshape(rows * taps, tile, tile), dinv, *tents, own_right)


def own_rows_kernel(members, left_own, right_all, own, left, right, sems):
    copies = [
        pltpu.make_async_copy(left_own, left, sems.at[0]),
        pltpu.make_async_copy(right_all, right, sems.at[1]),
    ]
    for copy in copies:
        copy.start()
    for copy in copies:
        copy.wait()
    product(left[...], right[...], (own,), {}, members, own.shape[-1])


def own_rows(left, right, members):
    tile = left.shape[0] // members
    block = (5, members, members, tile, tile)
    return pl.pallas_call(
        functools.partial(own_rows_kernel, members),
        grid=(1,),
        in_specs=[pl.BlockSpec(memory_space=pl.ANY)] * 2,
        out_specs=pl.BlockSpec(block, lambda s: (0,) * 5),
        out_shape=jax.ShapeDtypeStruct(block, jnp.float32),
        scratch_shapes=[
            pltpu.VMEM(left.shape, left.dtype),
            pltpu.VMEM(right.shape, right.dtype),
            pltpu.SemaphoreType.DMA((2,)),
        ],
        compiler_params=pltpu.CompilerParams(vmem_limit_bytes=32 * 1024 * 1024),
        cost_estimate=pl.CostEstimate(
            flops=2 * left.size * right.shape[0],
            bytes_accessed=2 * (left.size + right.size),
            transcendentals=0,
        ),
        name="own_rows",
    )(left, right)


def window_kernel(*refs):
    every = tuple(range(5))
    held = (kept_members(DOWN), kept_members(UP), every, every, every)
    behind, ahead = refs[5:7]
    for out, half in zip(refs[7:], HALVES):
        for position, offset in enumerate(half):
            if offset in (AHEAD, BEHIND):
                out[position] = (ahead if offset == AHEAD else behind)[0]
                continue
            total = None
            for shift, values, directions in zip(CROSS_SHIFTS, refs, held):
                for d, direction in enumerate(directions):
                    member = CROSS_SHIFTS[direction]
                    if (shift[0] + member[0], shift[1] + member[1]) == WINDOW_SHIFTS[offset]:
                        term = values[d].astype(jnp.float32)
                        total = term if total is None else total + term
            out[position] = total.astype(out.dtype)


def finished_window(blocks):
    _, members, _, tile, _ = blocks[0].shape
    spec = lambda lead: pl.BlockSpec(
        (lead, 1, members, tile, tile), lambda m: (0, m, 0, 0, 0)
    )
    return pl.pallas_call(
        window_kernel,
        grid=(members,),
        in_specs=[spec(block.shape[0]) for block in blocks],
        out_specs=[spec(len(half)) for half in HALVES],
        out_shape=[
            jax.ShapeDtypeStruct((len(half), members, members, tile, tile), jnp.bfloat16)
            for half in HALVES
        ],
        compiler_params=pltpu.CompilerParams(vmem_limit_bytes=32 * 1024 * 1024),
        cost_estimate=pl.CostEstimate(
            flops=5 * blocks[4].size, bytes_accessed=16 * blocks[4].size, transcendentals=0
        ),
        name="finished_window",
    )(*blocks)


def place_kernel(lists, edges, row, valid, *refs):
    arrays, (out, nothing, sems) = refs[: len(lists)], refs[-3:]
    count = out.shape[0]
    nothing[...] = jnp.zeros_like(nothing)

    def each(act):
        def move(source, target, offset, sem):
            act(pltpu.make_async_copy(source, out.at[target, :, offset], sems.at[sem]))

        for index, (array, (held, written)) in enumerate(zip(arrays, lists)):

            def write(offset, target):
                source = array.at[held.index(offset)] if offset in held else nothing
                move(source, target, offset, index * 13 + offset)

            here = row[index]

            @pl.when(valid[index] == 1)
            def _():
                for offset in written:
                    if offset not in (AHEAD, BEHIND):
                        write(offset, here)

            if AHEAD in written:

                @pl.when((valid[index] == 1) & (here + 1 < count))
                def _():
                    write(AHEAD, here + 1)

            if BEHIND in written:

                @pl.when((valid[index] == 1) & (here > 0))
                def _():
                    write(BEHIND, here - 1)

        if edges:
            move(nothing, 0, AHEAD, 13 * len(lists))
            move(nothing, count - 1, BEHIND, 13 * len(lists) + 1)

    each(lambda copy: copy.start())
    each(lambda copy: copy.wait())


def placed(out, pieces, count):
    arrays = [piece[0] for piece in pieces]
    members, _, tile, _ = arrays[0].shape[1:]
    scalars = pl.BlockSpec(memory_space=pltpu.SMEM)
    in_specs = [scalars] * 2 + [pl.BlockSpec(memory_space=pltpu.VMEM)] * len(arrays)
    operands = list(arrays)
    if out is not None:
        in_specs.append(pl.BlockSpec(memory_space=pl.ANY))
        operands.append(out)
    rows = jnp.stack([jnp.asarray(jnp.where(p[4], p[3], 0), jnp.int32) for p in pieces])
    valid = jnp.stack([jnp.asarray(p[4], jnp.int32) for p in pieces])
    return pl.pallas_call(
        functools.partial(place_kernel, tuple(p[1:3] for p in pieces), out is None),
        in_specs=in_specs,
        out_specs=pl.BlockSpec(memory_space=pl.ANY),
        scratch_shapes=[
            pltpu.VMEM((members, members, tile, tile), jnp.bfloat16),
            pltpu.SemaphoreType.DMA((len(pieces) * 13 + 2,)),
        ],
        out_shape=jax.ShapeDtypeStruct(
            (count, members, 13, members, tile, tile), jnp.bfloat16
        ),
        input_output_aliases={2 + len(arrays): 0} if out is not None else {},
        compiler_params=pltpu.CompilerParams(vmem_limit_bytes=24 * 1024 * 1024),
        cost_estimate=pl.CostEstimate(
            flops=0, bytes_accessed=6 * 13 * members * members * tile * tile, transcendentals=0
        ),
        name="placed",
    )(rows, valid, *operands)


def end_to_end(halves, grid_y, count_y):
    lower = tuple(o for o in TRAVEL if WINDOW_SHIFTS[o][1] in (0, 1))
    upper = tuple(o for o in TRAVEL if WINDOW_SHIFTS[o][1] in (-1, 0))
    start = jnp.where(grid_y == 0, TRAVEL.index(lower[0]), TRAVEL.index(upper[0]))
    sent = lax.dynamic_slice_in_dim(jnp.concatenate(halves, axis=0), start, len(lower), axis=0)
    last = count_y - 1
    moved = lax.ppermute(sent, "sy", [(0, last), (last, 0)])
    return [
        (moved, lower, TRAVEL, 0, grid_y == last),
        (moved, upper, TRAVEL, last, grid_y == 0),
    ]


def gathered_rows(halves, grid_y, count_y):
    chains = [(half, half) for half in halves]
    pieces = [(half, group, group, grid_y, True) for half, group in zip(halves, HALVES)]
    out = None
    for hop in range(1, count_y - 1):
        chains = [(shifted(a, "sy", 1), shifted(b, "sy", -1)) for a, b in chains]
        if hop == 1:
            direct = end_to_end(halves, grid_y, count_y)
        out = placed(out, pieces, count_y)
        if hop == 1:
            chains[1], out = lax.optimization_barrier((chains[1], out))
        pieces = []
        for (from_lower, from_upper), group in zip(chains, HALVES):
            pieces += [
                (from_lower, group, group, grid_y - hop, grid_y >= hop),
                (from_upper, group, group, grid_y + hop, grid_y + hop < count_y),
            ]
    out = placed(out, direct + pieces[2:], count_y)
    return placed(out, pieces[:2], count_y)


def local(a_tiles, columns, ptent, dinv, agg):
    grid_x = lax.axis_index("sx")
    grid_y = lax.axis_index("sy")
    count_y = lax.axis_size("sy")
    rows, taps, tile = a_tiles.shape[2], a_tiles.shape[3], a_tiles.shape[-1]
    coupling = a_tiles.reshape(rows, taps, tile, tile)
    inverse = dinv.reshape(rows, tile, tile)
    tent = jnp.swapaxes(ptent.reshape(rows, tile, tile), 1, 2)
    tents = (
        shifted(tent, "sy", 1),
        shifted(tent, "sy", -1),
        swapped(tent, "sx", 1),
        swapped(tent, "sx", 0),
    )
    own_right, own_left, *lists = own_slots(
        coupling,
        columns.reshape(rows * taps),
        inverse,
        tent,
        agg,
        jnp.stack([grid_x, grid_y]).astype(jnp.int32),
        count_y,
        MEMBERS,
    )
    to_lower_y, to_upper_y, to_lower_x, to_upper_x, behind, ahead, right = partial_blocks(
        coupling, inverse, tents, own_right, lists, MEMBERS
    )
    halves = finished_window(
        (
            shifted(to_upper_y, "sy", 1),
            shifted(to_lower_y, "sy", -1),
            shifted(to_upper_x, "sx", 1),
            shifted(to_lower_x, "sx", -1),
            own_rows(own_left, right, MEMBERS),
            behind,
            ahead,
        )
    )
    return gathered_rows(halves, grid_y, count_y)[None]


def solution(mesh):
    return jax.shard_map(
        local,
        mesh=mesh,
        in_specs=(
            P("sx", "sy", None, None, None, None),
            P("sx", "sy", None, None),
            P("sx", "sy", None, None, None),
            P("sx", "sy", None, None, None),
            P(),
        ),
        out_specs=P("sx", None, None, None, None, None, None),
        check_vma=False,
    )
```

```python
import functools

import jax
import jax.numpy as jnp
from jax import lax
from jax.experimental import pallas as pl
from jax.experimental.pallas import tpu as pltpu
from jax.sharding import PartitionSpec as P

CROSS_SHIFTS = ((0, -1), (0, 1), (-1, 0), (1, 0), (0, 0))
OWN = 4
DOWN, UP = CROSS_SHIFTS[:2]
HALO_ORDER = (0, 1, 3, 2)
WINDOW_SHIFTS = (
    (-2, 0),
    (-1, -1),
    (-1, 0),
    (-1, 1),
    (0, -2),
    (0, -1),
    (0, 0),
    (0, 1),
    (0, 2),
    (1, -1),
    (1, 0),
    (1, 1),
    (2, 0),
)
AHEAD, BEHIND = 4, 8
TRAVEL = (4, 1, 5, 9, 0, 2, 6, 10, 12, 3, 7, 11, 8)
HALVES = (TRAVEL[:6], TRAVEL[6:])
smoothing = 2.0 / 3.0
MEMBERS = 2
ROWS_PER_STEP = 4
UNROLL = 16
NT = (((1,), (1,)), ((), ()))


def shifted(x, axis, by):
    length = lax.axis_size(axis)
    pairs = [(i, i + by) for i in range(length) if 0 <= i + by < length]
    return lax.ppermute(x, axis, pairs)


def lane_tiles(g, tile):
    return pl.ds(pl.multiple_of(g * tile, tile), tile)


def swapped(x, axis, first):
    lows = range(first, lax.axis_size(axis) - 1, 2)
    return lax.ppermute(x, axis, [(i + a, i + 1 - a) for i in lows for a in (0, 1)])


def own_kernel(count_y, rows, members, taps, columns, agg, place, a_ref, dinv_ref, tent, *refs):
    right, left, tiles, sources, slots, ends, found = refs[:7]
    sums = refs[7:]
    tile = a_ref.shape[-1]
    step = pl.program_id(0)

    @pl.when(step == 0)
    def _():
        found[0] = 0

    listed = found[0]
    for u in range(ROWS_PER_STEP):
        g = step * ROWS_PER_STEP + u
        total = sums[u]
        total[...] = jnp.zeros_like(total)
        own_member = 0
        for k in range(taps):
            target = columns[g * taps + k]
            holder = target // rows
            step_x = holder // count_y - place[0]
            step_y = holder % count_y - place[1]
            direction = jnp.where(
                step_y == -1,
                0,
                jnp.where(step_y == 1, 1, jnp.where(step_x == -1, 2, jnp.where(step_x == 1, 3, OWN))),
            )
            member = agg[target] % members
            if k == 0:
                own_member = member
            else:
                tiles[listed] = g * taps + k
                seat = jnp.where(direction < 2, direction, 2 + (direction + place[0] + 1) % 2)
                sources[listed] = seat * rows + target % rows
                slots[listed] = direction * members + member
                listed += jnp.where(direction == OWN, 0, 1)
            z = lax.dot_general(
                tent[target % rows], a_ref[u, k], NT, preferred_element_type=jnp.float32
            )
            slot = jnp.where(direction == OWN, member, members)
            total[lane_tiles(slot, tile), :] += z.astype(jnp.bfloat16).astype(jnp.float32)
        here = slice(u * tile, (u + 1) * tile)
        applied = total[: members * tile, :].astype(jnp.bfloat16)
        right[:, here] = applied
        smooth = lax.dot_general(applied, dinv_ref[u], NT, preferred_element_type=jnp.float32)
        total[: members * tile, :] = -smoothing * smooth
        total[lane_tiles(own_member, tile), :] += tent[g].astype(jnp.float32)
        left[:, here] = total[: members * tile, :].astype(jnp.bfloat16)
    found[0] = listed
    ends[step] = listed


def own_slots(a_tiles, columns, dinv, tent, agg, place, count_y, members):
    rows, taps, tile = a_tiles.shape[0], a_tiles.shape[1], a_tiles.shape[-1]
    steps = rows // ROWS_PER_STEP
    span = ROWS_PER_STEP * tile
    scalars = pl.BlockSpec(memory_space=pltpu.SMEM)
    return pl.pallas_call(
        functools.partial(own_kernel, count_y, rows, members, taps),
        grid_spec=pltpu.PrefetchScalarGridSpec(
            num_scalar_prefetch=3,
            grid=(steps,),
            in_specs=[
                pl.BlockSpec((ROWS_PER_STEP, taps, tile, tile), lambda s, *_: (s, 0, 0, 0)),
                pl.BlockSpec((ROWS_PER_STEP, tile, tile), lambda s, *_: (s, 0, 0)),
                pl.BlockSpec((rows, tile, tile), lambda s, *_: (0, 0, 0)),
            ],
            out_specs=[pl.BlockSpec((members * tile, span), lambda s, *_: (0, s))] * 2
            + [scalars] * 4,
            scratch_shapes=[pltpu.SMEM((1,), jnp.int32)]
            + [pltpu.VMEM(((members + 1) * tile, tile), jnp.float32)] * ROWS_PER_STEP,
        ),
        out_shape=[jax.ShapeDtypeStruct((members * tile, rows * tile), jnp.bfloat16)] * 2
        + [jax.ShapeDtypeStruct((rows * taps,), jnp.int32)] * 3
        + [jax.ShapeDtypeStruct((steps,), jnp.int32)],
        compiler_params=pltpu.CompilerParams(vmem_limit_bytes=24 * 1024 * 1024),
        cost_estimate=pl.CostEstimate(
            flops=2 * tile**3 * rows * (taps + members),
            bytes_accessed=2 * (a_tiles.size + dinv.size * 6),
            transcendentals=0,
        ),
        name="own_slots",
    )(columns, agg, place, a_tiles, dinv, tent)


def kept_members(shift):
    lone = CROSS_SHIFTS.index(shift)
    return tuple((lone + 1 + p) % 5 for p in range(4))


def product(left, right, outs, lone, members, tile):
    width = members * tile
    for d1, out in enumerate(outs):
        value = lax.dot_general(
            left[d1 * width : (d1 + 1) * width],
            right,
            NT,
            preferred_element_type=jnp.float32,
        )
        for d2 in range(5):
            target, at = out, d2
            if d1 in lone:
                direction, single = lone[d1]
                target, at = (single, 0) if d2 == direction else (out, (d2 + 4 - direction) % 5)
            for m in range(members):
                for m2 in range(members):
                    row, column = m * tile, (d2 * members + m2) * tile
                    block = value[row : row + tile, column : column + tile]
                    target[at, m, m2] = block.astype(target.dtype)


def partial_kernel(members, taps, tiles, sources, slots, ends, *refs):
    a_tiles, dinv, *tents = refs[:6]
    right_own, *outs, behind, ahead, right_out = refs[6:14]
    tent, right, left, held, sems = refs[14:]
    tile = dinv.shape[-1]
    rows = dinv.shape[0]
    outer = 4 * members
    depth = rows * tile

    copies = [
        pltpu.make_async_copy(source, tent.at[pl.ds(d * rows, rows)], sems.at[d])
        for d, source in zip(HALO_ORDER, tents)
    ]
    own_part = (pl.ds(outer * tile, members * tile), pl.ds(0, depth))
    own_copy = pltpu.make_async_copy(right_own, right.at[own_part], sems.at[4])
    out_copy = pltpu.make_async_copy(right.at[:, pl.ds(0, depth)], right_out, sems.at[5])
    for copy in copies:
        copy.start()
    own_copy.start()
    right[: outer * tile, :] = jnp.zeros((outer * tile, right.shape[1]), right.dtype)
    left[...] = jnp.zeros_like(left)
    held[...] = jnp.zeros_like(held)
    for copy in copies:
        copy.wait()

    last = ends[rows // ROWS_PER_STEP - 1]
    batches = (last + UNROLL - 1) // UNROLL

    def entry(at):
        index = jnp.clip(at, 0, last - 1)
        row = tiles[index] // taps
        lanes = lane_tiles(jnp.where((at >= 0) & (at < last), row, rows), tile)
        return index, row, (lane_tiles(slots[index], tile), lanes)

    def some(n, carry):
        fresh, older = [], []
        for u in range(UNROLL):
            index, _, at = entry(UNROLL * n + u)
            z = lax.dot_general(
                tent[sources[index]],
                a_tiles[tiles[index]],
                NT,
                preferred_element_type=jnp.float32,
            ).astype(jnp.bfloat16)
            fresh.append((at, z))
            _, row, at = entry(UNROLL * (n - 1) + u)
            smooth = lax.dot_general(
                held[(n + 1) % 2, u], dinv[row], NT, preferred_element_type=jnp.float32
            )
            older.append((at, smooth))
        for u, ((at, z), (old_at, smooth)) in enumerate(zip(fresh, older)):
            held[n % 2, u] = z
            right[at] = (right[at].astype(jnp.float32) + z.astype(jnp.float32)).astype(
                jnp.bfloat16
            )
            left[old_at] = (left[old_at].astype(jnp.float32) - smoothing * smooth).astype(
                jnp.bfloat16
            )
        return carry

    lax.fori_loop(0, jnp.where(batches > 0, batches + 1, 0), some, 0)
    own_copy.wait()
    out_copy.start()
    lone = {d: (CROSS_SHIFTS.index(t), out) for d, t, out in ((0, UP, behind), (1, DOWN, ahead))}
    product(left[:, :depth], right[:, :depth], outs, lone, members, tile)
    out_copy.wait()


def partial_blocks(a_tiles, dinv, tents, own_right, lists, members):
    rows, taps, tile = a_tiles.shape[0], a_tiles.shape[1], a_tiles.shape[-1]
    leads = (4, 4, 5, 5, 1, 1)
    outer = 4 * members * tile
    slots = outer + members * tile
    scalars, inside, anywhere = (
        pl.BlockSpec(memory_space=space) for space in (pltpu.SMEM, pltpu.VMEM, pl.ANY)
    )
    return pl.pallas_call(
        functools.partial(partial_kernel, members, taps),
        in_specs=[scalars] * 4 + [inside] * 6 + [anywhere],
        out_specs=[inside] * 6 + [anywhere],
        scratch_shapes=[
            pltpu.VMEM((4 * rows, tile, tile), jnp.bfloat16),
            pltpu.VMEM((slots, (rows + 1) * tile), jnp.bfloat16),
            pltpu.VMEM((outer, (rows + 1) * tile), jnp.bfloat16),
            pltpu.VMEM((2, UNROLL, tile, tile), jnp.bfloat16),
            pltpu.SemaphoreType.DMA((6,)),
        ],
        out_shape=[
            jax.ShapeDtypeStruct((lead, members, members, tile, tile), jnp.bfloat16)
            for lead in leads
        ]
        + [jax.ShapeDtypeStruct((slots, rows * tile), jnp.bfloat16)],
        compiler_params=pltpu.CompilerParams(vmem_limit_bytes=36 * 1024 * 1024),
        cost_estimate=pl.CostEstimate(
            flops=2 * tile**3 * rows * (taps + 20 * members * members),
            bytes_accessed=2 * (a_tiles.size + 20 * dinv.size),
            transcendentals=0,
        ),
        name="partial_blocks",
    )(*lists, a_tiles.reshape(rows * taps, tile, tile), dinv, *tents, own_right)


def own_rows_kernel(members, left_own, right_all, own, left, right, sems):
    copies = [
        pltpu.make_async_copy(left_own, left, sems.at[0]),
        pltpu.make_async_copy(right_all, right, sems.at[1]),
    ]
    for copy in copies:
        copy.start()
    for copy in copies:
        copy.wait()
    product(left[...], right[...], (own,), {}, members, own.shape[-1])


def own_rows(left, right, members):
    tile = left.shape[0] // members
    block = (5, members, members, tile, tile)
    return pl.pallas_call(
        functools.partial(own_rows_kernel, members),
        grid=(1,),
        in_specs=[pl.BlockSpec(memory_space=pl.ANY)] * 2,
        out_specs=pl.BlockSpec(block, lambda s: (0,) * 5),
        out_shape=jax.ShapeDtypeStruct(block, jnp.float32),
        scratch_shapes=[
            pltpu.VMEM(left.shape, left.dtype),
            pltpu.VMEM(right.shape, right.dtype),
            pltpu.SemaphoreType.DMA((2,)),
        ],
        compiler_params=pltpu.CompilerParams(vmem_limit_bytes=32 * 1024 * 1024),
        cost_estimate=pl.CostEstimate(
            flops=2 * left.size * right.shape[0],
            bytes_accessed=2 * (left.size + right.size),
            transcendentals=0,
        ),
        name="own_rows",
    )(left, right)


def window_kernel(*refs):
    every = tuple(range(5))
    held = (kept_members(DOWN), kept_members(UP), every, every, every)
    behind, ahead = refs[5:7]
    for out, half in zip(refs[7:], HALVES):
        for position, offset in enumerate(half):
            if offset in (AHEAD, BEHIND):
                out[position] = (ahead if offset == AHEAD else behind)[0]
                continue
            total = None
            for shift, values, directions in zip(CROSS_SHIFTS, refs, held):
                for d, direction in enumerate(directions):
                    member = CROSS_SHIFTS[direction]
                    if (shift[0] + member[0], shift[1] + member[1]) == WINDOW_SHIFTS[offset]:
                        term = values[d].astype(jnp.float32)
                        total = term if total is None else total + term
            out[position] = total.astype(out.dtype)


def finished_window(blocks):
    _, members, _, tile, _ = blocks[0].shape
    spec = lambda lead: pl.BlockSpec(
        (lead, 1, members, tile, tile), lambda m: (0, m, 0, 0, 0)
    )
    return pl.pallas_call(
        window_kernel,
        grid=(members,),
        in_specs=[spec(block.shape[0]) for block in blocks],
        out_specs=[spec(len(half)) for half in HALVES],
        out_shape=[
            jax.ShapeDtypeStruct((len(half), members, members, tile, tile), jnp.bfloat16)
            for half in HALVES
        ],
        compiler_params=pltpu.CompilerParams(vmem_limit_bytes=32 * 1024 * 1024),
        cost_estimate=pl.CostEstimate(
            flops=5 * blocks[4].size, bytes_accessed=16 * blocks[4].size, transcendentals=0
        ),
        name="finished_window",
    )(*blocks)


def place_kernel(lists, edges, row, valid, *refs):
    arrays, (out, nothing, sems) = refs[: len(lists)], refs[-3:]
    count = out.shape[0]
    nothing[...] = jnp.zeros_like(nothing)

    def each(act):
        def move(source, target, offset, sem):
            act(pltpu.make_async_copy(source, out.at[target, :, offset], sems.at[sem]))

        for index, (array, (held, written)) in enumerate(zip(arrays, lists)):

            def write(offset, target):
                source = array.at[held.index(offset)] if offset in held else nothing
                move(source, target, offset, index * 13 + offset)

            here = row[index]

            @pl.when(valid[index] == 1)
            def _():
                for offset in written:
                    if offset not in (AHEAD, BEHIND):
                        write(offset, here)

            if AHEAD in written:

                @pl.when((valid[index] == 1) & (here + 1 < count))
                def _():
                    write(AHEAD, here + 1)

            if BEHIND in written:

                @pl.when((valid[index] == 1) & (here > 0))
                def _():
                    write(BEHIND, here - 1)

        if edges:
            move(nothing, 0, AHEAD, 13 * len(lists))
            move(nothing, count - 1, BEHIND, 13 * len(lists) + 1)

    each(lambda copy: copy.start())
    each(lambda copy: copy.wait())


def placed(out, pieces, count):
    arrays = [piece[0] for piece in pieces]
    members, _, tile, _ = arrays[0].shape[1:]
    scalars = pl.BlockSpec(memory_space=pltpu.SMEM)
    in_specs = [scalars] * 2 + [pl.BlockSpec(memory_space=pltpu.VMEM)] * len(arrays)
    operands = list(arrays)
    if out is not None:
        in_specs.append(pl.BlockSpec(memory_space=pl.ANY))
        operands.append(out)
    rows = jnp.stack([jnp.asarray(jnp.where(p[4], p[3], 0), jnp.int32) for p in pieces])
    valid = jnp.stack([jnp.asarray(p[4], jnp.int32) for p in pieces])
    return pl.pallas_call(
        functools.partial(place_kernel, tuple(p[1:3] for p in pieces), out is None),
        in_specs=in_specs,
        out_specs=pl.BlockSpec(memory_space=pl.ANY),
        scratch_shapes=[
            pltpu.VMEM((members, members, tile, tile), jnp.bfloat16),
            pltpu.SemaphoreType.DMA((len(pieces) * 13 + 2,)),
        ],
        out_shape=jax.ShapeDtypeStruct(
            (count, members, 13, members, tile, tile), jnp.bfloat16
        ),
        input_output_aliases={2 + len(arrays): 0} if out is not None else {},
        compiler_params=pltpu.CompilerParams(vmem_limit_bytes=24 * 1024 * 1024),
        cost_estimate=pl.CostEstimate(
            flops=0, bytes_accessed=6 * 13 * members * members * tile * tile, transcendentals=0
        ),
        name="placed",
    )(rows, valid, *operands)


def end_to_end(halves, grid_y, count_y):
    lower = tuple(o for o in TRAVEL if WINDOW_SHIFTS[o][1] in (0, 1))
    upper = tuple(o for o in TRAVEL if WINDOW_SHIFTS[o][1] in (-1, 0))
    start = jnp.where(grid_y == 0, TRAVEL.index(lower[0]), TRAVEL.index(upper[0]))
    sent = lax.dynamic_slice_in_dim(jnp.concatenate(halves, axis=0), start, len(lower), axis=0)
    last = count_y - 1
    moved = lax.ppermute(sent, "sy", [(0, last), (last, 0)])
    return [
        (moved, lower, TRAVEL, 0, grid_y == last),
        (moved, upper, TRAVEL, last, grid_y == 0),
    ]


def gathered_rows(halves, grid_y, count_y):
    chains = [(half, half) for half in halves]
    pieces = [(half, group, group, grid_y, True) for half, group in zip(halves, HALVES)]
    out = None
    for hop in range(1, count_y - 1):
        chains = [(shifted(a, "sy", 1), shifted(b, "sy", -1)) for a, b in chains]
        if hop == 1:
            direct = end_to_end(halves, grid_y, count_y)
        out = placed(out, pieces, count_y)
        if hop == 1:
            chains[1], out = lax.optimization_barrier((chains[1], out))
        pieces = []
        for (from_lower, from_upper), group in zip(chains, HALVES):
            pieces += [
                (from_lower, group, group, grid_y - hop, grid_y >= hop),
                (from_upper, group, group, grid_y + hop, grid_y + hop < count_y),
            ]
    out = placed(out, direct + pieces[2:], count_y)
    return placed(out, pieces[:2], count_y)


def local(a_tiles, columns, ptent, dinv, agg):
    grid_x = lax.axis_index("sx")
    grid_y = lax.axis_index("sy")
    count_y = lax.axis_size("sy")
    rows, taps, tile = a_tiles.shape[2], a_tiles.shape[3], a_tiles.shape[-1]
    coupling = a_tiles.reshape(rows, taps, tile, tile)
    inverse = dinv.reshape(rows, tile, tile)
    tent = jnp.swapaxes(ptent.reshape(rows, tile, tile), 1, 2)
    tents = (
        shifted(tent, "sy", 1),
        shifted(tent, "sy", -1),
        swapped(tent, "sx", 1),
        swapped(tent, "sx", 0),
    )
    own_right, own_left, *lists = own_slots(
        coupling,
        columns.reshape(rows * taps),
        inverse,
        tent,
        agg,
        jnp.stack([grid_x, grid_y]).astype(jnp.int32),
        count_y,
        MEMBERS,
    )
    to_lower_y, to_upper_y, to_lower_x, to_upper_x, behind, ahead, right = partial_blocks(
        coupling, inverse, tents, own_right, lists, MEMBERS
    )
    halves = finished_window(
        (
            shifted(to_upper_y, "sy", 1),
            shifted(to_lower_y, "sy", -1),
            shifted(to_upper_x, "sx", 1),
            shifted(to_lower_x, "sx", -1),
            own_rows(own_left, right, MEMBERS),
            behind,
            ahead,
        )
    )
    return gathered_rows(halves, grid_y, count_y)[None]


def solution(mesh):
    return jax.shard_map(
        local,
        mesh=mesh,
        in_specs=(
            P("sx", "sy", None, None, None, None),
            P("sx", "sy", None, None),
            P("sx", "sy", None, None, None),
            P("sx", "sy", None, None, None),
            P(),
        ),
        out_specs=P("sx", None, None, None, None, None, None),
        check_vma=False,
    )
```

```python
import functools

import jax
import jax.numpy as jnp
from jax import lax
from jax.experimental import pallas as pl
from jax.experimental.pallas import tpu as pltpu
from jax.sharding import PartitionSpec as P

CROSS_SHIFTS = ((0, -1), (0, 1), (-1, 0), (1, 0), (0, 0))
OWN = 4
DOWN, UP = CROSS_SHIFTS[:2]
HALO_ORDER = (0, 1, 3, 2)
WINDOW_SHIFTS = (
    (-2, 0),
    (-1, -1),
    (-1, 0),
    (-1, 1),
    (0, -2),
    (0, -1),
    (0, 0),
    (0, 1),
    (0, 2),
    (1, -1),
    (1, 0),
    (1, 1),
    (2, 0),
)
AHEAD, BEHIND = 4, 8
TRAVEL = (4, 1, 5, 9, 0, 2, 6, 10, 12, 3, 7, 11, 8)
HALVES = (TRAVEL[:5], TRAVEL[5:])
smoothing = 2.0 / 3.0
MEMBERS = 2
ROWS_PER_STEP = 4
UNROLL = 16
NT = (((1,), (1,)), ((), ()))


def shifted(x, axis, by):
    length = lax.axis_size(axis)
    pairs = [(i, i + by) for i in range(length) if 0 <= i + by < length]
    return lax.ppermute(x, axis, pairs)


def lane_tiles(g, tile):
    return pl.ds(pl.multiple_of(g * tile, tile), tile)


def swapped(x, axis, first):
    lows = range(first, lax.axis_size(axis) - 1, 2)
    return lax.ppermute(x, axis, [(i + a, i + 1 - a) for i in lows for a in (0, 1)])


def own_kernel(count_y, rows, members, taps, columns, agg, place, a_ref, dinv_ref, tent, *refs):
    right, left, tiles, sources, slots, ends, found = refs[:7]
    sums = refs[7:]
    tile = a_ref.shape[-1]
    step = pl.program_id(0)

    @pl.when(step == 0)
    def _():
        found[0] = 0

    listed = found[0]
    for u in range(ROWS_PER_STEP):
        g = step * ROWS_PER_STEP + u
        total = sums[u]
        total[...] = jnp.zeros_like(total)
        own_member = 0
        for k in range(taps):
            target = columns[g * taps + k]
            holder = target // rows
            step_x = holder // count_y - place[0]
            step_y = holder % count_y - place[1]
            direction = jnp.where(
                step_y == -1,
                0,
                jnp.where(step_y == 1, 1, jnp.where(step_x == -1, 2, jnp.where(step_x == 1, 3, OWN))),
            )
            member = agg[target] % members
            if k == 0:
                own_member = member
            else:
                tiles[listed] = g * taps + k
                seat = jnp.where(direction < 2, direction, 2 + (direction + place[0] + 1) % 2)
                sources[listed] = seat * rows + target % rows
                slots[listed] = direction * members + member
                listed += jnp.where(direction == OWN, 0, 1)
            z = lax.dot_general(
                tent[target % rows], a_ref[u, k], NT, preferred_element_type=jnp.float32
            )
            slot = jnp.where(direction == OWN, member, members)
            total[lane_tiles(slot, tile), :] += z.astype(jnp.bfloat16).astype(jnp.float32)
        here = slice(u * tile, (u + 1) * tile)
        applied = total[: members * tile, :].astype(jnp.bfloat16)
        right[:, here] = applied
        smooth = lax.dot_general(applied, dinv_ref[u], NT, preferred_element_type=jnp.float32)
        total[: members * tile, :] = -smoothing * smooth
        total[lane_tiles(own_member, tile), :] += tent[g].astype(jnp.float32)
        left[:, here] = total[: members * tile, :].astype(jnp.bfloat16)
    found[0] = listed
    ends[step] = listed


def own_slots(a_tiles, columns, dinv, tent, agg, place, count_y, members):
    rows, taps, tile = a_tiles.shape[0], a_tiles.shape[1], a_tiles.shape[-1]
    steps = rows // ROWS_PER_STEP
    span = ROWS_PER_STEP * tile
    scalars = pl.BlockSpec(memory_space=pltpu.SMEM)
    return pl.pallas_call(
        functools.partial(own_kernel, count_y, rows, members, taps),
        grid_spec=pltpu.PrefetchScalarGridSpec(
            num_scalar_prefetch=3,
            grid=(steps,),
            in_specs=[
                pl.BlockSpec((ROWS_PER_STEP, taps, tile, tile), lambda s, *_: (s, 0, 0, 0)),
                pl.BlockSpec((ROWS_PER_STEP, tile, tile), lambda s, *_: (s, 0, 0)),
                pl.BlockSpec((rows, tile, tile), lambda s, *_: (0, 0, 0)),
            ],
            out_specs=[pl.BlockSpec((members * tile, span), lambda s, *_: (0, s))] * 2
            + [scalars] * 4,
            scratch_shapes=[pltpu.SMEM((1,), jnp.int32)]
            + [pltpu.VMEM(((members + 1) * tile, tile), jnp.float32)] * ROWS_PER_STEP,
        ),
        out_shape=[jax.ShapeDtypeStruct((members * tile, rows * tile), jnp.bfloat16)] * 2
        + [jax.ShapeDtypeStruct((rows * taps,), jnp.int32)] * 3
        + [jax.ShapeDtypeStruct((steps,), jnp.int32)],
        compiler_params=pltpu.CompilerParams(vmem_limit_bytes=24 * 1024 * 1024),
        cost_estimate=pl.CostEstimate(
            flops=2 * tile**3 * rows * (taps + members),
            bytes_accessed=2 * (a_tiles.size + dinv.size * 6),
            transcendentals=0,
        ),
        name="own_slots",
    )(columns, agg, place, a_tiles, dinv, tent)


def kept_members(shift):
    lone = CROSS_SHIFTS.index(shift)
    return tuple((lone + 1 + p) % 5 for p in range(4))


def product(left, right, outs, lone, members, tile):
    width = members * tile
    for d1, out in enumerate(outs):
        value = lax.dot_general(
            left[d1 * width : (d1 + 1) * width],
            right,
            NT,
            preferred_element_type=jnp.float32,
        )
        for d2 in range(5):
            target, at = out, d2
            if d1 in lone:
                direction, single = lone[d1]
                target, at = (single, 0) if d2 == direction else (out, (d2 + 4 - direction) % 5)
            for m in range(members):
                for m2 in range(members):
                    row, column = m * tile, (d2 * members + m2) * tile
                    block = value[row : row + tile, column : column + tile]
                    target[at, m, m2] = block.astype(target.dtype)


def partial_kernel(members, taps, tiles, sources, slots, ends, *refs):
    a_tiles, dinv, *tents = refs[:6]
    right_own, *outs, behind, ahead, right_out = refs[6:14]
    tent, right, left, held, sems = refs[14:]
    tile = dinv.shape[-1]
    rows = dinv.shape[0]
    outer = 4 * members
    depth = rows * tile

    copies = [
        pltpu.make_async_copy(source, tent.at[pl.ds(d * rows, rows)], sems.at[d])
        for d, source in zip(HALO_ORDER, tents)
    ]
    own_part = (pl.ds(outer * tile, members * tile), pl.ds(0, depth))
    own_copy = pltpu.make_async_copy(right_own, right.at[own_part], sems.at[4])
    out_copy = pltpu.make_async_copy(right.at[:, pl.ds(0, depth)], right_out, sems.at[5])
    for copy in copies:
        copy.start()
    own_copy.start()
    right[: outer * tile, :] = jnp.zeros((outer * tile, right.shape[1]), right.dtype)
    left[...] = jnp.zeros_like(left)
    held[...] = jnp.zeros_like(held)
    for copy in copies:
        copy.wait()

    last = ends[rows // ROWS_PER_STEP - 1]
    batches = (last + UNROLL - 1) // UNROLL

    def entry(at):
        index = jnp.clip(at, 0, last - 1)
        row = tiles[index] // taps
        lanes = lane_tiles(jnp.where((at >= 0) & (at < last), row, rows), tile)
        return index, row, (lane_tiles(slots[index], tile), lanes)

    def some(n, carry):
        fresh, older = [], []
        for u in range(UNROLL):
            index, _, at = entry(UNROLL * n + u)
            z = lax.dot_general(
                tent[sources[index]],
                a_tiles[tiles[index]],
                NT,
                preferred_element_type=jnp.float32,
            ).astype(jnp.bfloat16)
            fresh.append((at, z))
            _, row, at = entry(UNROLL * (n - 1) + u)
            smooth = lax.dot_general(
                held[(n + 1) % 2, u], dinv[row], NT, preferred_element_type=jnp.float32
            )
            older.append((at, smooth))
        for u, ((at, z), (old_at, smooth)) in enumerate(zip(fresh, older)):
            held[n % 2, u] = z
            right[at] = (right[at].astype(jnp.float32) + z.astype(jnp.float32)).astype(
                jnp.bfloat16
            )
            left[old_at] = (left[old_at].astype(jnp.float32) - smoothing * smooth).astype(
                jnp.bfloat16
            )
        return carry

    lax.fori_loop(0, jnp.where(batches > 0, batches + 1, 0), some, 0)
    own_copy.wait()
    out_copy.start()
    lone = {d: (CROSS_SHIFTS.index(t), out) for d, t, out in ((0, UP, behind), (1, DOWN, ahead))}
    product(left[:, :depth], right[:, :depth], outs, lone, members, tile)
    out_copy.wait()


def partial_blocks(a_tiles, dinv, tents, own_right, lists, members):
    rows, taps, tile = a_tiles.shape[0], a_tiles.shape[1], a_tiles.shape[-1]
    leads = (4, 4, 5, 5, 1, 1)
    outer = 4 * members * tile
    slots = outer + members * tile
    scalars, inside, anywhere = (
        pl.BlockSpec(memory_space=space) for space in (pltpu.SMEM, pltpu.VMEM, pl.ANY)
    )
    return pl.pallas_call(
        functools.partial(partial_kernel, members, taps),
        in_specs=[scalars] * 4 + [inside] * 6 + [anywhere],
        out_specs=[inside] * 6 + [anywhere],
        scratch_shapes=[
            pltpu.VMEM((4 * rows, tile, tile), jnp.bfloat16),
            pltpu.VMEM((slots, (rows + 1) * tile), jnp.bfloat16),
            pltpu.VMEM((outer, (rows + 1) * tile), jnp.bfloat16),
            pltpu.VMEM((2, UNROLL, tile, tile), jnp.bfloat16),
            pltpu.SemaphoreType.DMA((6,)),
        ],
        out_shape=[
            jax.ShapeDtypeStruct((lead, members, members, tile, tile), jnp.bfloat16)
            for lead in leads
        ]
        + [jax.ShapeDtypeStruct((slots, rows * tile), jnp.bfloat16)],
        compiler_params=pltpu.CompilerParams(vmem_limit_bytes=36 * 1024 * 1024),
        cost_estimate=pl.CostEstimate(
            flops=2 * tile**3 * rows * (taps + 20 * members * members),
            bytes_accessed=2 * (a_tiles.size + 20 * dinv.size),
            transcendentals=0,
        ),
        name="partial_blocks",
    )(*lists, a_tiles.reshape(rows * taps, tile, tile), dinv, *tents, own_right)


def own_rows_kernel(members, left_own, right_all, own, left, right, sems):
    copies = [
        pltpu.make_async_copy(left_own, left, sems.at[0]),
        pltpu.make_async_copy(right_all, right, sems.at[1]),
    ]
    for copy in copies:
        copy.start()
    for copy in copies:
        copy.wait()
    product(left[...], right[...], (own,), {}, members, own.shape[-1])


def own_rows(left, right, members):
    tile = left.shape[0] // members
    block = (5, members, members, tile, tile)
    return pl.pallas_call(
        functools.partial(own_rows_kernel, members),
        grid=(1,),
        in_specs=[pl.BlockSpec(memory_space=pl.ANY)] * 2,
        out_specs=pl.BlockSpec(block, lambda s: (0,) * 5),
        out_shape=jax.ShapeDtypeStruct(block, jnp.float32),
        scratch_shapes=[
            pltpu.VMEM(left.shape, left.dtype),
            pltpu.VMEM(right.shape, right.dtype),
            pltpu.SemaphoreType.DMA((2,)),
        ],
        compiler_params=pltpu.CompilerParams(vmem_limit_bytes=32 * 1024 * 1024),
        cost_estimate=pl.CostEstimate(
            flops=2 * left.size * right.shape[0],
            bytes_accessed=2 * (left.size + right.size),
            transcendentals=0,
        ),
        name="own_rows",
    )(left, right)


def window_kernel(*refs):
    every = tuple(range(5))
    held = (kept_members(DOWN), kept_members(UP), every, every, every)
    behind, ahead = refs[5:7]
    for out, half in zip(refs[7:], HALVES):
        for position, offset in enumerate(half):
            if offset in (AHEAD, BEHIND):
                out[position] = (ahead if offset == AHEAD else behind)[0]
                continue
            total = None
            for shift, values, directions in zip(CROSS_SHIFTS, refs, held):
                for d, direction in enumerate(directions):
                    member = CROSS_SHIFTS[direction]
                    if (shift[0] + member[0], shift[1] + member[1]) == WINDOW_SHIFTS[offset]:
                        term = values[d].astype(jnp.float32)
                        total = term if total is None else total + term
            out[position] = total.astype(out.dtype)


def finished_window(blocks):
    _, members, _, tile, _ = blocks[0].shape
    spec = lambda lead: pl.BlockSpec(
        (lead, 1, members, tile, tile), lambda m: (0, m, 0, 0, 0)
    )
    return pl.pallas_call(
        window_kernel,
        grid=(members,),
        in_specs=[spec(block.shape[0]) for block in blocks],
        out_specs=[spec(len(half)) for half in HALVES],
        out_shape=[
            jax.ShapeDtypeStruct((len(half), members, members, tile, tile), jnp.bfloat16)
            for half in HALVES
        ],
        compiler_params=pltpu.CompilerParams(vmem_limit_bytes=32 * 1024 * 1024),
        cost_estimate=pl.CostEstimate(
            flops=5 * blocks[4].size, bytes_accessed=16 * blocks[4].size, transcendentals=0
        ),
        name="finished_window",
    )(*blocks)


def place_kernel(lists, edges, row, valid, *refs):
    arrays, (out, nothing, sems) = refs[: len(lists)], refs[-3:]
    count = out.shape[0]
    nothing[...] = jnp.zeros_like(nothing)

    def each(act):
        def move(source, target, offset, sem):
            act(pltpu.make_async_copy(source, out.at[target, :, offset], sems.at[sem]))

        for index, (array, (held, written)) in enumerate(zip(arrays, lists)):

            def write(offset, target):
                source = array.at[held.index(offset)] if offset in held else nothing
                move(source, target, offset, index * 13 + offset)

            here = row[index]

            @pl.when(valid[index] == 1)
            def _():
                for offset in written:
                    if offset not in (AHEAD, BEHIND):
                        write(offset, here)

            if AHEAD in written:

                @pl.when((valid[index] == 1) & (here + 1 < count))
                def _():
                    write(AHEAD, here + 1)

            if BEHIND in written:

                @pl.when((valid[index] == 1) & (here > 0))
                def _():
                    write(BEHIND, here - 1)

        if edges:
            move(nothing, 0, AHEAD, 13 * len(lists))
            move(nothing, count - 1, BEHIND, 13 * len(lists) + 1)

    each(lambda copy: copy.start())
    each(lambda copy: copy.wait())


def placed(out, pieces, count):
    arrays = [piece[0] for piece in pieces]
    members, _, tile, _ = arrays[0].shape[1:]
    scalars = pl.BlockSpec(memory_space=pltpu.SMEM)
    in_specs = [scalars] * 2 + [pl.BlockSpec(memory_space=pltpu.VMEM)] * len(arrays)
    operands = list(arrays)
    if out is not None:
        in_specs.append(pl.BlockSpec(memory_space=pl.ANY))
        operands.append(out)
    rows = jnp.stack([jnp.asarray(jnp.where(p[4], p[3], 0), jnp.int32) for p in pieces])
    valid = jnp.stack([jnp.asarray(p[4], jnp.int32) for p in pieces])
    return pl.pallas_call(
        functools.partial(place_kernel, tuple(p[1:3] for p in pieces), out is None),
        in_specs=in_specs,
        out_specs=pl.BlockSpec(memory_space=pl.ANY),
        scratch_shapes=[
            pltpu.VMEM((members, members, tile, tile), jnp.bfloat16),
            pltpu.SemaphoreType.DMA((len(pieces) * 13 + 2,)),
        ],
        out_shape=jax.ShapeDtypeStruct(
            (count, members, 13, members, tile, tile), jnp.bfloat16
        ),
        input_output_aliases={2 + len(arrays): 0} if out is not None else {},
        compiler_params=pltpu.CompilerParams(vmem_limit_bytes=24 * 1024 * 1024),
        cost_estimate=pl.CostEstimate(
            flops=0, bytes_accessed=6 * 13 * members * members * tile * tile, transcendentals=0
        ),
        name="placed",
    )(rows, valid, *operands)


def end_to_end(halves, grid_y, count_y):
    lower = tuple(o for o in TRAVEL if WINDOW_SHIFTS[o][1] in (0, 1))
    upper = tuple(o for o in TRAVEL if WINDOW_SHIFTS[o][1] in (-1, 0))
    start = jnp.where(grid_y == 0, TRAVEL.index(lower[0]), TRAVEL.index(upper[0]))
    sent = lax.dynamic_slice_in_dim(jnp.concatenate(halves, axis=0), start, len(lower), axis=0)
    last = count_y - 1
    moved = lax.ppermute(sent, "sy", [(0, last), (last, 0)])
    return [
        (moved, lower, TRAVEL, 0, grid_y == last),
        (moved, upper, TRAVEL, last, grid_y == 0),
    ]


def gathered_rows(halves, grid_y, count_y):
    chains = [(half, half) for half in halves]
    pieces = [(half, group, group, grid_y, True) for half, group in zip(halves, HALVES)]
    out = None
    for hop in range(1, count_y - 1):
        chains = [(shifted(a, "sy", 1), shifted(b, "sy", -1)) for a, b in chains]
        if hop == 1:
            direct = end_to_end(halves, grid_y, count_y)
        out = placed(out, pieces, count_y)
        if hop == 1:
            chains[1], out = lax.optimization_barrier((chains[1], out))
        pieces = []
        for (from_lower, from_upper), group in zip(chains, HALVES):
            pieces += [
                (from_lower, group, group, grid_y - hop, grid_y >= hop),
                (from_upper, group, group, grid_y + hop, grid_y + hop < count_y),
            ]
    out = placed(out, direct + pieces[2:], count_y)
    return placed(out, pieces[:2], count_y)


def local(a_tiles, columns, ptent, dinv, agg):
    grid_x = lax.axis_index("sx")
    grid_y = lax.axis_index("sy")
    count_y = lax.axis_size("sy")
    rows, taps, tile = a_tiles.shape[2], a_tiles.shape[3], a_tiles.shape[-1]
    coupling = a_tiles.reshape(rows, taps, tile, tile)
    inverse = dinv.reshape(rows, tile, tile)
    tent = jnp.swapaxes(ptent.reshape(rows, tile, tile), 1, 2)
    tents = (
        shifted(tent, "sy", 1),
        shifted(tent, "sy", -1),
        swapped(tent, "sx", 1),
        swapped(tent, "sx", 0),
    )
    own_right, own_left, *lists = own_slots(
        coupling,
        columns.reshape(rows * taps),
        inverse,
        tent,
        agg,
        jnp.stack([grid_x, grid_y]).astype(jnp.int32),
        count_y,
        MEMBERS,
    )
    to_lower_y, to_upper_y, to_lower_x, to_upper_x, behind, ahead, right = partial_blocks(
        coupling, inverse, tents, own_right, lists, MEMBERS
    )
    halves = finished_window(
        (
            shifted(to_upper_y, "sy", 1),
            shifted(to_lower_y, "sy", -1),
            shifted(to_upper_x, "sx", 1),
            shifted(to_lower_x, "sx", -1),
            own_rows(own_left, right, MEMBERS),
            behind,
            ahead,
        )
    )
    return gathered_rows(halves, grid_y, count_y)[None]


def solution(mesh):
    return jax.shard_map(
        local,
        mesh=mesh,
        in_specs=(
            P("sx", "sy", None, None, None, None),
            P("sx", "sy", None, None),
            P("sx", "sy", None, None, None),
            P("sx", "sy", None, None, None),
            P(),
        ),
        out_specs=P("sx", None, None, None, None, None, None),
        check_vma=False,
    )
```
